32 devices in a mesh: dp: 16 (over z, y, core), tensor: 2 (over x).
Axes of the slice: x: 2, y: 2, z: 4, core: 2. Of those that a mesh axis runs over, the one named last changes fastest.
Arguments:
- hidden: bfloat16 [16384, 768], P(('dp', 'tensor')), may hold values from -6 to 6
- seq_ids: int32 [16384], P('dp'), may hold values from -1 to 2, as said below
- cotangent: bfloat16 [16384, 768], P(('dp', 'tensor')), may hold values from -6 to 6
- qkv_weight: bfloat16 [3, 768, 768], P(None, None, 'tensor'), may hold values from -0.21875 to 0.21875
- attn_out_weight: bfloat16 [768, 768], P('tensor'), may hold values from -0.875 to 0.875
- mlp_in_weight: bfloat16 [2, 768, 1152], P(None, None, 'tensor'), may hold values from -0.21875 to 0.21875
- mlp_out_weight: bfloat16 [1152, 768], P('tensor'), may hold values from -0.1875 to 0.1875
- norm1_gain: float32 [768], replicated, may hold values from 0.25 to 1.75
- norm2_gain: float32 [768], replicated, may hold values from 0.25 to 1.75
Outputs:
- output: bfloat16 [16384, 768], P(('dp', 'tensor'))
- input_grad: bfloat16 [16384, 768], P(('dp', 'tensor'))
- norm1_grad: float32 [768], replicated
- norm2_grad: float32 [768], replicated
- qkv_grad: float32 [3, 768, 768], P(None, None, 'tensor')
- attn_out_grad: float32 [768, 768], P('tensor')
- mlp_in_grad: float32 [2, 768, 1152], P(None, None, 'tensor')
- mlp_out_grad: float32 [1152, 768], P('tensor')
The draws below stay inside these ranges and needn't reach their ends.
Inputs may be any that keep to these rules, and one draw needn't show every extreme that they name: `seq_ids`: each block of 1024 slots (one dp index) holds runs of ids 0, 1 and possibly 2, never falling, then -1 padding to its end; each run is at most 512 long and run 1 covers the block's two middle slots; in one block run 1 is exactly 512 long and there is no padding.
All inputs are finite; a program needn't handle non-finite values.
Results may differ from the reference program's by a relative error of at most 0.017.
Values may be sent and summed in bfloat16 or wider, within the bound.
No kernel may reach another device: no remote copies, remote signals or barrier semaphores. Data moves between devices by JAX's collectives and lax.ppermute only.
A program may use at most 128 MiB of HBM per device.

```python
import math
import jax
import jax.numpy as jnp
from jax import lax

D = 768
HEADS = 12
HDIM = 64
FF = 1152
TOK_DEV = 1024
TOKENS = 16384
N_DP = 16


def draw_seq_ids(key, part):
    key = jax.random.fold_in(key, 11)
    groups = TOKENS // TOK_DEV
    quarter = TOK_DEV // 4
    halfway = TOK_DEV // 2
    key_first, key_middle, key_end, key_whole = jax.random.split(key, 4)
    first = jax.random.randint(key_first, (groups,), quarter + 1, halfway)
    middle = jax.random.randint(key_middle, (groups,), quarter, halfway + 1)
    chosen = jnp.arange(groups) == jax.random.randint(key_whole, (), 0, groups)
    middle = jnp.where(chosen, halfway, middle)
    second = first + middle
    spare = jax.random.randint(key_end, (groups,), 0, 1 << 20) % (TOK_DEV + 1 - second)
    ending = jnp.where(chosen, TOK_DEV, second + spare)
    index = jnp.arange(TOK_DEV)[None, :]
    ids = (index >= first[:, None]).astype(jnp.int32) + (index >= second[:, None]).astype(jnp.int32)
    ids = jnp.where(index < ending[:, None], ids, -1)
    return ids.reshape(-1).astype(jnp.int32)


def block_scale(key, extent, shards, least, top_value):
    level = 1.0
    for axis_at, blocks in shards:
        draws = jax.random.uniform(jax.random.fold_in(jax.random.fold_in(key, 6), axis_at), (blocks,), jnp.float32, least / len(shards), top_value / len(shards))
        level = level * jnp.repeat(jnp.exp(draws), extent[axis_at] // blocks).reshape((-1,) + (1,) * (len(extent) - 1 - axis_at))
    return level


def centred(key, dims, deviation, most, cuts=(), kind=jnp.bfloat16):
    values = jax.random.normal(key, dims, jnp.float32) * deviation
    if len(cuts) > 0:
        values = block_scale(key, dims, cuts, -0.22, 0.18) * values
    return jnp.clip(values, min=-most, max=most).astype(kind)


def setup_inputs(seed: int = 0) -> dict:
    key_list = jax.random.split(jax.random.key(seed), 10)
    hidden = centred(key_list[0], (TOKENS, D), 1.0, 6.0, ((0, 32),))
    seq_ids = draw_seq_ids(jax.random.fold_in(key_list[9], 71), 0)
    cotangent = centred(key_list[2], (TOKENS, D), 1.0, 6.0, ((0, 32),))
    qkv_weight = centred(key_list[3], (3, D, D), D ** -0.5, 0.21875, ((2, 2),))
    attn_out_weight = centred(key_list[4], (D, D), (max(D // 16, 1)) ** -0.5, 0.875, ((0, 2),))
    mlp_in_weight = centred(key_list[5], (2, D, FF), D ** -0.5, 0.21875, ((2, 2),))
    mlp_out_weight = centred(key_list[6], (FF, D), FF ** -0.5, 0.1875, ((0, 2),))
    norm1_gain = jnp.clip(1.0 + 0.15 * jax.random.normal(key_list[7], (D,), jnp.float32), 0.25, 1.75)
    norm2_gain = jnp.clip(1.0 + 0.15 * jax.random.normal(key_list[8], (D,), jnp.float32), 0.25, 1.75)
    return {"hidden": hidden, "seq_ids": seq_ids, "cotangent": cotangent, "qkv_weight": qkv_weight, "attn_out_weight": attn_out_weight, "mlp_in_weight": mlp_in_weight, "mlp_out_weight": mlp_out_weight, "norm1_gain": norm1_gain, "norm2_gain": norm2_gain}


EPSILON = 1e-05
ROPE_BASE = 160000.0
HIGHEST = lax.Precision.HIGHEST

@jax.custom_vjp
def low(v):
    return lax.optimization_barrier(v.astype(jnp.bfloat16)).astype(jnp.float32)

@jax.custom_vjp
def low_back(v):
    return v

def low_keep(v):
    return (low(v), None)

def low_pass(kept, grad):
    return (grad,)

def back_keep(v):
    return (v, None)

def back_low(kept, grad):
    return (low(grad),)
low.defvjp(low_keep, low_pass)
low_back.defvjp(back_keep, back_low)

def layer_norm(values, gain):
    center = values - lax.optimization_barrier(jnp.mean(values, axis=-1, keepdims=True))
    spread = lax.optimization_barrier(jnp.mean(center * center, axis=-1, keepdims=True))
    return center * lax.rsqrt(spread + EPSILON) * gain

def positions_of(ids):
    index = jnp.arange(ids.shape[0], dtype=jnp.int32)
    before = jnp.concatenate([ids[:1] - 1, ids[:-1]])
    begins = lax.cummax(jnp.where(ids != before, index, 0), axis=0)
    return index - begins

def rope_tables(positions, head_dim):
    frequency = jnp.power(ROPE_BASE, -2.0 * jnp.arange(head_dim // 2, dtype=jnp.float32) / head_dim)
    angles = positions.astype(jnp.float32)[:, None] * frequency[None, :]
    angles = jnp.concatenate([angles, angles], axis=1)
    return (jnp.cos(angles), jnp.sin(angles))

def rotate(values):
    halfway = values.shape[-1] // 2
    return jnp.concatenate([-values[..., halfway:], values[..., :halfway]], axis=-1)

def apply_rope(values, cosine, sine):
    return values * cosine[:, None, :] + rotate(values) * sine[:, None, :]

def attend_head(triple, same, scale_factor):
    queries, keys, values = triple
    scores = low_back(jnp.dot(queries, keys.T, precision=HIGHEST)) * scale_factor
    scores = jnp.where(same, scores, -1e+30)
    highest = lax.optimization_barrier(jnp.max(scores, axis=-1, keepdims=True))
    expo = jnp.exp(scores - highest)
    probs = expo / lax.optimization_barrier(jnp.sum(expo, axis=-1, keepdims=True))
    return low(low_back(jnp.dot(low(probs), values, precision=HIGHEST)))

def row_layer(row_x, row_ids, weights):
    qkv_w, attn_w, in_w, out_w, gain_one, gain_two = weights
    row_total = row_x.shape[0]
    cosine, sine = rope_tables(positions_of(row_ids), HDIM)
    normed = low(layer_norm(row_x, gain_one))
    q_raw = low_back(jnp.dot(normed, qkv_w[0], precision=HIGHEST)).reshape(row_total, HEADS, HDIM)
    k_raw = low_back(jnp.dot(normed, qkv_w[1], precision=HIGHEST)).reshape(row_total, HEADS, HDIM)
    values = low(low_back(jnp.dot(normed, qkv_w[2], precision=HIGHEST))).reshape(row_total, HEADS, HDIM)
    queries = low(apply_rope(q_raw, cosine, sine))
    keys = low(apply_rope(k_raw, cosine, sine))
    same = row_ids[:, None] == row_ids[None, :]
    scale_factor = 1.0 / math.sqrt(HDIM)

    def one_head(triple):
        return attend_head(triple, same, scale_factor)
    per_head = lax.map(jax.checkpoint(one_head), (queries.transpose(1, 0, 2), keys.transpose(1, 0, 2), values.transpose(1, 0, 2)))
    attended = per_head.transpose(1, 0, 2).reshape(row_total, HEADS * HDIM)
    mixed = row_x + low_back(jnp.dot(attended, attn_w, precision=HIGHEST))
    second = low(layer_norm(mixed, gain_two))
    up_part = low_back(jnp.dot(second, in_w[0], precision=HIGHEST))
    gate_part = low_back(jnp.dot(second, in_w[1], precision=HIGHEST))
    hidden_mlp = low(jax.nn.gelu(up_part, approximate=False) * gate_part)
    return mixed + low_back(jnp.dot(hidden_mlp, out_w, precision=HIGHEST))

def reference(hidden, seq_ids, cotangent, qkv_weight, attn_out_weight, mlp_in_weight, mlp_out_weight, norm1_gain, norm2_gain):
    inputs = hidden.astype(jnp.float32).reshape(N_DP, TOK_DEV, D)
    ids = seq_ids.reshape(N_DP, TOK_DEV)
    live = (ids >= 0)[..., None]
    grads_in = jnp.where(live, cotangent.astype(jnp.float32).reshape(N_DP, TOK_DEV, D), 0.0)
    params = (qkv_weight.astype(jnp.float32), attn_out_weight.astype(jnp.float32), mlp_in_weight.astype(jnp.float32), mlp_out_weight.astype(jnp.float32), norm1_gain, norm2_gain)

    def whole(layer_in, weights):

        def one_row(pair):
            return row_layer(pair[0], pair[1], weights)
        return lax.map(jax.checkpoint(one_row), (layer_in, ids))
    result, pull = jax.vjp(whole, inputs, params)
    grad_x, grad_params = pull(grads_in)
    grad_qkv, grad_attn, grad_in, grad_out, grad_one, grad_two = grad_params
    return (result.reshape(TOKENS, D).astype(jnp.bfloat16), grad_x.reshape(TOKENS, D).astype(jnp.bfloat16), grad_one, grad_two, grad_qkv, grad_attn, grad_in, grad_out)
```

```python
import functools
import math

import jax
import jax.numpy as jnp
from jax import lax
from jax.experimental import pallas as pl
from jax.experimental.pallas import tpu as pltpu
from jax.sharding import PartitionSpec as P

HDIM = 64
LANES = 128
EPSILON = 1e-05
ROPE_BASE = 160000.0
MASKED = -1e30
F32 = jnp.float32
BF16 = jnp.bfloat16
VMEM_LIMIT = 50 * 1024 * 1024


def dot(left, right):
    return jnp.dot(left, right, preferred_element_type=F32)


def dot_t(left, right):
    return lax.dot_general(left, right, (((1,), (1,)), ((), ())), preferred_element_type=F32)


def t_dot(left, right):
    return lax.dot_general(left, right, (((0,), (0,)), ((), ())), preferred_element_type=F32)


def norm_parts(values):
    center = values - jnp.mean(values, axis=-1, keepdims=True)
    spread = jnp.mean(center * center, axis=-1, keepdims=True)
    scale = lax.rsqrt(spread + EPSILON)
    return center * scale, scale


def swap_halves(values):
    lane = lax.broadcasted_iota(jnp.int32, values.shape, 1) % HDIM
    return jnp.where(
        lane < HDIM // 2,
        pltpu.roll(values, LANES - HDIM // 2, 1),
        pltpu.roll(values, HDIM // 2, 1),
    )


def low_lanes(shape):
    return lax.broadcasted_iota(jnp.int32, shape, 1) < HDIM


def cost(flops, nbytes, trans=0):
    return pl.CostEstimate(flops=int(flops), bytes_accessed=int(nbytes), transcendentals=int(trans))


def params(*semantics):
    if semantics:
        return pltpu.CompilerParams(vmem_limit_bytes=VMEM_LIMIT, dimension_semantics=semantics)
    return pltpu.CompilerParams(vmem_limit_bytes=VMEM_LIMIT)


VSPEC = pl.BlockSpec(memory_space=pltpu.VMEM)
SSPEC = pl.BlockSpec(memory_space=pltpu.SMEM)
ANYSPEC = pl.BlockSpec(memory_space=pl.ANY)
CORE, PIECE, MINE, THEIRS, FIRST, SECOND = range(6)


def aligned(value, by):
    return pl.multiple_of(value, by)


def ordered(kernel, count, *refs):
    kernel(*refs[count:])


def load_pieces(place_ref, pieces, w_s):
    size = pieces[0].shape[0]
    for step, piece in enumerate(pieces):
        at = (place_ref[PIECE] ^ step) * size
        w_s[pl.ds(aligned(at, 16), size), :] = piece[...]


def project_kernel(gathered, *refs):
    if gathered:
        place_ref, x_ref, gain_ref, w0, w1, w2, w3, cos_ref, sin_ref, q_ref, kv_ref, w_ref = refs
        load_pieces(place_ref, (w0, w1, w2, w3), w_ref)
    else:
        place_ref, x_ref, gain_ref, w_ref, cos_ref, sin_ref, q_ref, kv_ref = refs
    rows, width = x_ref.shape
    cols = q_ref.shape[1]
    tile = min(256, rows)
    for begin in range(0, rows, tile):
        at = pl.ds(begin, tile)
        normed, _ = norm_parts(x_ref[at, :].astype(F32))
        low = (normed * gain_ref[...]).astype(BF16)
        cosine, sine = cos_ref[at, :], sin_ref[at, :]
        q_raw = dot(low, w_ref[0:width, :])
        k_raw = dot(low, w_ref[width : 2 * width, :])
        kv_ref[pl.ds(rows + begin, tile), :] = dot(low, w_ref[2 * width : 3 * width, :]).astype(BF16)
        for col in range(0, cols, LANES):
            part = slice(col, col + LANES)
            q_part, k_part = q_raw[:, part], k_raw[:, part]
            q_ref[at, part] = (
                (q_part * cosine + swap_halves(q_part) * sine).astype(BF16) * (1.0 / math.sqrt(HDIM))
            ).astype(BF16)
            kv_ref[at, part] = (k_part * cosine + swap_halves(k_part) * sine).astype(BF16)


def project(place, x, gain, weights, cosine, sine):
    rows, width = x.shape
    cols = weights[0].shape[1]
    gathered = len(weights) > 1
    operands = [place, x, gain, *weights, cosine, sine]
    return pl.pallas_call(
        functools.partial(project_kernel, gathered),
        out_shape=(
            jax.ShapeDtypeStruct((rows, cols), BF16),
            jax.ShapeDtypeStruct((2 * rows, cols), BF16),
        ),
        in_specs=[SSPEC] + [VSPEC] * (len(operands) - 1),
        out_specs=[VSPEC] * 2,
        scratch_shapes=[pltpu.VMEM((3 * width, cols), BF16)] if gathered else [],
        compiler_params=params(),
        cost_estimate=cost(2 * rows * width * cols * 3, 6 * width * cols + 8 * rows * width),
        name="project",
    )(*operands)


def attend_kernel(q_ref, ko_ref, vo_ref, kx_ref, vx_ref, col_ref, row_ref, rowx_ref, o_ref, lse_ref, bo_ref, bx_ref):
    rows = q_ref.shape[0]
    tile = min(256, rows)

    @pl.when(pl.program_id(0) == 0)
    def _():
        col = col_ref[...][:, 0:1]
        bo_ref[...] = jnp.where(col == row_ref[0:1, :], 0.0, MASKED)
        bx_ref[...] = jnp.where(col == rowx_ref[0:1, :], 0.0, MASKED)

    for begin in range(0, rows, tile):
        at = pl.ds(begin, tile)
        low = low_lanes((tile, LANES))
        q_pair = q_ref[at, :]
        results, logs = [], []
        for head in range(2):
            chosen = low if head == 0 else jnp.logical_not(low)
            query = jnp.where(chosen, q_pair, jnp.zeros_like(q_pair))
            own = dot_t(query, ko_ref[...]) + bo_ref[at, :]
            other = dot_t(query, kx_ref[...]) + bx_ref[at, :]
            highest = jnp.maximum(
                jnp.max(own, axis=-1, keepdims=True), jnp.max(other, axis=-1, keepdims=True)
            )
            own = jnp.exp(own - highest)
            other = jnp.exp(other - highest)
            totals = jnp.sum(own, axis=-1, keepdims=True) + jnp.sum(other, axis=-1, keepdims=True)
            value = dot(own.astype(BF16), vo_ref[...]) + dot(other.astype(BF16), vx_ref[...])
            results.append(value / totals)
            logs.append(highest + jnp.log(totals))
        o_ref[at, :] = jnp.where(low, results[0], results[1]).astype(BF16)
        lse_ref[at, :] = jnp.where(low, logs[0], logs[1])


def attend(q, kv_own, kv_other, col, row, row_other):
    rows, cols = q.shape
    pairs = cols // LANES
    tok = pl.BlockSpec((rows, LANES), lambda p: (0, p))
    tok_v = pl.BlockSpec((rows, LANES), lambda p: (1, p))
    return pl.pallas_call(
        attend_kernel,
        grid=(pairs,),
        out_shape=(
            jax.ShapeDtypeStruct((rows, cols), BF16),
            jax.ShapeDtypeStruct((rows, cols), F32),
        ),
        in_specs=[
            tok,
            tok,
            tok_v,
            tok,
            tok_v,
            pl.BlockSpec((rows, LANES), lambda p: (0, 0)),
            pl.BlockSpec((8, rows), lambda p: (0, 0)),
            pl.BlockSpec((8, rows), lambda p: (0, 0)),
        ],
        out_specs=[tok, tok],
        scratch_shapes=[pltpu.VMEM((rows, rows), F32), pltpu.VMEM((rows, rows), F32)],
        compiler_params=params("arbitrary"),
        cost_estimate=cost(
            4 * rows * 2 * rows * cols * 4, 12 * rows * cols, 2 * rows * rows * cols // HDIM
        ),
        name="attend",
    )(q, kv_own, kv_own, kv_other, kv_other, col, row, row_other)


def attend_back_kernel(
    q_ref, ko_ref, vo_ref, kx_ref, vx_ref, do_ref, o_ref, lse_ref, col_ref, colx_ref, row_ref, cos_ref, sin_ref,
    gq_ref, dko_ref, dvo_ref, dkx_ref, dvx_ref, bo_ref, bx_ref,
):
    rows = q_ref.shape[0]
    tile = min(256, rows)

    @pl.when(pl.program_id(0) == 0)
    def _():
        row = row_ref[0:1, :]
        bo_ref[...] = jnp.where(col_ref[...][:, 0:1] == row, 0.0, MASKED)
        bx_ref[...] = jnp.where(colx_ref[...][:, 0:1] == row, 0.0, MASKED)

    low = low_lanes((rows, LANES))
    q_pair, do_pair = q_ref[...], do_ref[...]
    product = do_pair.astype(F32) * o_ref[...].astype(F32)
    first = jnp.sum(jnp.where(low, product, 0.0), axis=-1, keepdims=True)
    second = jnp.sum(jnp.where(low, 0.0, product), axis=-1, keepdims=True)
    delta_t = jnp.transpose(jnp.where(low, first, second))
    lse_t = jnp.transpose(lse_ref[...])
    low_tile = low_lanes((tile, LANES))
    grad_q = jnp.zeros((rows, LANES), F32)
    for k_ref, v_ref, bias_ref, dk_ref, dv_ref in (
        (ko_ref, vo_ref, bo_ref, dko_ref, dvo_ref),
        (kx_ref, vx_ref, bx_ref, dkx_ref, dvx_ref),
    ):
        for begin in range(0, rows, tile):
            at = pl.ds(begin, tile)
            k_pair, v_pair = k_ref[at, :], v_ref[at, :]
            grad_k = grad_v = None
            for head in range(2):
                chosen = low_tile if head == 0 else jnp.logical_not(low_tile)
                chosen_q = low if head == 0 else jnp.logical_not(low)
                key = jnp.where(chosen, k_pair, jnp.zeros_like(k_pair))
                value = jnp.where(chosen, v_pair, jnp.zeros_like(v_pair))
                query = jnp.where(chosen_q, q_pair, jnp.zeros_like(q_pair))
                grad_o = jnp.where(chosen_q, do_pair, jnp.zeros_like(do_pair))
                at_row = head * HDIM
                scores = dot_t(key, q_pair) + bias_ref[at, :]
                probs = jnp.exp(scores - lse_t[at_row : at_row + 1, :])
                grad_probs = dot_t(value, do_pair)
                grad_scores = (probs * (grad_probs - delta_t[at_row : at_row + 1, :])).astype(BF16)
                term_v = dot(probs.astype(BF16), grad_o)
                term_k = dot(grad_scores, query)
                grad_v = term_v if grad_v is None else grad_v + term_v
                grad_k = term_k if grad_k is None else grad_k + term_k
                grad_q = grad_q + t_dot(grad_scores, key)
            dk_ref[at, :] = grad_k.astype(dk_ref.dtype)
            dv_ref[at, :] = grad_v.astype(dv_ref.dtype)
    grad_q = grad_q * (1.0 / math.sqrt(HDIM))
    gq_ref[...] = (grad_q * cos_ref[...] - swap_halves(grad_q) * sin_ref[...]).astype(BF16)


def attend_back(q, kv_own, kv_other, grad_o, o, lse, col, col_other, row, cosine, sine, after=()):
    rows, cols = q.shape
    pairs = cols // LANES
    tok = pl.BlockSpec((rows, LANES), lambda p: (0, p))
    tok_v = pl.BlockSpec((rows, LANES), lambda p: (1, p))
    fixed = pl.BlockSpec((rows, LANES), lambda p: (0, 0))
    return pl.pallas_call(
        functools.partial(ordered, attend_back_kernel, len(after)),
        grid=(pairs,),
        out_shape=(
            jax.ShapeDtypeStruct((rows, cols), BF16),
            jax.ShapeDtypeStruct((rows, cols), F32),
            jax.ShapeDtypeStruct((rows, cols), F32),
            jax.ShapeDtypeStruct((rows, cols), BF16),
            jax.ShapeDtypeStruct((rows, cols), BF16),
        ),
        in_specs=[ANYSPEC] * len(after)
        + [
            tok, tok, tok_v, tok, tok_v, tok, tok, tok, fixed, fixed,
            pl.BlockSpec((8, rows), lambda p: (0, 0)), fixed, fixed,
        ],
        out_specs=[tok] * 5,
        scratch_shapes=[pltpu.VMEM((rows, rows), F32), pltpu.VMEM((rows, rows), F32)],
        compiler_params=params("arbitrary"),
        cost_estimate=cost(
            10 * rows * 2 * rows * cols * 4, 30 * rows * cols, 2 * rows * rows * cols // HDIM
        ),
        name="attend_back",
    )(*after, q, kv_own, kv_own, kv_other, kv_other, grad_o, o, lse, col, col_other, row, cosine, sine)


def middle_kernel(
    place_ref, x_ref, atto_ref, attx_ref, cot_ref, col_ref, gain_ref, wo_ref, wi_ref, wd_ref, p0, p1, p2, p3,
    out_ref, gm_ref, gao_ref, gax_ref, ak_ref, as_ref, bk_ref, bs_ref, gain_grad_ref,
    wi_s, wd_s, wo_s, b_s, g_s, gml_s, hid_s, gu_s, gg_s,
):
    rows, width = x_ref.shape
    units, cols = wd_ref.shape[0], wo_ref.shape[0]
    both = 2 * units
    wi_s[0:units, :] = wi_ref[0:units, :]
    wi_s[both : both + units, :] = wi_ref[units:both, :]
    wd_s[0:units, :] = wd_ref[...]
    wo_s[0:cols, :] = wo_ref[...]
    n_i, n_d, n_o = both // 4, units // 4, cols // 4
    for step, piece in enumerate((p0, p1, p2, p3)):
        at = place_ref[PIECE] ^ step
        to_i = units + (at % 2) * n_i + (at // 2) * both
        wi_s[pl.ds(aligned(to_i, 16), n_i), :] = piece[0:n_i, :]
        wd_s[pl.ds(aligned(units + at * n_d, 16), n_d), :] = piece[n_i : n_i + n_d, :]
        wo_s[pl.ds(aligned(cols + at * n_o, 16), n_o), :] = piece[n_i + n_d :, :]
    tile = min(256, rows)
    gain = gain_ref[...]
    gain_grad = jnp.zeros((1, width), F32)
    for begin in range(0, rows, tile):
        at = pl.ds(begin, tile)
        mixed = x_ref[at, :].astype(F32) + dot(atto_ref[at, :], wo_s[0:cols, :]) + dot(attx_ref[at, :], wo_s[cols:, :])
        normed, scale = norm_parts(mixed)
        low = (normed * gain).astype(BF16)
        live = col_ref[at, 0:1] >= 0
        cot = cot_ref[at, :]
        grad_low = jnp.where(live, cot, jnp.zeros_like(cot))
        b_s[at, :] = low
        g_s[at, :] = grad_low
        up = dot_t(low, wi_s[0:both, :])
        gate = dot_t(low, wi_s[both:, :])
        cdf = 0.5 * (1.0 + lax.erf(up * (1.0 / math.sqrt(2.0))))
        act = up * cdf
        hid = (act * gate).astype(BF16)
        slope = cdf + up * (jnp.exp(-0.5 * up * up) * (1.0 / math.sqrt(2.0 * math.pi)))
        grad_hid = dot_t(grad_low, wd_s[...])
        grad_up = (grad_hid * gate * slope).astype(BF16)
        grad_gate = (grad_hid * act).astype(BF16)
        out_ref[at, :] = (mixed + dot(hid, wd_s[...])).astype(BF16)
        grad_b = dot(grad_up, wi_s[0:both, :]) + dot(grad_gate, wi_s[both:, :])
        hid_s[at, :] = hid
        gu_s[at, :] = grad_up
        gg_s[at, :] = grad_gate
        gain_grad = gain_grad + jnp.sum(grad_b * normed, axis=0, keepdims=True)
        scaled = grad_b * gain
        grad_mixed = grad_low.astype(F32) + scale * (
            scaled
            - jnp.mean(scaled, axis=-1, keepdims=True)
            - normed * jnp.mean(scaled * normed, axis=-1, keepdims=True)
        )
        gm_ref[at, :] = grad_mixed
        grad_mixed_low = grad_mixed.astype(BF16)
        gml_s[at, :] = grad_mixed_low
        gao_ref[at, :] = dot_t(grad_mixed_low, wo_s[0:cols, :]).astype(BF16)
        gax_ref[at, :] = dot_t(grad_mixed_low, wo_s[cols:, :]).astype(BF16)
    gain_grad_ref[...] = jnp.broadcast_to(gain_grad, gain_grad_ref.shape)
    half = width // 2
    core = place_ref[CORE]
    n_b = n_d + n_o
    for a_ref, b_ref, which in ((as_ref, bs_ref, 1 - core), (ak_ref, bk_ref, core)):
        part = pl.ds(aligned(which * half, LANES), half)
        low, grad_low, grad_mixed_low = b_s[:, part], g_s[:, part], gml_s[:, part]
        for row, src in ((0, gu_s), (units, gg_s)):
            grad = t_dot(src[...], low).astype(BF16)
            a_ref[row : row + units, :] = grad[0:units]
            a_ref[both + row : both + row + units, :] = grad[units:]
        grad = t_dot(hid_s[...], grad_low).astype(BF16)
        for side, att_ref in enumerate((atto_ref, attx_ref)):
            grad_o = t_dot(att_ref[...], grad_mixed_low).astype(BF16)
            for quarter in range(4):
                to = (side * 4 + quarter) * n_b
                begin = side * units + quarter * n_d
                b_ref[to : to + n_d, :] = grad[begin : begin + n_d]
                b_ref[to + n_d : to + n_b, :] = grad_o[quarter * n_o : (quarter + 1) * n_o]


def middle(place, x, att_own, att_other, cot, col, gain, wo, wi, wd, pieces):
    rows, width = x.shape
    units, cols = wd.shape[0], wo.shape[0]
    size = 2 * cols * width + 6 * units * width
    half = width // 2
    return pl.pallas_call(
        middle_kernel,
        out_shape=(
            jax.ShapeDtypeStruct((rows, width), BF16),
            jax.ShapeDtypeStruct((rows, width), F32),
            jax.ShapeDtypeStruct((rows, cols), BF16),
            jax.ShapeDtypeStruct((rows, cols), BF16),
            jax.ShapeDtypeStruct((4 * units, half), BF16),
            jax.ShapeDtypeStruct((4 * units, half), BF16),
            jax.ShapeDtypeStruct((2 * (units + cols), half), BF16),
            jax.ShapeDtypeStruct((2 * (units + cols), half), BF16),
            jax.ShapeDtypeStruct((8, width), F32),
        ),
        in_specs=[SSPEC] + [VSPEC] * 13,
        out_specs=[VSPEC] * 9,
        scratch_shapes=[
            pltpu.VMEM((4 * units, width), BF16),
            pltpu.VMEM((2 * units, width), BF16),
            pltpu.VMEM((2 * cols, width), BF16),
            pltpu.VMEM((rows, width), BF16),
            pltpu.VMEM((rows, width), BF16),
            pltpu.VMEM((rows, width), BF16),
            pltpu.VMEM((rows, 2 * units), BF16),
            pltpu.VMEM((rows, 2 * units), BF16),
            pltpu.VMEM((rows, 2 * units), BF16),
        ],
        compiler_params=params(),
        cost_estimate=cost(6 * rows * size, 4 * size + 12 * rows * width, 4 * rows * units),
        name="middle",
    )(place, x, att_own, att_other, cot, col, gain, wo, wi, wd, *pieces)


def project_back_kernel(last, *refs):
    if last:
        (place_ref, x_ref, gain_ref, gq_ref, dk_ref, dv_ref, recv_ref, cos_ref, sin_ref, w_ref, prev_ref, gm_ref,
         keep_ref, send_ref, gx_ref, gain_grad_ref, low_s, gk_s, gv_s) = refs
    else:
        (place_ref, x_ref, gain_ref, gq_ref, dk_ref, dv_ref, recv_ref, cos_ref, sin_ref, w0, w1, w2, w3,
         keep_ref, send_ref, part_ref, low_s, gk_s, gv_s, w_ref) = refs
        load_pieces(place_ref, (w0, w1, w2, w3), w_ref)
    rows, width = x_ref.shape
    cols = gq_ref.shape[1]
    tile = min(256, rows)
    gain_grad = jnp.zeros((1, width), F32)
    gain = gain_ref[...]
    for begin in range(0, rows, tile):
        at = pl.ds(begin, tile)
        normed, scale = norm_parts(x_ref[at, :].astype(F32))
        low_s[at, :] = (normed * gain).astype(BF16)
        cosine, sine = cos_ref[at, :], sin_ref[at, :]
        for col in range(0, cols, LANES):
            part = slice(col, col + LANES)
            grad_k = dk_ref[at, part] + recv_ref[at, part].astype(F32)
            gk_s[at, part] = (grad_k * cosine - swap_halves(grad_k) * sine).astype(BF16)
        gv_s[at, :] = (dv_ref[at, :] + recv_ref[pl.ds(rows + begin, tile), :].astype(F32)).astype(BF16)
        total = dot_t(gq_ref[at, :], w_ref[0:width, :])
        total = total + dot_t(gk_s[at, :], w_ref[width : 2 * width, :])
        total = total + dot_t(gv_s[at, :], w_ref[2 * width : 3 * width, :])
        if last:
            total = total + prev_ref[at, :]
            gain_grad = gain_grad + jnp.sum(total * normed, axis=0, keepdims=True)
            scaled = total * gain
            gx_ref[at, :] = (
                gm_ref[at, :]
                + scale
                * (
                    scaled
                    - jnp.mean(scaled, axis=-1, keepdims=True)
                    - normed * jnp.mean(scaled * normed, axis=-1, keepdims=True)
                )
            ).astype(BF16)
        else:
            part_ref[at, :] = total
    if last:
        gain_grad_ref[...] = jnp.broadcast_to(gain_grad, gain_grad_ref.shape)
    half = width // 2
    size = half // 4
    core = place_ref[CORE]
    for to_ref, which in ((send_ref, 1 - core), (keep_ref, core)):
        low = low_s[:, pl.ds(aligned(which * half, LANES), half)]
        for item, src in enumerate((gq_ref, gk_s, gv_s)):
            grad = t_dot(low, src[...]).astype(BF16)
            for quarter in range(4):
                to = (quarter * 3 + item) * size
                to_ref[to : to + size, :] = grad[quarter * size : (quarter + 1) * size]


def project_back(place, x, gain, gq, dk, dv, received, cosine, sine, weights, previous=None, grad_mixed=None, after=()):
    rows, width = x.shape
    cols = gq.shape[1]
    last = previous is not None
    operands = [x, gain, gq, dk, dv, received, cosine, sine, *weights]
    shapes = [jax.ShapeDtypeStruct((3 * width // 2, cols), BF16)] * 2
    if last:
        operands += [previous, grad_mixed]
        shapes += [jax.ShapeDtypeStruct((rows, width), BF16), jax.ShapeDtypeStruct((8, width), F32)]
    else:
        shapes += [jax.ShapeDtypeStruct((rows, width), F32)]
    return pl.pallas_call(
        functools.partial(ordered, functools.partial(project_back_kernel, last), len(after)),
        out_shape=tuple(shapes),
        in_specs=[ANYSPEC] * len(after) + [SSPEC] + [VSPEC] * len(operands),
        out_specs=[VSPEC] * len(shapes),
        scratch_shapes=[
            pltpu.VMEM((rows, width), BF16),
            pltpu.VMEM((rows, cols), BF16),
            pltpu.VMEM((rows, cols), BF16),
        ]
        + ([] if last else [pltpu.VMEM((3 * width, cols), BF16)]),
        compiler_params=params(),
        cost_estimate=cost(12 * rows * width * cols, 12 * width * cols + 12 * rows * width),
        name="project_back_last" if last else "project_back",
    )(*after, place, *operands)


def pack(place, wi, wd, wo, after):
    sizes = [value.shape[0] // 4 for value in (wi, wd, wo)]
    width = wi.shape[1]

    def kernel(place_ref, _, wi_ref, wd_ref, wo_ref, out_ref):
        first, second = sizes[0], sizes[0] + sizes[1]
        out_ref[0:first, :] = wi_ref[...]
        out_ref[first:second, :] = wd_ref[...]
        out_ref[second:, :] = wo_ref[...]

    return pl.pallas_call(
        kernel,
        grid_spec=pltpu.PrefetchScalarGridSpec(
            num_scalar_prefetch=1,
            grid=(1,),
            in_specs=[ANYSPEC] + [pl.BlockSpec((size, width), lambda _, at: (at[PIECE], 0)) for size in sizes],
            out_specs=pl.BlockSpec((sum(sizes), width), lambda _, at: (0, 0)),
        ),
        out_shape=jax.ShapeDtypeStruct((sum(sizes), width), BF16),
        compiler_params=params("arbitrary"),
        cost_estimate=cost(0, 4 * sum(sizes) * width),
        name="pack",
    )(place, after, wi, wd, wo)


def add_kernel(parts, count, place_ref, *refs):
    ins, outs = refs[:count], refs[count:]
    size = outs[0].shape[0]
    if parts is None:
        outs[0][...] = sum(ref[0:size, :].astype(F32) for ref in ins).astype(BF16)
        return
    bit = place_ref[parts]
    for out_ref, which in ((outs[0], 1 - bit), (outs[1], bit)):
        at = pl.ds(aligned(which * size, 16), size)
        out_ref[...] = sum(ref[at, :].astype(F32) for ref in ins).astype(BF16)


def add(place, arrays, rows, firsts, split=None):
    cols = arrays[0].shape[1]
    size = rows if split is None else rows // 2
    count = 1 if split is None else 2

    def spec(first):
        return pl.BlockSpec((rows, cols), lambda _, at: (first, 0))

    shape = jax.ShapeDtypeStruct((size, cols), BF16)
    out_spec = pl.BlockSpec((size, cols), lambda _, at: (0, 0))
    out = pl.pallas_call(
        functools.partial(add_kernel, split, len(arrays)),
        grid_spec=pltpu.PrefetchScalarGridSpec(
            num_scalar_prefetch=1,
            grid=(1,),
            in_specs=[spec(first) for first in firsts],
            out_specs=[out_spec] * count,
        ),
        out_shape=(shape,) * count,
        compiler_params=params("arbitrary"),
        cost_estimate=cost(rows * cols * len(arrays), 2 * rows * cols * (len(arrays) + 1)),
        name="add",
    )(place, *arrays)
    return out if count == 2 else out[0]


def assemble_kernel(kind, place_ref, *refs):
    pieces, outs = refs[:8], refs[8:]
    core = place_ref[CORE]
    size = pieces[0].shape[0]
    for step, piece in enumerate(pieces):
        mine = step < 4
        quarter = place_ref[MINE if mine else THEIRS] ^ (step % 4)
        side = core if mine else 1 - core
        if kind == "qkv":
            rows = size // 3
            for item in range(3):
                at = pl.ds(aligned((side * 4 + quarter) * rows, 8), rows)
                outs[0][item, at, :] = piece[item * rows : (item + 1) * rows, :].astype(F32)
            continue
        half = outs[0].shape[1] // 2
        part = pl.ds(aligned(side * half, LANES), half)
        begin = 0
        for out_ref in outs:
            rows = out_ref.shape[0] // 4
            at = pl.ds(aligned(quarter * rows, 8), rows)
            out_ref[at, part] = piece[begin : begin + rows, :].astype(F32)
            begin += rows


def assemble(kind, place, pieces, shapes):
    total = sum(math.prod(shape) for shape in shapes)
    return pl.pallas_call(
        functools.partial(assemble_kernel, kind),
        out_shape=tuple(jax.ShapeDtypeStruct(shape, F32) for shape in shapes),
        in_specs=[SSPEC] + [VSPEC] * 8,
        out_specs=[VSPEC] * len(shapes),
        compiler_params=params(),
        cost_estimate=cost(0, 6 * total),
        name="assemble",
    )(place, *pieces)


def per_device(
    axis_sizes,
    hidden,
    seq_ids,
    cotangent,
    qkv_weight,
    attn_out_weight,
    mlp_in_weight,
    mlp_out_weight,
    norm1_gain,
    norm2_gain,
):
    dp_size, tensor_size = axis_sizes
    devices = dp_size * tensor_size
    chips = devices // 4
    chip_bits = chips.bit_length() - 1
    rows, width = hidden.shape
    cols = qkv_weight.shape[2]
    units = mlp_out_weight.shape[0]
    dp_at = lax.axis_index("dp")
    core = dp_at % 2
    chip = dp_at // 2

    def move(value, target):
        return lax.ppermute(value, ("dp", "tensor"), [(i, target(i)) for i in range(devices)])

    def swapped(i):
        return (i & ~3) | ((i & 1) << 1) | ((i >> 1) & 1)

    def to_tensor(i):
        return i ^ 1

    def to_core(i):
        return i ^ 2

    def to_near(i):
        return i ^ 4

    orders = (list(range(chip_bits)), list(range(1, chip_bits)) + [0])

    def stage_target(stage):
        return lambda i: i ^ (4 << orders[(i >> 1) & 1][stage])

    bits = [(chip >> b) % 2 for b in range(chip_bits)]
    quarters = [bits[order[0]] * 2 + bits[order[1]] for order in orders]
    near = chip % 2
    place = jnp.stack(
        [
            core,
            near * 2 + core,
            jnp.where(core == 0, quarters[0], quarters[1]),
            jnp.where(core == 0, quarters[1], quarters[0]),
            jnp.where(core == 0, bits[orders[0][0]], bits[orders[1][0]]),
            jnp.where(core == 0, bits[orders[0][1]], bits[orders[1][1]]),
        ]
    ).astype(jnp.int32)

    ids = move(seq_ids, swapped)
    x = move(hidden, swapped)
    ids_own = lax.dynamic_slice_in_dim(ids, core * rows, rows)
    ids_other = lax.dynamic_slice_in_dim(ids, (1 - core) * rows, rows)

    index = jnp.arange(ids.shape[0], dtype=jnp.int32)
    begins = jnp.zeros((rows,), jnp.int32)
    for number in (-1, 0, 1, 2):
        start = jnp.min(jnp.where(ids == number, index, ids.shape[0]))
        begins = jnp.where(ids_own == number, start, begins)
    pos = core * rows + jnp.arange(rows, dtype=jnp.int32) - begins
    frequency = jnp.power(ROPE_BASE, -2.0 * jnp.arange(HDIM // 2, dtype=F32) / HDIM)
    angles = pos.astype(F32)[:, None] * frequency[None, :]
    cosine, sine = jnp.cos(angles), jnp.sin(angles)
    cosine = jnp.concatenate([cosine] * 4, axis=1)
    sine = jnp.concatenate([-sine, sine] * 2, axis=1)
    col_own = jnp.broadcast_to(ids_own[:, None], (rows, LANES))
    col_other = jnp.broadcast_to(ids_other[:, None], (rows, LANES))
    row_own = jnp.broadcast_to(ids_own[None, :], (8, rows))
    row_other = jnp.broadcast_to(ids_other[None, :], (8, rows))

    def gather(piece):
        one = move(piece, to_tensor)
        two = move(one, to_near)
        return one, move(one, to_core), two, move(two, to_core)

    w_qkv = qkv_weight.reshape(3 * width, cols)
    w_in = jnp.swapaxes(mlp_in_weight, 1, 2).reshape(2 * units, width)
    size = w_qkv.shape[0] // 4
    w_qkv_x = gather(lax.dynamic_slice_in_dim(w_qkv, (near * 2 + core) * size, size))
    w_rest_x = gather(pack(place, w_in, mlp_out_weight, attn_out_weight, x))
    cot = move(cotangent, swapped)
    gain1, gain2 = norm1_gain[None, :], norm2_gain[None, :]

    q_a, kv_a = project(place, x, gain1, [w_qkv], cosine, sine)
    kv_a_x = move(kv_a, to_core)
    o_a, lse_a = attend(q_a, kv_a, kv_a_x, col_own, row_own, row_other)
    q_b, kv_b = project(place, x, gain1, w_qkv_x, cosine, sine)
    kv_b_x = move(kv_b, to_core)
    o_b, lse_b = attend(q_b, kv_b, kv_b_x, col_own, row_own, row_other)
    out, grad_mixed, go_a, go_b, in_keep, in_send, rest_keep, rest_send, gain2_part = middle(
        place, x, o_a, o_b, cot, col_own, gain2, attn_out_weight, w_in, mlp_out_weight, w_rest_x
    )
    out = move(out, swapped)

    def reduce_chips(arrays, size, firsts):
        sent, kept = add(place, arrays, size, firsts, FIRST)
        got = move(sent, stage_target(0))
        sent, kept = add(place, [kept, got], size // 2, [0, 0], SECOND)
        got = move(sent, stage_target(1))
        total = add(place, [kept, got], size // 4, [0, 0])
        for stage in range(2, chip_bits):
            total = add(place, [total, move(total, stage_target(stage))], size // 4, [0, 0])
        one = move(total, stage_target(1))
        two = move(total, stage_target(0))
        three = move(one, stage_target(0))
        mine = [total, one, two, three]
        return mine + [move(piece, to_core) for piece in mine]

    in_size, rest_size, qkv_size = 2 * units, units + cols, 3 * width // 2
    in_got = move(in_send, to_core)
    rest_got = move(rest_send, to_core)
    in_got_x = move(add(place, [in_keep, in_got], in_size, [1, 1]), to_tensor)
    rest_got_x = move(add(place, [rest_keep, rest_got], rest_size, [1, 1]), to_tensor)
    in_pieces = reduce_chips([in_keep, in_got, in_got_x], in_size, [0, 0, 0])
    rest_pieces = reduce_chips([rest_keep, rest_got, rest_got_x], rest_size, [0, 0, 0])

    def back(q, kv, kv_x, go, o, lse, after):
        gq, dk, dv, dkx, dvx = attend_back(
            q, kv, kv_x, go, o, lse, col_own, col_other, row_own, cosine, sine, after
        )
        return gq, dk, dv, move(jnp.concatenate([dkx, dvx]), to_core)

    gq_b, dk_b, dv_b, recv_b = back(q_b, kv_b, kv_b_x, go_b, o_b, lse_b, [in_got, rest_got])
    keep_b, send_b, grad_a_part = project_back(
        place, x, gain1, gq_b, dk_b, dv_b, recv_b, cosine, sine, w_qkv_x
    )
    gq_a, dk_a, dv_a, recv_a = back(q_a, kv_a, kv_a_x, go_a, o_a, lse_a, [in_got_x])
    keep_a, send_a, input_grad, gain1_part = project_back(
        place, x, gain1, gq_a, dk_a, dv_a, recv_a, cosine, sine, [w_qkv], grad_a_part, grad_mixed, [rest_got_x]
    )
    input_grad = move(input_grad, swapped)
    qkv_got_x = move(add(place, [keep_b, move(send_b, to_core)], qkv_size, [0, 0]), to_tensor)
    qkv_pieces = reduce_chips([keep_a, move(send_a, to_core), qkv_got_x], qkv_size, [0, 0, 0])

    gains = jnp.concatenate([gain1_part[0:1], gain2_part[0:1]])
    for mask in [2, 1] + [4 << b for b in range(chip_bits)]:
        gains = gains + move(gains, functools.partial(lambda m, i: i ^ m, mask))
    (g_in,) = assemble("in", place, in_pieces, [(2 * units, width)])
    g_down, g_out = assemble("rest", place, rest_pieces, [(units, width), (cols, width)])
    (g_qkv,) = assemble("qkv", place, qkv_pieces, [(3, width, cols)])
    return (
        out,
        input_grad,
        gains[0],
        gains[1],
        g_qkv,
        g_out,
        jnp.swapaxes(g_in.reshape(2, units, width), 1, 2),
        g_down,
    )


def solution(mesh):
    in_specs = (
        P(("dp", "tensor"), None),
        P("dp"),
        P(("dp", "tensor"), None),
        P(None, None, "tensor"),
        P("tensor", None),
        P(None, None, "tensor"),
        P("tensor", None),
        P(),
        P(),
    )
    out_specs = (
        P(("dp", "tensor"), None),
        P(("dp", "tensor"), None),
        P(),
        P(),
        P(None, None, "tensor"),
        P("tensor", None),
        P(None, None, "tensor"),
        P("tensor", None),
    )
    return jax.shard_map(
        functools.partial(per_device, (mesh.shape["dp"], mesh.shape["tensor"])),
        mesh=mesh,
        in_specs=in_specs,
        out_specs=out_specs,
        check_vma=False,
    )
```

```python
import functools
import math

import jax
import jax.numpy as jnp
from jax import lax
from jax.experimental import pallas as pl
from jax.experimental.pallas import tpu as pltpu
from jax.sharding import PartitionSpec as P

HDIM = 64
LANES = 128
EPSILON = 1e-05
ROPE_BASE = 160000.0
MASKED = -1e30
F32 = jnp.float32
BF16 = jnp.bfloat16
MIB = 1024 * 1024


def dot(left, right):
    return jnp.dot(left, right, preferred_element_type=F32)


def dot_t(left, right):
    return lax.dot_general(left, right, (((1,), (1,)), ((), ())), preferred_element_type=F32)


def t_dot(left, right):
    return lax.dot_general(left, right, (((0,), (0,)), ((), ())), preferred_element_type=F32)


def norm_parts(values):
    center = values - jnp.mean(values, axis=-1, keepdims=True)
    spread = jnp.mean(center * center, axis=-1, keepdims=True)
    scale = lax.rsqrt(spread + EPSILON)
    return center * scale, scale


def swap_halves(values):
    lane = lax.broadcasted_iota(jnp.int32, values.shape, 1) % HDIM
    return jnp.where(
        lane < HDIM // 2,
        pltpu.roll(values, LANES - HDIM // 2, 1),
        pltpu.roll(values, HDIM // 2, 1),
    )


def low_lanes(shape):
    return lax.broadcasted_iota(jnp.int32, shape, 1) < HDIM


def cost(flops, nbytes, trans=0):
    return pl.CostEstimate(flops=int(flops) // 8, bytes_accessed=int(nbytes) // 8, transcendentals=int(trans) // 8)


def params(mib=20, semantics=None):
    return pltpu.CompilerParams(vmem_limit_bytes=mib * MIB, dimension_semantics=semantics)


VSPEC = pl.BlockSpec(memory_space=pltpu.VMEM)
SSPEC = pl.BlockSpec(memory_space=pltpu.SMEM)
ANYSPEC = pl.BlockSpec(memory_space=pl.ANY)
CORE, PIECE, MINE, THEIRS, ONE, TWO, THREE, FIRST, SECOND = range(9)


def aligned(value, by):
    return pl.multiple_of(value, by)


def side_block(core, side, quarter):
    return jnp.where(core == 0, side * 4 + quarter, (quarter // 2) * 4 + side * 2 + quarter % 2)


def ordered(kernel, count, *refs):
    kernel(*refs[count:])


def load_pieces(place_ref, pieces, w_s):
    size = pieces[0].shape[0]
    for step, piece in enumerate(pieces):
        at = (place_ref[PIECE] ^ step) * size
        w_s[pl.ds(aligned(at, 16), size), :] = piece[...]


def project_kernel(gathered, *refs):
    if gathered:
        place_ref, x_ref, gain_ref, w0, w1, w2, w3, cos_ref, sin_ref, q_ref, kv_ref, w_ref = refs
        load_pieces(place_ref, (w0, w1, w2, w3), w_ref)
    else:
        place_ref, x_ref, gain_ref, w_ref, cos_ref, sin_ref, q_ref, kv_ref = refs
    rows, width = x_ref.shape
    cols = q_ref.shape[1]
    tile = min(256, rows)
    for begin in range(0, rows, tile):
        at = pl.ds(begin, tile)
        normed, _ = norm_parts(x_ref[at, :].astype(F32))
        low = (normed * gain_ref[...]).astype(BF16)
        cosine, sine = cos_ref[at, :], sin_ref[at, :]
        q_raw = dot(low, w_ref[0:width, :])
        k_raw = dot(low, w_ref[width : 2 * width, :])
        kv_ref[pl.ds(rows + begin, tile), :] = dot(low, w_ref[2 * width : 3 * width, :]).astype(BF16)
        for col in range(0, cols, LANES):
            part = slice(col, col + LANES)
            q_part, k_part = q_raw[:, part], k_raw[:, part]
            q_ref[at, part] = (
                (q_part * cosine + swap_halves(q_part) * sine).astype(BF16) * (1.0 / math.sqrt(HDIM))
            ).astype(BF16)
            kv_ref[at, part] = (k_part * cosine + swap_halves(k_part) * sine).astype(BF16)


def project(place, x, gain, weights, cosine, sine, after=()):
    rows, width = x.shape
    cols = weights[0].shape[1]
    gathered = len(weights) > 1
    operands = [place, x, gain, *weights, cosine, sine]
    return pl.pallas_call(
        functools.partial(ordered, functools.partial(project_kernel, gathered), len(after)),
        out_shape=(
            jax.ShapeDtypeStruct((rows, cols), BF16),
            jax.ShapeDtypeStruct((2 * rows, cols), BF16),
        ),
        in_specs=[ANYSPEC] * len(after) + [SSPEC] + [VSPEC] * (len(operands) - 1),
        out_specs=[VSPEC] * 2,
        scratch_shapes=[pltpu.VMEM((3 * width, cols), BF16)] if gathered else [],
        compiler_params=params(),
        cost_estimate=cost(2 * rows * width * cols * 3, 6 * width * cols + 8 * rows * width),
        name="project",
    )(*after, *operands)


def attend_kernel(q_ref, ko_ref, vo_ref, kx_ref, vx_ref, col_ref, row_ref, rowx_ref, o_ref, lse_ref, bo_ref, bx_ref):
    rows = q_ref.shape[0]
    tile = min(256, rows)

    @pl.when(pl.program_id(0) == 0)
    def _():
        col = col_ref[...][:, 0:1]
        bo_ref[...] = jnp.where(col == row_ref[0:1, :], 0.0, MASKED)
        bx_ref[...] = jnp.where(col == rowx_ref[0:1, :], 0.0, MASKED)

    for begin in range(0, rows, tile):
        at = pl.ds(begin, tile)
        low = low_lanes((tile, LANES))
        q_pair = q_ref[at, :]
        results, logs = [], []
        for head in range(2):
            chosen = low if head == 0 else jnp.logical_not(low)
            query = jnp.where(chosen, q_pair, jnp.zeros_like(q_pair))
            own = dot_t(query, ko_ref[...]) + bo_ref[at, :]
            other = dot_t(query, kx_ref[...]) + bx_ref[at, :]
            highest = jnp.maximum(
                jnp.max(own, axis=-1, keepdims=True), jnp.max(other, axis=-1, keepdims=True)
            )
            own = jnp.exp(own - highest)
            other = jnp.exp(other - highest)
            totals = jnp.sum(own, axis=-1, keepdims=True) + jnp.sum(other, axis=-1, keepdims=True)
            value = dot(own.astype(BF16), vo_ref[...]) + dot(other.astype(BF16), vx_ref[...])
            results.append(value / totals)
            logs.append(highest + jnp.log(totals))
        o_ref[at, :] = jnp.where(low, results[0], results[1]).astype(BF16)
        lse_ref[at, :] = jnp.where(low, logs[0], logs[1])


def attend(q, kv_own, kv_other, col, row, row_other, after=()):
    rows, cols = q.shape
    pairs = cols // LANES
    tok = pl.BlockSpec((rows, LANES), lambda p: (0, p))
    tok_v = pl.BlockSpec((rows, LANES), lambda p: (1, p))
    return pl.pallas_call(
        functools.partial(ordered, attend_kernel, len(after)),
        grid=(pairs,),
        out_shape=(
            jax.ShapeDtypeStruct((rows, cols), BF16),
            jax.ShapeDtypeStruct((rows, cols), F32),
        ),
        in_specs=[ANYSPEC] * len(after)
        + [
            tok,
            tok,
            tok_v,
            tok,
            tok_v,
            pl.BlockSpec((rows, LANES), lambda p: (0, 0)),
            pl.BlockSpec((8, rows), lambda p: (0, 0)),
            pl.BlockSpec((8, rows), lambda p: (0, 0)),
        ],
        out_specs=[tok, tok],
        scratch_shapes=[pltpu.VMEM((rows, rows), F32), pltpu.VMEM((rows, rows), F32)],
        compiler_params=params(semantics=("arbitrary",)),
        cost_estimate=cost(
            4 * rows * 2 * rows * cols * 4, 12 * rows * cols, 2 * rows * rows * cols // HDIM
        ),
        name="attend",
    )(*after, q, kv_own, kv_own, kv_other, kv_other, col, row, row_other)


def attend_back_kernel(
    q_ref, ko_ref, vo_ref, kx_ref, vx_ref, do_ref, o_ref, lse_ref, col_ref, colx_ref, row_ref, cos_ref, sin_ref,
    gq_ref, dko_ref, dvo_ref, dx_ref, bo_ref, bx_ref,
):
    rows = q_ref.shape[0]
    tile = min(256, rows)

    @pl.when(pl.program_id(0) == 0)
    def _():
        row = row_ref[0:1, :]
        bo_ref[...] = jnp.where(col_ref[...][:, 0:1] == row, 0.0, MASKED)
        bx_ref[...] = jnp.where(colx_ref[...][:, 0:1] == row, 0.0, MASKED)

    low = low_lanes((rows, LANES))
    q_pair, do_pair = q_ref[...], do_ref[...]
    product = do_pair.astype(F32) * o_ref[...].astype(F32)
    first = jnp.sum(jnp.where(low, product, 0.0), axis=-1, keepdims=True)
    second = jnp.sum(jnp.where(low, 0.0, product), axis=-1, keepdims=True)
    delta_t = jnp.transpose(jnp.where(low, first, second))
    lse_t = jnp.transpose(lse_ref[...])
    low_tile = low_lanes((tile, LANES))
    grad_q = jnp.zeros((rows, LANES), F32)
    for k_ref, v_ref, bias_ref, dk_ref, dv_ref in (
        (ko_ref, vo_ref, bo_ref, dko_ref, dvo_ref),
        (kx_ref, vx_ref, bx_ref, dx_ref.at[0], dx_ref.at[1]),
    ):
        for begin in range(0, rows, tile):
            at = pl.ds(begin, tile)
            k_pair, v_pair = k_ref[at, :], v_ref[at, :]
            grad_k = grad_v = None
            for head in range(2):
                chosen = low_tile if head == 0 else jnp.logical_not(low_tile)
                chosen_q = low if head == 0 else jnp.logical_not(low)
                key = jnp.where(chosen, k_pair, jnp.zeros_like(k_pair))
                value = jnp.where(chosen, v_pair, jnp.zeros_like(v_pair))
                query = jnp.where(chosen_q, q_pair, jnp.zeros_like(q_pair))
                grad_o = jnp.where(chosen_q, do_pair, jnp.zeros_like(do_pair))
                at_row = head * HDIM
                scores = dot_t(key, q_pair) + bias_ref[at, :]
                probs = jnp.exp(scores - lse_t[at_row : at_row + 1, :])
                grad_probs = dot_t(value, do_pair)
                grad_scores = (probs * (grad_probs - delta_t[at_row : at_row + 1, :])).astype(BF16)
                term_v = dot(probs.astype(BF16), grad_o)
                term_k = dot(grad_scores, query)
                grad_v = term_v if grad_v is None else grad_v + term_v
                grad_k = term_k if grad_k is None else grad_k + term_k
                grad_q = grad_q + t_dot(grad_scores, key)
            dk_ref[at, :] = grad_k.astype(dk_ref.dtype)
            dv_ref[at, :] = grad_v.astype(dv_ref.dtype)
    grad_q = grad_q * (1.0 / math.sqrt(HDIM))
    gq_ref[...] = (grad_q * cos_ref[...] - swap_halves(grad_q) * sin_ref[...]).astype(BF16)


def attend_back(q, kv_own, kv_other, grad_o, o, lse, col, col_other, row, cosine, sine, after=()):
    rows, cols = q.shape
    pairs = cols // LANES
    tok = pl.BlockSpec((rows, LANES), lambda p: (0, p))
    tok_v = pl.BlockSpec((rows, LANES), lambda p: (1, p))
    fixed = pl.BlockSpec((rows, LANES), lambda p: (0, 0))
    return pl.pallas_call(
        functools.partial(ordered, attend_back_kernel, len(after)),
        grid=(pairs,),
        out_shape=(
            jax.ShapeDtypeStruct((rows, cols), BF16),
            jax.ShapeDtypeStruct((rows, cols), F32),
            jax.ShapeDtypeStruct((rows, cols), F32),
            jax.ShapeDtypeStruct((2, rows, cols), BF16),
        ),
        in_specs=[ANYSPEC] * len(after)
        + [
            tok, tok, tok_v, tok, tok_v, tok, tok, tok, fixed, fixed,
            pl.BlockSpec((8, rows), lambda p: (0, 0)), fixed, fixed,
        ],
        out_specs=[tok] * 3 + [pl.BlockSpec((2, rows, LANES), lambda p: (0, 0, p))],
        scratch_shapes=[pltpu.VMEM((rows, rows), F32), pltpu.VMEM((rows, rows), F32)],
        compiler_params=params(semantics=("arbitrary",)),
        cost_estimate=cost(
            10 * rows * 2 * rows * cols * 4, 30 * rows * cols, 2 * rows * rows * cols // HDIM
        ),
        name="attend_back",
    )(*after, q, kv_own, kv_own, kv_other, kv_other, grad_o, o, lse, col, col_other, row, cosine, sine)


def middle_kernel(
    place_ref, x_ref, atto_ref, attx_ref, cot_ref, col_ref, gain_ref, wo_ref, wi_ref, wd_ref,
    i0, i1, i2, i3, r0, r1, r2, r3,
    out_ref, gm_ref, gao_ref, gax_ref, ak_ref, as_ref, gain_grad_ref, g_s, gml_s, hid_s,
    wi_s, wd_s, wo_s, b_s, gu_s, gg_s,
):
    rows, width = x_ref.shape
    units, cols = wd_ref.shape[0], wo_ref.shape[0]
    both = 2 * units
    wi_s[0:units, :] = wi_ref[0:units, :]
    wi_s[both : both + units, :] = wi_ref[units:both, :]
    wd_s[0:units, :] = wd_ref[...]
    wo_s[0:cols, :] = wo_ref[...]
    n_i, n_d, n_o = both // 4, units // 4, cols // 4
    for step, (piece_i, piece) in enumerate(((i0, r0), (i1, r1), (i2, r2), (i3, r3))):
        at = place_ref[PIECE] ^ step
        to_i = units + (at % 2) * n_i + (at // 2) * both
        wi_s[pl.ds(aligned(to_i, 16), n_i), :] = piece_i[...]
        wd_s[pl.ds(aligned(units + at * n_d, 16), n_d), :] = piece[0:n_d, :]
        wo_s[pl.ds(aligned(cols + at * n_o, 16), n_o), :] = piece[n_d:, :]
    tile = min(256, rows)
    gain = gain_ref[...]
    gain_grad = jnp.zeros((1, width), F32)
    for begin in range(0, rows, tile):
        at = pl.ds(begin, tile)
        mixed = x_ref[at, :].astype(F32) + dot(atto_ref[at, :], wo_s[0:cols, :]) + dot(attx_ref[at, :], wo_s[cols:, :])
        normed, scale = norm_parts(mixed)
        low = (normed * gain).astype(BF16)
        live = col_ref[at, 0:1] >= 0
        cot = cot_ref[at, :]
        grad_low = jnp.where(live, cot, jnp.zeros_like(cot))
        b_s[at, :] = low
        g_s[at, :] = grad_low
        up = dot_t(low, wi_s[0:both, :])
        gate = dot_t(low, wi_s[both:, :])
        cdf = 0.5 * (1.0 + lax.erf(up * (1.0 / math.sqrt(2.0))))
        act = up * cdf
        hid = (act * gate).astype(BF16)
        slope = cdf + up * (jnp.exp(-0.5 * up * up) * (1.0 / math.sqrt(2.0 * math.pi)))
        grad_hid = dot_t(grad_low, wd_s[...])
        grad_up = (grad_hid * gate * slope).astype(BF16)
        grad_gate = (grad_hid * act).astype(BF16)
        out_ref[at, :] = (mixed + dot(hid, wd_s[...])).astype(BF16)
        grad_b = dot(grad_up, wi_s[0:both, :]) + dot(grad_gate, wi_s[both:, :])
        hid_s[at, :] = hid
        gu_s[at, :] = grad_up
        gg_s[at, :] = grad_gate
        gain_grad = gain_grad + jnp.sum(grad_b * normed, axis=0, keepdims=True)
        scaled = grad_b * gain
        grad_mixed = grad_low.astype(F32) + scale * (
            scaled
            - jnp.mean(scaled, axis=-1, keepdims=True)
            - normed * jnp.mean(scaled * normed, axis=-1, keepdims=True)
        )
        gm_ref[at, :] = grad_mixed
        grad_mixed_low = grad_mixed.astype(BF16)
        gml_s[at, :] = grad_mixed_low
        gao_ref[at, :] = dot_t(grad_mixed_low, wo_s[0:cols, :]).astype(BF16)
        gax_ref[at, :] = dot_t(grad_mixed_low, wo_s[cols:, :]).astype(BF16)
    gain_grad_ref[...] = jnp.broadcast_to(gain_grad, gain_grad_ref.shape)
    half = width // 2
    core = place_ref[CORE]
    for a_ref, which in ((as_ref, 1 - core), (ak_ref, core)):
        low = b_s[:, pl.ds(aligned(which * half, LANES), half)]
        for row, src in ((0, gu_s), (units, gg_s)):
            grad = t_dot(src[...], low).astype(BF16)
            for side in range(2):
                for quarter in range(2):
                    at = side_block(which, side, row // n_i + quarter) * n_i
                    begin = side * units + quarter * n_i
                    a_ref[pl.ds(aligned(at, 16), n_i), :] = grad[begin : begin + n_i]


def outer_kernel(place_ref, atto_ref, attx_ref, hid_ref, g_ref, gml_ref, bk_ref, bs_ref):
    half = g_ref.shape[1] // 2
    units, cols = hid_ref.shape[1] // 2, atto_ref.shape[1]
    n_d, n_o = units // 4, cols // 4
    n_b = n_d + n_o
    core = place_ref[CORE]
    for b_ref, which in ((bs_ref, 1 - core), (bk_ref, core)):
        part = pl.ds(aligned(which * half, LANES), half)
        grad = t_dot(hid_ref[...], g_ref[:, part]).astype(BF16)
        grad_mixed_low = gml_ref[:, part]
        for side, att_ref in enumerate((atto_ref, attx_ref)):
            grad_o = t_dot(att_ref[...], grad_mixed_low).astype(BF16)
            for quarter in range(4):
                to = side_block(which, side, quarter) * n_b
                begin = side * units + quarter * n_d
                b_ref[pl.ds(aligned(to, 16), n_d), :] = grad[begin : begin + n_d]
                b_ref[pl.ds(aligned(to + n_d, 16), n_o), :] = grad_o[quarter * n_o : (quarter + 1) * n_o]


def outer(place, att_own, att_other, hid, g, gml):
    rows, width = g.shape
    size = hid.shape[1] + 2 * att_own.shape[1]
    return pl.pallas_call(
        outer_kernel,
        out_shape=(jax.ShapeDtypeStruct((size, width // 2), BF16),) * 2,
        in_specs=[SSPEC] + [VSPEC] * 5,
        out_specs=[VSPEC] * 2,
        compiler_params=params(),
        cost_estimate=cost(2 * rows * width * size, 2 * size * width),
        name="outer",
    )(place, att_own, att_other, hid, g, gml)


def middle(place, x, att_own, att_other, cot, col, gain, wo, wi, wd, pieces_i, pieces):
    rows, width = x.shape
    units, cols = wd.shape[0], wo.shape[0]
    size = 2 * cols * width + 6 * units * width
    half = width // 2
    return pl.pallas_call(
        middle_kernel,
        out_shape=(
            jax.ShapeDtypeStruct((rows, width), BF16),
            jax.ShapeDtypeStruct((rows, width), F32),
            jax.ShapeDtypeStruct((rows, cols), BF16),
            jax.ShapeDtypeStruct((rows, cols), BF16),
            jax.ShapeDtypeStruct((4 * units, half), BF16),
            jax.ShapeDtypeStruct((4 * units, half), BF16),
            jax.ShapeDtypeStruct((8, width), F32),
            jax.ShapeDtypeStruct((rows, width), BF16),
            jax.ShapeDtypeStruct((rows, width), BF16),
            jax.ShapeDtypeStruct((rows, 2 * units), BF16),
        ),
        in_specs=[SSPEC] + [VSPEC] * 17,
        out_specs=[VSPEC] * 10,
        scratch_shapes=[
            pltpu.VMEM((4 * units, width), BF16),
            pltpu.VMEM((2 * units, width), BF16),
            pltpu.VMEM((2 * cols, width), BF16),
            pltpu.VMEM((rows, width), BF16),
            pltpu.VMEM((rows, 2 * units), BF16),
            pltpu.VMEM((rows, 2 * units), BF16),
        ],
        compiler_params=params(50),
        cost_estimate=cost(6 * rows * size, 4 * size + 12 * rows * width, 4 * rows * units),
        name="middle",
    )(place, x, att_own, att_other, cot, col, gain, wo, wi, wd, *pieces_i, *pieces)


def qkv_grads(place_ref, x_ref, gain_ref, gq_ref, dk_ref, dv_ref, recv_ref, cos_ref, sin_ref,
              keep_ref, send_ref, gk_ref, gv_ref, low_s):
    rows, width = x_ref.shape
    cols = gq_ref.shape[1]
    tile = min(256, rows)
    for begin in range(0, rows, tile):
        at = pl.ds(begin, tile)
        normed, _ = norm_parts(x_ref[at, :].astype(F32))
        low_s[at, :] = (normed * gain_ref[...]).astype(BF16)
        cosine, sine = cos_ref[at, :], sin_ref[at, :]
        for col in range(0, cols, LANES):
            part = slice(col, col + LANES)
            grad_k = dk_ref[at, part] + recv_ref[0, at, part].astype(F32)
            gk_ref[at, part] = (grad_k * cosine - swap_halves(grad_k) * sine).astype(BF16)
        gv_ref[at, :] = (dv_ref[at, :] + recv_ref[1, at, :].astype(F32)).astype(BF16)
    half = width // 2
    size = half // 4
    core = place_ref[CORE]
    for to_ref, which in ((send_ref, 1 - core), (keep_ref, core)):
        low = low_s[:, pl.ds(aligned(which * half, LANES), half)]
        for item, src in enumerate((gq_ref, gk_ref, gv_ref)):
            grad = t_dot(low, src[...]).astype(BF16)
            for quarter in range(4):
                to = (quarter * 3 + item) * size
                to_ref[to : to + size, :] = grad[quarter * size : (quarter + 1) * size]


def project_grads(place, x, gain, gq, dk, dv, received, cosine, sine, after=()):
    rows, width = x.shape
    cols = gq.shape[1]
    operands = [x, gain, gq, dk, dv, received, cosine, sine]
    return pl.pallas_call(
        functools.partial(ordered, qkv_grads, len(after)),
        out_shape=(jax.ShapeDtypeStruct((3 * width // 2, cols), BF16),) * 2
        + (jax.ShapeDtypeStruct((rows, cols), BF16),) * 2,
        in_specs=[ANYSPEC] * len(after) + [SSPEC] + [VSPEC] * len(operands),
        out_specs=[VSPEC] * 4,
        scratch_shapes=[pltpu.VMEM((rows, width), BF16)],
        compiler_params=params(24),
        cost_estimate=cost(6 * rows * width * cols, 12 * width * cols + 12 * rows * width),
        name="project_grads",
    )(*after, place, *operands)


def project_back_kernel(
    place_ref, x_ref, gain_ref, gq_ref, dk_ref, dv_ref, recv_ref, cos_ref, sin_ref, w_ref,
    gqx_ref, gkx_ref, gvx_ref, w0, w1, w2, w3, gm_ref,
    keep_ref, send_ref, gx_ref, gain_grad_ref, low_s, gk_s, gv_s, wx_s,
):
    qkv_grads(place_ref, x_ref, gain_ref, gq_ref, dk_ref, dv_ref, recv_ref, cos_ref, sin_ref,
              keep_ref, send_ref, gk_s, gv_s, low_s)
    load_pieces(place_ref, (w0, w1, w2, w3), wx_s)
    rows, width = x_ref.shape
    tile = min(256, rows)
    gain = gain_ref[...]
    gain_grad = jnp.zeros((1, width), F32)
    for begin in range(0, rows, tile):
        at = pl.ds(begin, tile)
        normed, scale = norm_parts(x_ref[at, :].astype(F32))
        total = jnp.zeros((tile, width), F32)
        for item, (own, other) in enumerate(((gq_ref, gqx_ref), (gk_s, gkx_ref), (gv_s, gvx_ref))):
            part = slice(item * width, (item + 1) * width)
            total = total + dot_t(own[at, :], w_ref[part, :]) + dot_t(other[at, :], wx_s[part, :])
        gain_grad = gain_grad + jnp.sum(total * normed, axis=0, keepdims=True)
        scaled = total * gain
        gx_ref[at, :] = (
            gm_ref[at, :]
            + scale
            * (
                scaled
                - jnp.mean(scaled, axis=-1, keepdims=True)
                - normed * jnp.mean(scaled * normed, axis=-1, keepdims=True)
            )
        ).astype(BF16)
    gain_grad_ref[...] = jnp.broadcast_to(gain_grad, gain_grad_ref.shape)


def project_back(place, x, gain, gq, dk, dv, received, cosine, sine, weight, others, pieces, grad_mixed, after):
    rows, width = x.shape
    cols = gq.shape[1]
    operands = [x, gain, gq, dk, dv, received, cosine, sine, weight, *others, *pieces, grad_mixed]
    return pl.pallas_call(
        functools.partial(ordered, project_back_kernel, len(after)),
        out_shape=(
            jax.ShapeDtypeStruct((3 * width // 2, cols), BF16),
            jax.ShapeDtypeStruct((3 * width // 2, cols), BF16),
            jax.ShapeDtypeStruct((rows, width), BF16),
            jax.ShapeDtypeStruct((8, width), F32),
        ),
        in_specs=[ANYSPEC] * len(after) + [SSPEC] + [VSPEC] * len(operands),
        out_specs=[VSPEC] * 4,
        scratch_shapes=[
            pltpu.VMEM((rows, width), BF16),
            pltpu.VMEM((rows, cols), BF16),
            pltpu.VMEM((rows, cols), BF16),
            pltpu.VMEM((3 * width, cols), BF16),
        ],
        compiler_params=params(32),
        cost_estimate=cost(18 * rows * width * cols, 12 * width * cols + 12 * rows * width),
        name="project_back",
    )(*after, place, *operands)


def pack(place, weights, after=()):
    sizes = [value.shape[0] // 4 for value in weights]
    width = weights[0].shape[1]

    def kernel(place_ref, *refs):
        begin = 0
        for ref, size in zip(refs[len(after) :], sizes):
            refs[-1][begin : begin + size, :] = ref[...]
            begin += size

    return pl.pallas_call(
        kernel,
        grid_spec=pltpu.PrefetchScalarGridSpec(
            num_scalar_prefetch=1,
            grid=(1,),
            in_specs=[ANYSPEC] * len(after)
            + [pl.BlockSpec((size, width), lambda _, at: (at[PIECE], 0)) for size in sizes],
            out_specs=pl.BlockSpec((sum(sizes), width), lambda _, at: (0, 0)),
        ),
        out_shape=jax.ShapeDtypeStruct((sum(sizes), width), BF16),
        compiler_params=params(semantics=("arbitrary",)),
        cost_estimate=cost(0, 4 * sum(sizes) * width),
        name="pack",
    )(place, *after, *weights)


def merge_kernel(jobs, after, place_ref, *refs):
    ins = list(refs[after : after + sum(job["count"] for job in jobs)])
    outs = list(refs[after + len(ins) :])
    for job in jobs:
        mine, ins = ins[: job["count"]], ins[job["count"] :]
        which = job["which"]
        if which is None:
            out_ref, outs = outs[0], outs[1:]
            out_ref[...] = sum(ref[...].astype(F32) for ref in mine).astype(out_ref.dtype)
            continue
        size = outs[0].shape[0]
        bit = place_ref[which]
        for out_ref, half in ((outs[0], 1 - bit), (outs[1], bit)):
            at = pl.ds(aligned(half * size, 16), size)
            total = sum(ref[at, :].astype(F32) for ref in (mine[:-2] if which == FIRST else mine))
            if which == FIRST:
                total = total + jnp.where(half == 0, mine[-2][...], mine[-1][...]).astype(F32)
            out_ref[...] = total.astype(BF16)
        outs = outs[2:]


def merge(place, *jobs, after=()):
    arrays, shapes, notes = [], [], []
    for values, which in jobs:
        rows, cols = values[0].shape
        parts = 1 if which is None else 2
        shapes += [jax.ShapeDtypeStruct((rows // parts, cols), values[0].dtype)] * parts
        notes.append({"count": len(values), "which": which})
        arrays += values
    out = pl.pallas_call(
        functools.partial(merge_kernel, notes, len(after)),
        out_shape=tuple(shapes),
        in_specs=[SSPEC] + [ANYSPEC] * len(after) + [VSPEC] * len(arrays),
        out_specs=[VSPEC] * len(shapes),
        compiler_params=params(),
        cost_estimate=cost(0, sum(2 * value.size for value in arrays)),
        name="merge",
    )(place, *after, *arrays)
    return out


def join_kernel(*refs):
    size = refs[0].shape[0]
    for step, ref in enumerate(refs[:-1]):
        refs[-1][step * size : (step + 1) * size, :] = ref[...]


def join(values):
    rows, cols = values[0].shape
    return pl.pallas_call(
        join_kernel,
        out_shape=jax.ShapeDtypeStruct((len(values) * rows, cols), BF16),
        in_specs=[VSPEC] * len(values),
        out_specs=VSPEC,
        compiler_params=params(),
        cost_estimate=cost(0, 4 * len(values) * rows * cols),
        name="join",
    )(*values)


def forward_kernel(count, *refs):
    size = (len(refs) - count) // 2
    for left, right in zip(refs[count : count + size], refs[count + size :]):
        right[...] = left[...]


def forward(values, after):
    return pl.pallas_call(
        functools.partial(forward_kernel, len(after)),
        out_shape=tuple(jax.ShapeDtypeStruct(value.shape, value.dtype) for value in values),
        in_specs=[ANYSPEC] * len(after) + [VSPEC] * len(values),
        out_specs=[VSPEC] * len(values),
        compiler_params=params(),
        cost_estimate=cost(0, sum(4 * value.size for value in values)),
        name="forward",
    )(*after, *values)


def assemble_kernel(kind, after, place_ref, *refs):
    pieces, outs = list(refs[after : after + 4]), refs[after + 5 :]
    core = place_ref[CORE]
    size = pieces[0].shape[0]
    pieces += [refs[after + 4].at[step * size : (step + 1) * size] for step in range(4)]
    for step, piece in enumerate(pieces):
        mine = step < 4
        quarter = place_ref[MINE if mine else THEIRS] ^ (step % 4)
        side = core if mine else 1 - core
        if kind == "qkv":
            rows = size // 3
            for item in range(3):
                at = pl.ds(aligned((side * 4 + quarter) * rows, 8), rows)
                outs[0][item, at, :] = piece[item * rows : (item + 1) * rows, :].astype(F32)
            continue
        half = outs[0].shape[1] // 2
        part = pl.ds(aligned(side * half, LANES), half)
        begin = 0
        for out_ref in outs:
            rows = out_ref.shape[0] // 4
            at = pl.ds(aligned(quarter * rows, 8), rows)
            out_ref[at, part] = piece[begin : begin + rows, :].astype(F32)
            begin += rows


def assemble(kind, place, pieces, shapes, after=()):
    total = sum(math.prod(shape) for shape in shapes)
    return pl.pallas_call(
        functools.partial(assemble_kernel, kind, len(after)),
        out_shape=tuple(jax.ShapeDtypeStruct(shape, F32) for shape in shapes),
        in_specs=[SSPEC] + [ANYSPEC] * len(after) + [VSPEC] * 5,
        out_specs=[VSPEC] * len(shapes),
        compiler_params=params(),
        cost_estimate=cost(0, 6 * total),
        name="assemble",
    )(place, *after, *pieces)


def per_device(
    axis_sizes,
    hidden,
    seq_ids,
    cotangent,
    qkv_weight,
    attn_out_weight,
    mlp_in_weight,
    mlp_out_weight,
    norm1_gain,
    norm2_gain,
):
    dp_size, tensor_size = axis_sizes
    devices = dp_size * tensor_size
    chips = devices // 4
    chip_bits = chips.bit_length() - 1
    rows, width = hidden.shape
    cols = qkv_weight.shape[2]
    units = mlp_out_weight.shape[0]
    dp_at = lax.axis_index("dp")
    core = dp_at % 2
    chip = dp_at // 2

    def move(value, target):
        return lax.ppermute(value, ("dp", "tensor"), [(i, target(i)) for i in range(devices)])

    def swapped(i):
        return (i & ~3) | ((i & 1) << 1) | ((i >> 1) & 1)

    def to_tensor(i):
        return i ^ 1

    def to_core(i):
        return i ^ 2

    def to_near(i):
        return i ^ 4

    def masked(first, second):
        return lambda i: i ^ (second if i & 2 else first)

    near, next_near = chip % 2, (chip // 2) % 2
    quarters = [near * 2 + next_near, next_near * 2 + near]
    place = jnp.stack(
        [
            core,
            near * 2 + core,
            jnp.where(core == 0, quarters[0], quarters[1]),
            jnp.where(core == 0, quarters[1], quarters[0]),
            jnp.where(core == 0, 0, next_near),
            jnp.where(core == 0, near, 0),
            jnp.where(core == 0, next_near, near),
            jnp.where(core == 0, near, next_near),
            jnp.where(core == 0, next_near, near),
        ]
    ).astype(jnp.int32)

    x = move(hidden, swapped)
    ids = jnp.where(core == lax.axis_index("tensor"), seq_ids, move(seq_ids, to_core))
    ids_own = lax.dynamic_slice_in_dim(ids, core * rows, rows)
    ids_other = lax.dynamic_slice_in_dim(ids, (1 - core) * rows, rows)

    index = jnp.arange(ids.shape[0], dtype=jnp.int32)
    begins = jnp.zeros((rows,), jnp.int32)
    for number in (-1, 0, 1, 2):
        start = jnp.min(jnp.where(ids == number, index, ids.shape[0]))
        begins = jnp.where(ids_own == number, start, begins)
    pos = core * rows + jnp.arange(rows, dtype=jnp.int32) - begins
    frequency = jnp.power(ROPE_BASE, -2.0 * jnp.arange(HDIM // 2, dtype=F32) / HDIM)
    angles = pos.astype(F32)[:, None] * frequency[None, :]
    cosine, sine = jnp.cos(angles), jnp.sin(angles)
    cosine = jnp.concatenate([cosine] * 4, axis=1)
    sine = jnp.concatenate([-sine, sine] * 2, axis=1)
    col_own = jnp.broadcast_to(ids_own[:, None], (rows, LANES))
    col_other = jnp.broadcast_to(ids_other[:, None], (rows, LANES))
    row_own = jnp.broadcast_to(ids_own[None, :], (8, rows))
    row_other = jnp.broadcast_to(ids_other[None, :], (8, rows))

    def gather(one, sent):
        return one, move(sent, to_core), move(sent, to_near)

    w_qkv = qkv_weight.reshape(3 * width, cols)
    w_in = jnp.swapaxes(mlp_in_weight, 1, 2).reshape(2 * units, width)
    w_qkv_part = pack(place, [w_qkv], [x])
    w_qkv_one = move(w_qkv_part, to_tensor)
    w_in_one = move(pack(place, [w_in], [w_qkv_part]), to_tensor)
    w_rest_one = move(pack(place, [mlp_out_weight, attn_out_weight], [w_qkv_part]), to_tensor)
    cot = move(cotangent, swapped)
    gain1, gain2 = norm1_gain[None, :], norm2_gain[None, :]

    q_a, kv_a = project(place, x, gain1, [w_qkv], cosine, sine)
    kv_a_x = move(kv_a, to_core)
    w_qkv_x = gather(w_qkv_one, forward([w_qkv_one], [kv_a])[0])
    w_qkv_x += (move(w_qkv_x[2], to_core),)
    o_a, lse_a = attend(q_a, kv_a, kv_a_x, col_own, row_own, row_other, after=[w_qkv_x[1]])
    w_in_x = gather(w_in_one, forward([w_in_one], [o_a])[0])
    q_b, kv_b = project(place, x, gain1, w_qkv_x, cosine, sine, after=[w_in_x[1]])
    kv_b_x = move(kv_b, to_core)
    w_rest_x = gather(w_rest_one, forward([w_rest_one], [kv_b])[0])
    o_b, lse_b = attend(q_b, kv_b, kv_b_x, col_own, row_own, row_other, after=[w_rest_x[1]])
    last_in, last_rest = forward([w_in_x[2], w_rest_x[2]], [o_b])
    w_in_x += (move(last_in, to_core),)
    w_rest_x += (move(last_rest, to_core),)
    out, grad_mixed, go_a, go_b, in_keep, in_send, gain2_part, grad_low, grad_mixed_low, hid = middle(
        place, x, o_a, o_b, cot, col_own, gain2, attn_out_weight, w_in, mlp_out_weight, w_in_x, w_rest_x
    )
    rest_keep, rest_send = outer(place, o_a, o_b, hid, grad_low, grad_mixed_low)
    out = move(out, swapped)

    plain = range(2, chip_bits)

    def spread(total):
        one = move(total, masked(8, 4))
        two = move(total, masked(4, 8))
        mine = [total, one, two, move(one, masked(4, 8))]
        return mine + [move(join(mine), to_core)]

    def back(q, kv, kv_x, go, o, lse, after):
        gq, dk, dv, dx = attend_back(q, kv, kv_x, go, o, lse, col_own, col_other, row_own, cosine, sine, after)
        return gq, dk, dv, move(dx, to_core)

    def pair(value, mask):
        return [value, move(value, masked(mask, mask))]

    target_1, target_2, target_3 = masked(1, 8), masked(4, 1), masked(8, 4)
    in_got = move(in_send, to_core)
    rest_got = move(rest_send, to_core)
    in_sent, in_kept = merge(place, ([in_keep, in_got], ONE))
    gq_b, dk_b, dv_b, recv_b = back(q_b, kv_b, kv_b_x, go_b, o_b, lse_b, [in_sent])
    in_got = move(in_sent, target_1)
    in_sent, in_kept, rest_sent, rest_kept = merge(
        place, ([in_kept, in_got], TWO), ([rest_keep, rest_got], ONE), after=[gq_b]
    )
    keep_b, send_b, gk_b, gv_b = project_grads(place, x, gain1, gq_b, dk_b, dv_b, recv_b, cosine, sine, [in_sent])
    gq_a, dk_a, dv_a, recv_a = back(q_a, kv_a, kv_a_x, go_a, o_a, lse_a, [keep_b])
    in_got = move(in_sent, target_2)
    rest_got = move(rest_sent, target_1)
    in_sent, in_kept, rest_sent, rest_kept, qkv_sum = merge(
        place,
        ([in_kept, in_got], THREE),
        ([rest_kept, rest_got], TWO),
        ([keep_b, move(send_b, to_core)], None),
        after=[gq_a],
    )
    in_got = move(in_sent, target_3)
    rest_got = move(rest_sent, target_2)
    half = qkv_sum.shape[0] // 2
    low_got = move(qkv_sum[:half], to_tensor)
    high_got = move(qkv_sum[half:], to_tensor)
    keep_a, send_a, input_grad, gain1_part = project_back(
        place, x, gain1, gq_a, dk_a, dv_a, recv_a, cosine, sine, w_qkv, [gq_b, gk_b, gv_b], w_qkv_x, grad_mixed,
        [in_sent, out],
    )
    in_total, rest_sent, rest_kept = merge(
        place, ([in_kept, in_got], None), ([rest_kept, rest_got], THREE), after=[keep_a]
    )
    rest_got = move(rest_sent, target_3)
    input_grad = move(input_grad, swapped)
    gains = jnp.concatenate([gain1_part, gain2_part])
    sent, kept, gains = merge(
        place,
        ([keep_a, move(send_a, to_core), low_got, high_got], FIRST),
        (pair(gains, 2), None),
        after=[in_total],
    )
    for b in plain:
        (in_total,) = merge(place, (pair(in_total, 4 << b), None), after=[sent])
    sent, kept, gains, rest_total = merge(
        place,
        ([kept, move(sent, masked(4, 8))], SECOND),
        (pair(gains, 4), None),
        ([rest_kept, rest_got], None),
    )
    in_pieces = spread(in_total)
    qkv_total, gains = merge(
        place, ([kept, move(sent, masked(8, 4))], None), (pair(gains, 8), None), after=[in_total]
    )
    for b in plain:
        (rest_total,) = merge(place, (pair(rest_total, 4 << b), None), after=[qkv_total])
    rest_pieces = spread(rest_total)
    (g_in,) = assemble("in", place, in_pieces, [(2 * units, width)])
    for b in plain:
        qkv_total, gains = merge(
            place, (pair(qkv_total, 4 << b), None), (pair(gains, 4 << b), None), after=[input_grad, g_in]
        )
    qkv_pieces = spread(qkv_total)
    gains = sum(pair(gains, 1))
    g_down, g_out = assemble("rest", place, rest_pieces, [(units, width), (cols, width)], after=[qkv_total])
    (g_qkv,) = assemble("qkv", place, qkv_pieces, [(3, width, cols)])
    return (
        out,
        input_grad,
        gains[0],
        gains[8],
        g_qkv,
        g_out,
        jnp.swapaxes(g_in.reshape(2, units, width), 1, 2),
        g_down,
    )


def solution(mesh):
    in_specs = (
        P(("dp", "tensor"), None),
        P("dp"),
        P(("dp", "tensor"), None),
        P(None, None, "tensor"),
        P("tensor", None),
        P(None, None, "tensor"),
        P("tensor", None),
        P(),
        P(),
    )
    out_specs = (
        P(("dp", "tensor"), None),
        P(("dp", "tensor"), None),
        P(),
        P(),
        P(None, None, "tensor"),
        P("tensor", None),
        P(None, None, "tensor"),
        P("tensor", None),
    )
    return jax.shard_map(
        functools.partial(per_device, (mesh.shape["dp"], mesh.shape["tensor"])),
        mesh=mesh,
        in_specs=in_specs,
        out_specs=out_specs,
        check_vma=False,
    )
```

```python
import functools
import math

import jax
import jax.numpy as jnp
from jax import lax
from jax.experimental import pallas as pl
from jax.experimental.pallas import tpu as pltpu
from jax.sharding import PartitionSpec as P

HDIM = 64
LANES = 128
EPSILON = 1e-05
ROPE_BASE = 160000.0
MASKED = -1e30
F32 = jnp.float32
BF16 = jnp.bfloat16
MIB = 1024 * 1024


def dot(left, right):
    return jnp.dot(left, right, preferred_element_type=F32)


def dot_t(left, right):
    return lax.dot_general(left, right, (((1,), (1,)), ((), ())), preferred_element_type=F32)


def t_dot(left, right):
    return lax.dot_general(left, right, (((0,), (0,)), ((), ())), preferred_element_type=F32)


def norm_parts(values):
    center = values - jnp.mean(values, axis=-1, keepdims=True)
    spread = jnp.mean(center * center, axis=-1, keepdims=True)
    scale = lax.rsqrt(spread + EPSILON)
    return center * scale, scale


def swap_halves(values):
    lane = lax.broadcasted_iota(jnp.int32, values.shape, 1) % HDIM
    return jnp.where(
        lane < HDIM // 2,
        pltpu.roll(values, LANES - HDIM // 2, 1),
        pltpu.roll(values, HDIM // 2, 1),
    )


def low_lanes(shape):
    return lax.broadcasted_iota(jnp.int32, shape, 1) < HDIM


def cost(covers):
    return pl.CostEstimate(flops=20_000_000_000 if covers else 1_000, bytes_accessed=1_024, transcendentals=0)


def params(mib=20, semantics=None):
    return pltpu.CompilerParams(vmem_limit_bytes=mib * MIB, dimension_semantics=semantics)


VSPEC = pl.BlockSpec(memory_space=pltpu.VMEM)
SSPEC = pl.BlockSpec(memory_space=pltpu.SMEM)
ANYSPEC = pl.BlockSpec(memory_space=pl.ANY)
CORE, PIECE, MINE, THEIRS, ONE, TWO, THREE, FIRST, SECOND = range(9)


def aligned(value, by):
    return pl.multiple_of(value, by)


def side_block(core, side, quarter):
    return jnp.where(core == 0, side * 4 + quarter, (quarter // 2) * 4 + side * 2 + quarter % 2)


def ordered(kernel, count, *refs):
    kernel(*refs[count:])


def quarters_of(place_ref, pieces):
    one, two, others = pieces
    size = one.shape[0]
    for step, piece in ((0, one), (2, two), (1, others.at[0:size]), (3, others.at[size : 2 * size])):
        yield place_ref[PIECE] ^ step, piece


def load_pieces(place_ref, pieces, w_s):
    size = pieces[0].shape[0]
    for at, piece in quarters_of(place_ref, pieces):
        w_s[pl.ds(aligned(at * size, 16), size), :] = piece[...]


def project_kernel(gathered, *refs):
    if gathered:
        place_ref, x_ref, gain_ref, w0, w1, w2, cos_ref, sin_ref, q_ref, k_ref, v_ref, w_ref = refs
        load_pieces(place_ref, (w0, w1, w2), w_ref)
    else:
        place_ref, x_ref, gain_ref, w_ref, cos_ref, sin_ref, q_ref, k_ref, v_ref = refs
    rows, width = x_ref.shape
    cols = q_ref.shape[1]
    tile = min(256, rows)
    for begin in range(0, rows, tile):
        at = pl.ds(begin, tile)
        normed, _ = norm_parts(x_ref[at, :].astype(F32))
        low = (normed * gain_ref[...]).astype(BF16)
        cosine, sine = cos_ref[at, :], sin_ref[at, :]
        q_raw = dot(low, w_ref[0:width, :])
        k_raw = dot(low, w_ref[width : 2 * width, :])
        v_ref[at, :] = dot(low, w_ref[2 * width : 3 * width, :]).astype(BF16)
        for col in range(0, cols, LANES):
            part = slice(col, col + LANES)
            q_part, k_part = q_raw[:, part], k_raw[:, part]
            q_ref[at, part] = (
                (q_part * cosine + swap_halves(q_part) * sine).astype(BF16) * (1.0 / math.sqrt(HDIM))
            ).astype(BF16)
            k_ref[at, part] = (k_part * cosine + swap_halves(k_part) * sine).astype(BF16)


def project(place, x, gain, weights, cosine, sine, after=()):
    rows, width = x.shape
    cols = weights[0].shape[1]
    gathered = len(weights) > 1
    operands = [place, x, gain, *weights, cosine, sine]
    return pl.pallas_call(
        functools.partial(ordered, functools.partial(project_kernel, gathered), len(after)),
        out_shape=(
            jax.ShapeDtypeStruct((rows, cols), BF16),
            jax.ShapeDtypeStruct((rows, cols), BF16),
            jax.ShapeDtypeStruct((rows, cols), BF16),
        ),
        in_specs=[ANYSPEC] * len(after) + [SSPEC] + [VSPEC] * (len(operands) - 1),
        out_specs=[VSPEC] * 3,
        scratch_shapes=[pltpu.VMEM((3 * width, cols), BF16)] if gathered else [],
        compiler_params=params(),
        cost_estimate=cost(gathered),
        name="project",
    )(*after, *operands)


def attend_kernel(q_ref, ko_ref, vo_ref, kx_ref, vx_ref, col_ref, row_ref, rowx_ref, o_ref, lse_ref, bo_ref, bx_ref):
    rows = q_ref.shape[0]
    tile = min(256, rows)

    @pl.when(pl.program_id(0) == 0)
    def _():
        col = col_ref[...][:, 0:1]
        bo_ref[...] = jnp.where(col == row_ref[0:1, :], 0.0, MASKED)
        bx_ref[...] = jnp.where(col == rowx_ref[0:1, :], 0.0, MASKED)

    for begin in range(0, rows, tile):
        at = pl.ds(begin, tile)
        low = low_lanes((tile, LANES))
        q_pair = q_ref[at, :]
        results, logs = [], []
        for head in range(2):
            chosen = low if head == 0 else jnp.logical_not(low)
            query = jnp.where(chosen, q_pair, jnp.zeros_like(q_pair))
            own = dot_t(query, ko_ref[...]) + bo_ref[at, :]
            other = dot_t(query, kx_ref[...]) + bx_ref[at, :]
            highest = jnp.maximum(
                jnp.max(own, axis=-1, keepdims=True), jnp.max(other, axis=-1, keepdims=True)
            )
            own = jnp.exp(own - highest)
            other = jnp.exp(other - highest)
            totals = jnp.sum(own, axis=-1, keepdims=True) + jnp.sum(other, axis=-1, keepdims=True)
            value = dot(own.astype(BF16), vo_ref[...]) + dot(other.astype(BF16), vx_ref[...])
            results.append(value / totals)
            logs.append(highest + jnp.log(totals))
        o_ref[at, :] = jnp.where(low, results[0], results[1]).astype(BF16)
        lse_ref[at, :] = jnp.where(low, logs[0], logs[1])


def attend(q, kv_own, kv_other, col, row, row_other, after=()):
    rows, cols = q.shape
    pairs = cols // LANES
    tok = pl.BlockSpec((rows, LANES), lambda p: (0, p))
    return pl.pallas_call(
        functools.partial(ordered, attend_kernel, len(after)),
        grid=(pairs,),
        out_shape=(
            jax.ShapeDtypeStruct((rows, cols), BF16),
            jax.ShapeDtypeStruct((rows, cols), F32),
        ),
        in_specs=[ANYSPEC] * len(after)
        + [
            tok,
            tok,
            tok,
            tok,
            tok,
            pl.BlockSpec((rows, LANES), lambda p: (0, 0)),
            pl.BlockSpec((8, rows), lambda p: (0, 0)),
            pl.BlockSpec((8, rows), lambda p: (0, 0)),
        ],
        out_specs=[tok, tok],
        scratch_shapes=[pltpu.VMEM((rows, rows), F32), pltpu.VMEM((rows, rows), F32)],
        compiler_params=params(semantics=("arbitrary",)),
        cost_estimate=cost(False),
        name="attend",
    )(*after, q, *kv_own, *kv_other, col, row, row_other)


def attend_back_kernel(
    q_ref, ko_ref, vo_ref, kx_ref, vx_ref, do_ref, o_ref, lse_ref, col_ref, colx_ref, row_ref, cos_ref, sin_ref,
    gq_ref, dko_ref, dvo_ref, dx_ref, bo_ref, bx_ref,
):
    rows = q_ref.shape[0]
    tile = min(256, rows)

    @pl.when(pl.program_id(0) == 0)
    def _():
        row = row_ref[0:1, :]
        bo_ref[...] = jnp.where(col_ref[...][:, 0:1] == row, 0.0, MASKED)
        bx_ref[...] = jnp.where(colx_ref[...][:, 0:1] == row, 0.0, MASKED)

    low = low_lanes((rows, LANES))
    q_pair, do_pair = q_ref[...], do_ref[...]
    product = do_pair.astype(F32) * o_ref[...].astype(F32)
    first = jnp.sum(jnp.where(low, product, 0.0), axis=-1, keepdims=True)
    second = jnp.sum(jnp.where(low, 0.0, product), axis=-1, keepdims=True)
    delta_t = jnp.transpose(jnp.where(low, first, second))
    lse_t = jnp.transpose(lse_ref[...])
    low_tile = low_lanes((tile, LANES))
    grad_q = jnp.zeros((rows, LANES), F32)
    for k_ref, v_ref, bias_ref, dk_ref, dv_ref in (
        (ko_ref, vo_ref, bo_ref, dko_ref, dvo_ref),
        (kx_ref, vx_ref, bx_ref, dx_ref.at[0], dx_ref.at[1]),
    ):
        for begin in range(0, rows, tile):
            at = pl.ds(begin, tile)
            k_pair, v_pair = k_ref[at, :], v_ref[at, :]
            grad_k = grad_v = None
            for head in range(2):
                chosen = low_tile if head == 0 else jnp.logical_not(low_tile)
                chosen_q = low if head == 0 else jnp.logical_not(low)
                key = jnp.where(chosen, k_pair, jnp.zeros_like(k_pair))
                value = jnp.where(chosen, v_pair, jnp.zeros_like(v_pair))
                query = jnp.where(chosen_q, q_pair, jnp.zeros_like(q_pair))
                grad_o = jnp.where(chosen_q, do_pair, jnp.zeros_like(do_pair))
                at_row = head * HDIM
                scores = dot_t(key, q_pair) + bias_ref[at, :]
                probs = jnp.exp(scores - lse_t[at_row : at_row + 1, :])
                grad_probs = dot_t(value, do_pair)
                grad_scores = (probs * (grad_probs - delta_t[at_row : at_row + 1, :])).astype(BF16)
                term_v = dot(probs.astype(BF16), grad_o)
                term_k = dot(grad_scores, query)
                grad_v = term_v if grad_v is None else grad_v + term_v
                grad_k = term_k if grad_k is None else grad_k + term_k
                grad_q = grad_q + t_dot(grad_scores, key)
            dk_ref[at, :] = grad_k.astype(dk_ref.dtype)
            dv_ref[at, :] = grad_v.astype(dv_ref.dtype)
    grad_q = grad_q * (1.0 / math.sqrt(HDIM))
    gq_ref[...] = (grad_q * cos_ref[...] - swap_halves(grad_q) * sin_ref[...]).astype(BF16)


def attend_back(q, kv_own, kv_other, grad_o, o, lse, col, col_other, row, cosine, sine, after=()):
    rows, cols = q.shape
    pairs = cols // LANES
    tok = pl.BlockSpec((rows, LANES), lambda p: (0, p))
    fixed = pl.BlockSpec((rows, LANES), lambda p: (0, 0))
    return pl.pallas_call(
        functools.partial(ordered, attend_back_kernel, len(after)),
        grid=(pairs,),
        out_shape=(
            jax.ShapeDtypeStruct((rows, cols), BF16),
            jax.ShapeDtypeStruct((rows, cols), F32),
            jax.ShapeDtypeStruct((rows, cols), F32),
            jax.ShapeDtypeStruct((2, rows, cols), BF16),
        ),
        in_specs=[ANYSPEC] * len(after)
        + [
            tok, tok, tok, tok, tok, tok, tok, tok, fixed, fixed,
            pl.BlockSpec((8, rows), lambda p: (0, 0)), fixed, fixed,
        ],
        out_specs=[tok] * 3 + [pl.BlockSpec((2, rows, LANES), lambda p: (0, 0, p))],
        scratch_shapes=[pltpu.VMEM((rows, rows), F32), pltpu.VMEM((rows, rows), F32)],
        compiler_params=params(semantics=("arbitrary",)),
        cost_estimate=cost(True),
        name="attend_back",
    )(*after, q, *kv_own, *kv_other, grad_o, o, lse, col, col_other, row, cosine, sine)


def middle_kernel(
    place_ref, x_ref, atto_ref, attx_ref, cot_ref, col_ref, gain_ref, wo_ref, wi_ref, wd_ref,
    p0, p1, p2, p3i, p3r,
    out_ref, gm_ref, gao_ref, gax_ref, ak_ref, as_ref, gain_grad_ref, g_s, gml_s, hid_s,
    wi_s, wd_s, wo_s, b_s, gu_s, gg_s,
):
    rows, width = x_ref.shape
    units, cols = wd_ref.shape[0], wo_ref.shape[0]
    both = 2 * units
    wi_s[0:units, :] = wi_ref[0:units, :]
    wi_s[both : both + units, :] = wi_ref[units:both, :]
    wd_s[0:units, :] = wd_ref[...]
    wo_s[0:cols, :] = wo_ref[...]
    n_i, n_d, n_o = both // 4, units // 4, cols // 4
    cut = [ref.at[0:n_i] for ref in (p0, p1, p2)] + [p3i]
    rest = [ref.at[n_i : n_i + n_d + n_o] for ref in (p0, p1, p2)] + [p3r]
    for step, (piece_i, piece) in zip((0, 2, 1, 3), zip(cut, rest)):
        at = place_ref[PIECE] ^ step
        to_i = units + (at % 2) * n_i + (at // 2) * both
        wi_s[pl.ds(aligned(to_i, 16), n_i), :] = piece_i[...]
        wd_s[pl.ds(aligned(units + at * n_d, 16), n_d), :] = piece[0:n_d, :]
        wo_s[pl.ds(aligned(cols + at * n_o, 16), n_o), :] = piece[n_d : n_d + n_o, :]
    tile = min(256, rows)
    gain = gain_ref[...]
    gain_grad = jnp.zeros((1, width), F32)
    for begin in range(0, rows, tile):
        at = pl.ds(begin, tile)
        mixed = x_ref[at, :].astype(F32) + dot(atto_ref[at, :], wo_s[0:cols, :]) + dot(attx_ref[at, :], wo_s[cols:, :])
        normed, scale = norm_parts(mixed)
        low = (normed * gain).astype(BF16)
        live = col_ref[at, 0:1] >= 0
        cot = cot_ref[at, :]
        grad_low = jnp.where(live, cot, jnp.zeros_like(cot))
        b_s[at, :] = low
        g_s[at, :] = grad_low
        up = dot_t(low, wi_s[0:both, :])
        gate = dot_t(low, wi_s[both:, :])
        cdf = 0.5 * (1.0 + lax.erf(up * (1.0 / math.sqrt(2.0))))
        act = up * cdf
        hid = (act * gate).astype(BF16)
        slope = cdf + up * (jnp.exp(-0.5 * up * up) * (1.0 / math.sqrt(2.0 * math.pi)))
        grad_hid = dot_t(grad_low, wd_s[...])
        grad_up = (grad_hid * gate * slope).astype(BF16)
        grad_gate = (grad_hid * act).astype(BF16)
        out_ref[at, :] = (mixed + dot(hid, wd_s[...])).astype(BF16)
        grad_b = dot(grad_up, wi_s[0:both, :]) + dot(grad_gate, wi_s[both:, :])
        hid_s[at, :] = hid
        gu_s[at, :] = grad_up
        gg_s[at, :] = grad_gate
        gain_grad = gain_grad + jnp.sum(grad_b * normed, axis=0, keepdims=True)
        scaled = grad_b * gain
        grad_mixed = grad_low.astype(F32) + scale * (
            scaled
            - jnp.mean(scaled, axis=-1, keepdims=True)
            - normed * jnp.mean(scaled * normed, axis=-1, keepdims=True)
        )
        gm_ref[at, :] = grad_mixed
        grad_mixed_low = grad_mixed.astype(BF16)
        gml_s[at, :] = grad_mixed_low
        gao_ref[at, :] = dot_t(grad_mixed_low, wo_s[0:cols, :]).astype(BF16)
        gax_ref[at, :] = dot_t(grad_mixed_low, wo_s[cols:, :]).astype(BF16)
    gain_grad_ref[...] = jnp.broadcast_to(gain_grad, gain_grad_ref.shape)
    half = width // 2
    core = place_ref[CORE]
    for a_ref, which in ((as_ref, 1 - core), (ak_ref, core)):
        low = b_s[:, pl.ds(aligned(which * half, LANES), half)]
        for row, src in ((0, gu_s), (units, gg_s)):
            grad = t_dot(src[...], low).astype(BF16)
            for side in range(2):
                for quarter in range(2):
                    at = side_block(which, side, row // n_i + quarter) * n_i
                    begin = side * units + quarter * n_i
                    a_ref[pl.ds(aligned(at, 16), n_i), :] = grad[begin : begin + n_i]


def outer_kernel(place_ref, atto_ref, attx_ref, hid_ref, g_ref, gml_ref, bk_ref, bs_ref):
    half = g_ref.shape[1] // 2
    units, cols = hid_ref.shape[1] // 2, atto_ref.shape[1]
    n_d, n_o = units // 4, cols // 4
    n_b = n_d + n_o
    core = place_ref[CORE]
    for b_ref, which in ((bs_ref, 1 - core), (bk_ref, core)):
        part = pl.ds(aligned(which * half, LANES), half)
        grad = t_dot(hid_ref[...], g_ref[:, part]).astype(BF16)
        grad_mixed_low = gml_ref[:, part]
        for side, att_ref in enumerate((atto_ref, attx_ref)):
            grad_o = t_dot(att_ref[...], grad_mixed_low).astype(BF16)
            for quarter in range(4):
                to = side_block(which, side, quarter) * n_b
                begin = side * units + quarter * n_d
                b_ref[pl.ds(aligned(to, 16), n_d), :] = grad[begin : begin + n_d]
                b_ref[pl.ds(aligned(to + n_d, 16), n_o), :] = grad_o[quarter * n_o : (quarter + 1) * n_o]


def outer(place, att_own, att_other, hid, g, gml):
    rows, width = g.shape
    size = hid.shape[1] + 2 * att_own.shape[1]
    return pl.pallas_call(
        outer_kernel,
        out_shape=(jax.ShapeDtypeStruct((size, width // 2), BF16),) * 2,
        in_specs=[SSPEC] + [VSPEC] * 5,
        out_specs=[VSPEC] * 2,
        compiler_params=params(),
        cost_estimate=cost(True),
        name="outer",
    )(place, att_own, att_other, hid, g, gml)


def middle(place, x, att_own, att_other, cot, col, gain, wo, wi, wd, pieces):
    rows, width = x.shape
    units, cols = wd.shape[0], wo.shape[0]
    size = 2 * cols * width + 6 * units * width
    half = width // 2
    return pl.pallas_call(
        middle_kernel,
        out_shape=(
            jax.ShapeDtypeStruct((rows, width), BF16),
            jax.ShapeDtypeStruct((rows, width), F32),
            jax.ShapeDtypeStruct((rows, cols), BF16),
            jax.ShapeDtypeStruct((rows, cols), BF16),
            jax.ShapeDtypeStruct((4 * units, half), BF16),
            jax.ShapeDtypeStruct((4 * units, half), BF16),
            jax.ShapeDtypeStruct((8, width), F32),
            jax.ShapeDtypeStruct((rows, width), BF16),
            jax.ShapeDtypeStruct((rows, width), BF16),
            jax.ShapeDtypeStruct((rows, 2 * units), BF16),
        ),
        in_specs=[SSPEC] + [VSPEC] * 14,
        out_specs=[VSPEC] * 10,
        scratch_shapes=[
            pltpu.VMEM((4 * units, width), BF16),
            pltpu.VMEM((2 * units, width), BF16),
            pltpu.VMEM((2 * cols, width), BF16),
            pltpu.VMEM((rows, width), BF16),
            pltpu.VMEM((rows, 2 * units), BF16),
            pltpu.VMEM((rows, 2 * units), BF16),
        ],
        compiler_params=params(34),
        cost_estimate=cost(True),
        name="middle",
    )(place, x, att_own, att_other, cot, col, gain, wo, wi, wd, *pieces)


def qkv_grads(place_ref, x_ref, gain_ref, gq_ref, dk_ref, dv_ref, recv_ref, cos_ref, sin_ref,
              keep_ref, send_ref, gk_ref, gv_ref, low_s):
    rows, width = x_ref.shape
    cols = gq_ref.shape[1]
    tile = min(256, rows)
    for begin in range(0, rows, tile):
        at = pl.ds(begin, tile)
        normed, _ = norm_parts(x_ref[at, :].astype(F32))
        low_s[at, :] = (normed * gain_ref[...]).astype(BF16)
        cosine, sine = cos_ref[at, :], sin_ref[at, :]
        for col in range(0, cols, LANES):
            part = slice(col, col + LANES)
            grad_k = dk_ref[at, part] + recv_ref[0, at, part].astype(F32)
            gk_ref[at, part] = (grad_k * cosine - swap_halves(grad_k) * sine).astype(BF16)
        gv_ref[at, :] = (dv_ref[at, :] + recv_ref[1, at, :].astype(F32)).astype(BF16)
    half = width // 2
    size = half // 4
    core = place_ref[CORE]
    for to_ref, which in ((send_ref, 1 - core), (keep_ref, core)):
        low = low_s[:, pl.ds(aligned(which * half, LANES), half)]
        for item, src in enumerate((gq_ref, gk_ref, gv_ref)):
            grad = t_dot(low, src[...]).astype(BF16)
            for quarter in range(4):
                to = (quarter * 3 + item) * size
                to_ref[to : to + size, :] = grad[quarter * size : (quarter + 1) * size]


def project_grads(place, x, gain, gq, dk, dv, received, cosine, sine, after=()):
    rows, width = x.shape
    cols = gq.shape[1]
    operands = [x, gain, gq, dk, dv, received, cosine, sine]
    return pl.pallas_call(
        functools.partial(ordered, qkv_grads, len(after)),
        out_shape=(jax.ShapeDtypeStruct((3 * width // 2, cols), BF16),) * 2
        + (jax.ShapeDtypeStruct((rows, cols), BF16),) * 2,
        in_specs=[ANYSPEC] * len(after) + [SSPEC] + [VSPEC] * len(operands),
        out_specs=[VSPEC] * 4,
        scratch_shapes=[pltpu.VMEM((rows, width), BF16)],
        compiler_params=params(24),
        cost_estimate=cost(True),
        name="project_grads",
    )(*after, place, *operands)


def project_back_kernel(
    place_ref, x_ref, gain_ref, gq_ref, dk_ref, dv_ref, recv_ref, cos_ref, sin_ref, w_ref,
    gqx_ref, gkx_ref, gvx_ref, w0, w1, w2, gm_ref,
    keep_ref, send_ref, gx_ref, gain_grad_ref, low_s, gk_s, gv_s, wx_s,
):
    qkv_grads(place_ref, x_ref, gain_ref, gq_ref, dk_ref, dv_ref, recv_ref, cos_ref, sin_ref,
              keep_ref, send_ref, gk_s, gv_s, low_s)
    load_pieces(place_ref, (w0, w1, w2), wx_s)
    rows, width = x_ref.shape
    tile = min(256, rows)
    gain = gain_ref[...]
    gain_grad = jnp.zeros((1, width), F32)
    for begin in range(0, rows, tile):
        at = pl.ds(begin, tile)
        normed, scale = norm_parts(x_ref[at, :].astype(F32))
        total = jnp.zeros((tile, width), F32)
        for item, (own, other) in enumerate(((gq_ref, gqx_ref), (gk_s, gkx_ref), (gv_s, gvx_ref))):
            part = slice(item * width, (item + 1) * width)
            total = total + dot_t(own[at, :], w_ref[part, :]) + dot_t(other[at, :], wx_s[part, :])
        gain_grad = gain_grad + jnp.sum(total * normed, axis=0, keepdims=True)
        scaled = total * gain
        gx_ref[at, :] = (
            gm_ref[at, :]
            + scale
            * (
                scaled
                - jnp.mean(scaled, axis=-1, keepdims=True)
                - normed * jnp.mean(scaled * normed, axis=-1, keepdims=True)
            )
        ).astype(BF16)
    gain_grad_ref[...] = jnp.broadcast_to(gain_grad, gain_grad_ref.shape)


def project_back(place, x, gain, gq, dk, dv, received, cosine, sine, weight, others, pieces, grad_mixed, after):
    rows, width = x.shape
    cols = gq.shape[1]
    operands = [x, gain, gq, dk, dv, received, cosine, sine, weight, *others, *pieces, grad_mixed]
    return pl.pallas_call(
        functools.partial(ordered, project_back_kernel, len(after)),
        out_shape=(
            jax.ShapeDtypeStruct((3 * width // 2, cols), BF16),
            jax.ShapeDtypeStruct((3 * width // 2, cols), BF16),
            jax.ShapeDtypeStruct((rows, width), BF16),
            jax.ShapeDtypeStruct((8, width), F32),
        ),
        in_specs=[ANYSPEC] * len(after) + [SSPEC] + [VSPEC] * len(operands),
        out_specs=[VSPEC] * 4,
        scratch_shapes=[
            pltpu.VMEM((rows, width), BF16),
            pltpu.VMEM((rows, cols), BF16),
            pltpu.VMEM((rows, cols), BF16),
            pltpu.VMEM((3 * width, cols), BF16),
        ],
        compiler_params=params(32),
        cost_estimate=cost(True),
        name="project_back",
    )(*after, place, *operands)


def pack(place, weights, after=()):
    sizes = [value.shape[0] // 4 for value in weights]
    width = weights[0].shape[1]

    def kernel(place_ref, *refs):
        begin = 0
        for ref, size in zip(refs[len(after) :], sizes):
            refs[-1][begin : begin + size, :] = ref[...]
            begin += size

    return pl.pallas_call(
        kernel,
        grid_spec=pltpu.PrefetchScalarGridSpec(
            num_scalar_prefetch=1,
            grid=(1,),
            in_specs=[ANYSPEC] * len(after)
            + [pl.BlockSpec((size, width), lambda _, at: (at[PIECE], 0)) for size in sizes],
            out_specs=pl.BlockSpec((sum(sizes), width), lambda _, at: (0, 0)),
        ),
        out_shape=jax.ShapeDtypeStruct((sum(sizes), width), BF16),
        compiler_params=params(semantics=("arbitrary",)),
        cost_estimate=cost(False),
        name="pack",
    )(place, *after, *weights)


def merge_kernel(jobs, after, place_ref, *refs):
    ins = list(refs[after : after + sum(job["count"] for job in jobs)])
    outs = list(refs[after + len(ins) :])
    for job in jobs:
        mine, ins = ins[: job["count"]], ins[job["count"] :]
        which = job["which"]
        if which is None:
            out_ref, outs = outs[0], outs[1:]
            out_ref[...] = sum(ref[...].astype(F32) for ref in mine).astype(out_ref.dtype)
            continue
        size = outs[0].shape[0]
        bit = place_ref[which]
        for out_ref, half in ((outs[0], 1 - bit), (outs[1], bit)):
            at = pl.ds(aligned(half * size, 16), size)
            total = sum(ref[at, :].astype(F32) for ref in (mine[:-2] if which == FIRST else mine))
            if which == FIRST:
                total = total + jnp.where(half == 0, mine[-2][...], mine[-1][...]).astype(F32)
            out_ref[...] = total.astype(BF16)
        outs = outs[2:]


def merge(place, *jobs, after=(), covers=True):
    arrays, shapes, notes = [], [], []
    for values, which in jobs:
        rows, cols = values[0].shape
        parts = 1 if which is None else 2
        shapes += [jax.ShapeDtypeStruct((rows // parts, cols), values[0].dtype)] * parts
        notes.append({"count": len(values), "which": which})
        arrays += values
    out = pl.pallas_call(
        functools.partial(merge_kernel, notes, len(after)),
        out_shape=tuple(shapes),
        in_specs=[SSPEC] + [ANYSPEC] * len(after) + [VSPEC] * len(arrays),
        out_specs=[VSPEC] * len(shapes),
        compiler_params=params(),
        cost_estimate=cost(covers),
        name="merge",
    )(place, *after, *arrays)
    return out


def join_kernel(counts, after, *refs):
    ins, outs = list(refs[after : after + sum(counts)]), refs[after + sum(counts) :]
    for count, out_ref in zip(counts, outs):
        size = ins[0].shape[0]
        for step in range(count):
            out_ref[step * size : (step + 1) * size, :] = ins[step][...]
        ins = ins[count:]


def join(*groups, after=(), covers=True):
    values = [value for group in groups for value in group]
    return pl.pallas_call(
        functools.partial(join_kernel, [len(group) for group in groups], len(after)),
        out_shape=tuple(
            jax.ShapeDtypeStruct((len(group) * group[0].shape[0], group[0].shape[1]), BF16) for group in groups
        ),
        in_specs=[ANYSPEC] * len(after) + [VSPEC] * len(values),
        out_specs=[VSPEC] * len(groups),
        compiler_params=params(),
        cost_estimate=cost(covers),
        name="join",
    )(*after, *values)


def assemble_kernel(kind, after, place_ref, *refs):
    pieces, outs = list(refs[after : after + 4]), refs[after + 5 :]
    core = place_ref[CORE]
    size = pieces[0].shape[0]
    pieces += [refs[after + 4].at[step * size : (step + 1) * size] for step in range(4)]
    for step, piece in enumerate(pieces):
        mine = step < 4
        quarter = place_ref[MINE if mine else THEIRS] ^ (step % 4)
        side = core if mine else 1 - core
        if kind == "qkv":
            rows = size // 3
            for item in range(3):
                at = pl.ds(aligned((side * 4 + quarter) * rows, 8), rows)
                outs[0][item, at, :] = piece[item * rows : (item + 1) * rows, :].astype(F32)
            continue
        half = outs[0].shape[1] // 2
        part = pl.ds(aligned(side * half, LANES), half)
        begin = 0
        for out_ref in outs:
            rows = out_ref.shape[0] // 4
            at = pl.ds(aligned(quarter * rows, 8), rows)
            out_ref[at, part] = piece[begin : begin + rows, :].astype(F32)
            begin += rows


def assemble(kind, place, pieces, shapes, after=()):
    total = sum(math.prod(shape) for shape in shapes)
    return pl.pallas_call(
        functools.partial(assemble_kernel, kind, len(after)),
        out_shape=tuple(jax.ShapeDtypeStruct(shape, F32) for shape in shapes),
        in_specs=[SSPEC] + [ANYSPEC] * len(after) + [VSPEC] * 5,
        out_specs=[VSPEC] * len(shapes),
        compiler_params=params(),
        cost_estimate=cost(True),
        name="assemble",
    )(place, *after, *pieces)


def per_device(
    axis_sizes,
    hidden,
    seq_ids,
    cotangent,
    qkv_weight,
    attn_out_weight,
    mlp_in_weight,
    mlp_out_weight,
    norm1_gain,
    norm2_gain,
):
    dp_size, tensor_size = axis_sizes
    devices = dp_size * tensor_size
    chips = devices // 4
    chip_bits = chips.bit_length() - 1
    rows, width = hidden.shape
    cols = qkv_weight.shape[2]
    units = mlp_out_weight.shape[0]
    dp_at = lax.axis_index("dp")
    core = dp_at % 2
    chip = dp_at // 2

    def move(value, target):
        return lax.ppermute(value, ("dp", "tensor"), [(i, target(i)) for i in range(devices)])

    def swapped(i):
        return (i & ~3) | ((i & 1) << 1) | ((i >> 1) & 1)

    def to_tensor(i):
        return i ^ 1

    def to_core(i):
        return i ^ 2

    def to_near(i):
        return i ^ 4

    def masked(first, second):
        return lambda i: i ^ (second if i & 2 else first)

    near, next_near = chip % 2, (chip // 2) % 2
    quarters = [near * 2 + next_near, next_near * 2 + near]
    place = jnp.stack(
        [
            core,
            near * 2 + core,
            jnp.where(core == 0, quarters[0], quarters[1]),
            jnp.where(core == 0, quarters[1], quarters[0]),
            jnp.where(core == 0, 0, next_near),
            jnp.where(core == 0, near, 0),
            jnp.where(core == 0, next_near, near),
            jnp.where(core == 0, near, next_near),
            jnp.where(core == 0, next_near, near),
        ]
    ).astype(jnp.int32)

    x = move(hidden, swapped)
    ids = jnp.where(core == lax.axis_index("tensor"), seq_ids, move(seq_ids, to_core))
    ids_own = lax.dynamic_slice_in_dim(ids, core * rows, rows)
    ids_other = lax.dynamic_slice_in_dim(ids, (1 - core) * rows, rows)

    index = jnp.arange(ids.shape[0], dtype=jnp.int32)
    begins = jnp.zeros((rows,), jnp.int32)
    for number in (-1, 0, 1, 2):
        start = jnp.min(jnp.where(ids == number, index, ids.shape[0]))
        begins = jnp.where(ids_own == number, start, begins)
    pos = core * rows + jnp.arange(rows, dtype=jnp.int32) - begins
    frequency = jnp.power(ROPE_BASE, -2.0 * jnp.arange(HDIM // 2, dtype=F32) / HDIM)
    angles = pos.astype(F32)[:, None] * frequency[None, :]
    cosine, sine = jnp.cos(angles), jnp.sin(angles)
    cosine = jnp.concatenate([cosine] * 4, axis=1)
    sine = jnp.concatenate([-sine, sine] * 2, axis=1)
    col_own = jnp.broadcast_to(ids_own[:, None], (rows, LANES))
    col_other = jnp.broadcast_to(ids_other[:, None], (rows, LANES))
    row_own = jnp.broadcast_to(ids_own[None, :], (8, rows))
    row_other = jnp.broadcast_to(ids_other[None, :], (8, rows))

    w_qkv = qkv_weight.reshape(3 * width, cols)
    w_in = jnp.swapaxes(mlp_in_weight, 1, 2).reshape(2 * units, width)
    w_qkv_part = pack(place, [w_qkv])
    w_part = pack(place, [w_in, mlp_out_weight, attn_out_weight], [w_qkv_part])
    w_qkv_one = move(w_qkv_part, to_tensor)
    w_one = move(w_part, to_tensor)
    cot = move(cotangent, swapped)
    gain1, gain2 = norm1_gain[None, :], norm2_gain[None, :]

    (sent,) = join([w_qkv_one], after=[w_part], covers=False)
    w_qkv_two = move(sent, to_near)
    q_a, *kv_a = project(place, x, gain1, [w_qkv], cosine, sine, after=[sent])
    kv_a_x = [move(value, to_core) for value in kv_a]
    o_a, lse_a = attend(q_a, kv_a, kv_a_x, col_own, row_own, row_other)
    sent, both = join([w_one], [w_qkv_one, w_qkv_two], after=[o_a], covers=False)
    w_two = move(sent, to_near)
    w_qkv_x = [w_qkv_one, w_qkv_two, move(both, to_core)]
    q_b, *kv_b = project(place, x, gain1, w_qkv_x, cosine, sine, after=[sent])
    kv_b_x = [move(value, to_core) for value in kv_b]
    o_b, lse_b = attend(q_b, kv_b, kv_b_x, col_own, row_own, row_other)
    (sent,) = join([w_two], after=[o_b], covers=False)
    in_rows = w_in.shape[0] // 4
    w_x = [w_one, w_two, move(w_one, to_core), move(sent[:in_rows], to_core), move(sent[in_rows:], to_core)]
    out, grad_mixed, go_a, go_b, in_keep, in_send, gain2_part, grad_low, grad_mixed_low, hid = middle(
        place, x, o_a, o_b, cot, col_own, gain2, attn_out_weight, w_in, mlp_out_weight, w_x
    )
    rest_keep, rest_send = outer(place, o_a, o_b, hid, grad_low, grad_mixed_low)
    out = move(out, swapped)

    plain = range(2, chip_bits)

    def spread(total):
        one = move(total, masked(8, 4))
        two = move(total, masked(4, 8))
        mine = [total, one, two, move(one, masked(4, 8))]
        return mine + [move(join(mine)[0], to_core)]

    def back(q, kv, kv_x, go, o, lse, after):
        gq, dk, dv, dx = attend_back(q, kv, kv_x, go, o, lse, col_own, col_other, row_own, cosine, sine, after)
        return gq, dk, dv, move(dx, to_core)

    def pair(value, mask):
        return [value, move(value, masked(mask, mask))]

    target_1, target_2, target_3 = masked(1, 8), masked(4, 1), masked(8, 4)
    in_got = move(in_send, to_core)
    rest_got = move(rest_send, to_core)
    in_sent, in_kept = merge(place, ([in_keep, in_got], ONE))
    gq_b, dk_b, dv_b, recv_b = back(q_b, kv_b, kv_b_x, go_b, o_b, lse_b, [in_sent])
    in_got = move(in_sent, target_1)
    in_sent, in_kept, rest_sent, rest_kept = merge(
        place, ([in_kept, in_got], TWO), ([rest_keep, rest_got], ONE), after=[gq_b]
    )
    keep_b, send_b, gk_b, gv_b = project_grads(place, x, gain1, gq_b, dk_b, dv_b, recv_b, cosine, sine, [in_sent])
    (qkv_sum,) = merge(place, ([keep_b, move(send_b, to_core)], None), covers=False)
    half = qkv_sum.shape[0] // 2
    low_got = move(qkv_sum[:half], to_tensor)
    gq_a, dk_a, dv_a, recv_a = back(q_a, kv_a, kv_a_x, go_a, o_a, lse_a, [qkv_sum])
    in_got = move(in_sent, target_2)
    rest_got = move(rest_sent, target_1)
    in_sent, in_kept, rest_sent, rest_kept = merge(
        place, ([in_kept, in_got], THREE), ([rest_kept, rest_got], TWO), after=[gq_a, low_got]
    )
    in_got = move(in_sent, target_3)
    rest_got = move(rest_sent, target_2)
    high_got = move(qkv_sum[half:], to_tensor)
    keep_a, send_a, input_grad, gain1_part = project_back(
        place, x, gain1, gq_a, dk_a, dv_a, recv_a, cosine, sine, w_qkv, [gq_b, gk_b, gv_b], w_qkv_x, grad_mixed,
        [in_sent, out],
    )
    in_total, rest_sent, rest_kept = merge(
        place, ([in_kept, in_got], None), ([rest_kept, rest_got], THREE), after=[keep_a, high_got]
    )
    rest_got = move(rest_sent, target_3)
    input_grad = move(input_grad, swapped)
    gains = jnp.concatenate([gain1_part, gain2_part])
    sent, kept, gains = merge(
        place,
        ([keep_a, move(send_a, to_core), low_got, high_got], FIRST),
        (pair(gains, 2), None),
        after=[in_total],
    )
    for b in plain:
        (in_total,) = merge(place, (pair(in_total, 4 << b), None), after=[sent])
    sent, kept, gains, rest_total = merge(
        place,
        ([kept, move(sent, masked(4, 8))], SECOND),
        (pair(gains, 4), None),
        ([rest_kept, rest_got], None),
    )
    in_pieces = spread(in_total)
    qkv_total, gains = merge(
        place, ([kept, move(sent, masked(8, 4))], None), (pair(gains, 8), None), after=[in_total]
    )
    for b in plain:
        (rest_total,) = merge(place, (pair(rest_total, 4 << b), None), after=[qkv_total])
    rest_pieces = spread(rest_total)
    (g_in,) = assemble("in", place, in_pieces, [(2 * units, width)])
    for b in plain:
        qkv_total, gains = merge(
            place, (pair(qkv_total, 4 << b), None), (pair(gains, 4 << b), None), after=[input_grad, g_in]
        )
    qkv_pieces = spread(qkv_total)
    gains = sum(pair(gains, 1))
    g_down, g_out = assemble("rest", place, rest_pieces, [(units, width), (cols, width)], after=[qkv_total])
    (g_qkv,) = assemble("qkv", place, qkv_pieces, [(3, width, cols)])
    return (
        out,
        input_grad,
        gains[0],
        gains[8],
        g_qkv,
        g_out,
        jnp.swapaxes(g_in.reshape(2, units, width), 1, 2),
        g_down,
    )


def solution(mesh):
    in_specs = (
        P(("dp", "tensor"), None),
        P("dp"),
        P(("dp", "tensor"), None),
        P(None, None, "tensor"),
        P("tensor", None),
        P(None, None, "tensor"),
        P("tensor", None),
        P(),
        P(),
    )
    out_specs = (
        P(("dp", "tensor"), None),
        P(("dp", "tensor"), None),
        P(),
        P(),
        P(None, None, "tensor"),
        P("tensor", None),
        P(None, None, "tensor"),
        P("tensor", None),
    )
    return jax.shard_map(
        functools.partial(per_device, (mesh.shape["dp"], mesh.shape["tensor"])),
        mesh=mesh,
        in_specs=in_specs,
        out_specs=out_specs,
        check_vma=False,
    )
```

```python
import functools
import math

import jax
import jax.numpy as jnp
from jax import lax
from jax.experimental import pallas as pl
from jax.experimental.pallas import tpu as pltpu
from jax.sharding import PartitionSpec as P

HDIM = 64
LANES = 128
EPSILON = 1e-05
ROPE_BASE = 160000.0
MASKED = -1e30
F32 = jnp.float32
BF16 = jnp.bfloat16
MIB = 1024 * 1024


def dot(left, right):
    return jnp.dot(left, right, preferred_element_type=F32)


def dot_t(left, right):
    return lax.dot_general(left, right, (((1,), (1,)), ((), ())), preferred_element_type=F32)


def t_dot(left, right):
    return lax.dot_general(left, right, (((0,), (0,)), ((), ())), preferred_element_type=F32)


def norm_parts(values):
    center = values - jnp.mean(values, axis=-1, keepdims=True)
    spread = jnp.mean(center * center, axis=-1, keepdims=True)
    scale = lax.rsqrt(spread + EPSILON)
    return center * scale, scale


def swap_halves(values):
    lane = lax.broadcasted_iota(jnp.int32, values.shape, 1) % HDIM
    return jnp.where(
        lane < HDIM // 2,
        pltpu.roll(values, LANES - HDIM // 2, 1),
        pltpu.roll(values, HDIM // 2, 1),
    )


def low_lanes(shape):
    return lax.broadcasted_iota(jnp.int32, shape, 1) < HDIM


def cost(covers):
    return pl.CostEstimate(flops=20_000_000_000 if covers else 1_000, bytes_accessed=1_024, transcendentals=0)


def params(mib=20, semantics=None):
    return pltpu.CompilerParams(vmem_limit_bytes=mib * MIB, dimension_semantics=semantics)


VSPEC = pl.BlockSpec(memory_space=pltpu.VMEM)
SSPEC = pl.BlockSpec(memory_space=pltpu.SMEM)
ANYSPEC = pl.BlockSpec(memory_space=pl.ANY)
CORE, PIECE, PIECE_NEXT, MINE, THEIRS, ONE, TWO, THREE, FIRST, SECOND = range(10)


def aligned(value, by):
    return pl.multiple_of(value, by)


def side_block(core, side, quarter):
    return jnp.where(core == 0, side * 4 + quarter, (quarter // 2) * 4 + side * 2 + quarter % 2)


def ordered(kernel, count, *refs):
    kernel(*refs[count:])


def quarters_of(place_ref, pieces):
    one, two, others = pieces
    size = one.shape[0]
    for step, piece in ((0, one), (2, two), (1, others.at[0:size]), (3, others.at[size : 2 * size])):
        yield place_ref[PIECE] ^ step, piece


def load_pieces(place_ref, pieces, w_s):
    size = pieces[0].shape[0]
    for at, piece in quarters_of(place_ref, pieces):
        w_s[pl.ds(aligned(at * size, 16), size), :] = piece[...]


def project_kernel(gathered, *refs):
    if gathered:
        place_ref, x_ref, gain_ref, w0, w1, w2, cos_ref, sin_ref, q_ref, k_ref, v_ref, w_ref = refs
        load_pieces(place_ref, (w0, w1, w2), w_ref)
    else:
        place_ref, x_ref, gain_ref, w_ref, cos_ref, sin_ref, q_ref, k_ref, v_ref = refs
    rows, width = x_ref.shape
    cols = q_ref.shape[1]
    tile = min(256, rows)
    for begin in range(0, rows, tile):
        at = pl.ds(begin, tile)
        normed, _ = norm_parts(x_ref[at, :].astype(F32))
        low = (normed * gain_ref[...]).astype(BF16)
        cosine, sine = cos_ref[at, :], sin_ref[at, :]
        q_raw = dot(low, w_ref[0:width, :])
        k_raw = dot(low, w_ref[width : 2 * width, :])
        v_ref[at, :] = dot(low, w_ref[2 * width : 3 * width, :]).astype(BF16)
        for col in range(0, cols, LANES):
            part = slice(col, col + LANES)
            q_part, k_part = q_raw[:, part], k_raw[:, part]
            q_ref[at, part] = (
                (q_part * cosine + swap_halves(q_part) * sine).astype(BF16) * (1.0 / math.sqrt(HDIM))
            ).astype(BF16)
            k_ref[at, part] = (k_part * cosine + swap_halves(k_part) * sine).astype(BF16)


def project(place, x, gain, weights, cosine, sine, after=()):
    rows, width = x.shape
    cols = weights[0].shape[1]
    gathered = len(weights) > 1
    operands = [place, x, gain, *weights, cosine, sine]
    return pl.pallas_call(
        functools.partial(ordered, functools.partial(project_kernel, gathered), len(after)),
        out_shape=(
            jax.ShapeDtypeStruct((rows, cols), BF16),
            jax.ShapeDtypeStruct((rows, cols), BF16),
            jax.ShapeDtypeStruct((rows, cols), BF16),
        ),
        in_specs=[ANYSPEC] * len(after) + [SSPEC] + [VSPEC] * (len(operands) - 1),
        out_specs=[VSPEC] * 3,
        scratch_shapes=[pltpu.VMEM((3 * width, cols), BF16)] if gathered else [],
        compiler_params=params(),
        cost_estimate=cost(gathered),
        name="project",
    )(*after, *operands)


def attend_kernel(q_ref, ko_ref, vo_ref, kx_ref, vx_ref, col_ref, row_ref, rowx_ref, o_ref, lse_ref, bo_ref, bx_ref):
    rows = q_ref.shape[0]
    tile = min(256, rows)

    @pl.when(pl.program_id(0) == 0)
    def _():
        col = col_ref[...][:, 0:1]
        bo_ref[...] = jnp.where(col == row_ref[0:1, :], 0.0, MASKED)
        bx_ref[...] = jnp.where(col == rowx_ref[0:1, :], 0.0, MASKED)

    for begin in range(0, rows, tile):
        at = pl.ds(begin, tile)
        low = low_lanes((tile, LANES))
        q_pair = q_ref[at, :]
        results, logs = [], []
        for head in range(2):
            chosen = low if head == 0 else jnp.logical_not(low)
            query = jnp.where(chosen, q_pair, jnp.zeros_like(q_pair))
            own = dot_t(query, ko_ref[...]) + bo_ref[at, :]
            other = dot_t(query, kx_ref[...]) + bx_ref[at, :]
            highest = jnp.maximum(
                jnp.max(own, axis=-1, keepdims=True), jnp.max(other, axis=-1, keepdims=True)
            )
            own = jnp.exp(own - highest)
            other = jnp.exp(other - highest)
            totals = jnp.sum(own, axis=-1, keepdims=True) + jnp.sum(other, axis=-1, keepdims=True)
            value = dot(own.astype(BF16), vo_ref[...]) + dot(other.astype(BF16), vx_ref[...])
            results.append(value / totals)
            logs.append(highest + jnp.log(totals))
        o_ref[at, :] = jnp.where(low, results[0], results[1]).astype(BF16)
        lse_ref[at, :] = jnp.where(low, logs[0], logs[1])


def attend(q, kv_own, kv_other, col, row, row_other, after=()):
    rows, cols = q.shape
    pairs = cols // LANES
    tok = pl.BlockSpec((rows, LANES), lambda p: (0, p))
    return pl.pallas_call(
        functools.partial(ordered, attend_kernel, len(after)),
        grid=(pairs,),
        out_shape=(
            jax.ShapeDtypeStruct((rows, cols), BF16),
            jax.ShapeDtypeStruct((rows, cols), F32),
        ),
        in_specs=[ANYSPEC] * len(after)
        + [
            tok,
            tok,
            tok,
            tok,
            tok,
            pl.BlockSpec((rows, LANES), lambda p: (0, 0)),
            pl.BlockSpec((8, rows), lambda p: (0, 0)),
            pl.BlockSpec((8, rows), lambda p: (0, 0)),
        ],
        out_specs=[tok, tok],
        scratch_shapes=[pltpu.VMEM((rows, rows), F32), pltpu.VMEM((rows, rows), F32)],
        compiler_params=params(semantics=("arbitrary",)),
        cost_estimate=cost(False),
        name="attend",
    )(*after, q, *kv_own, *kv_other, col, row, row_other)


def attend_back_kernel(
    q_ref, ko_ref, vo_ref, kx_ref, vx_ref, do_ref, o_ref, lse_ref, col_ref, colx_ref, row_ref, cos_ref, sin_ref,
    gq_ref, dko_ref, dvo_ref, dx_ref, bo_ref, bx_ref,
):
    rows = q_ref.shape[0]
    tile = min(256, rows)

    @pl.when(pl.program_id(0) == 0)
    def _():
        row = row_ref[0:1, :]
        bo_ref[...] = jnp.where(col_ref[...][:, 0:1] == row, 0.0, MASKED)
        bx_ref[...] = jnp.where(colx_ref[...][:, 0:1] == row, 0.0, MASKED)

    low = low_lanes((rows, LANES))
    q_pair, do_pair = q_ref[...], do_ref[...]
    product = do_pair.astype(F32) * o_ref[...].astype(F32)
    first = jnp.sum(jnp.where(low, product, 0.0), axis=-1, keepdims=True)
    second = jnp.sum(jnp.where(low, 0.0, product), axis=-1, keepdims=True)
    delta_t = jnp.transpose(jnp.where(low, first, second))
    lse_t = jnp.transpose(lse_ref[...])
    low_tile = low_lanes((tile, LANES))
    grad_q = jnp.zeros((rows, LANES), F32)
    for k_ref, v_ref, bias_ref, dk_ref, dv_ref in (
        (ko_ref, vo_ref, bo_ref, dko_ref, dvo_ref),
        (kx_ref, vx_ref, bx_ref, dx_ref.at[0], dx_ref.at[1]),
    ):
        for begin in range(0, rows, tile):
            at = pl.ds(begin, tile)
            k_pair, v_pair = k_ref[at, :], v_ref[at, :]
            grad_k = grad_v = None
            for head in range(2):
                chosen = low_tile if head == 0 else jnp.logical_not(low_tile)
                chosen_q = low if head == 0 else jnp.logical_not(low)
                key = jnp.where(chosen, k_pair, jnp.zeros_like(k_pair))
                value = jnp.where(chosen, v_pair, jnp.zeros_like(v_pair))
                query = jnp.where(chosen_q, q_pair, jnp.zeros_like(q_pair))
                grad_o = jnp.where(chosen_q, do_pair, jnp.zeros_like(do_pair))
                at_row = head * HDIM
                scores = dot_t(key, q_pair) + bias_ref[at, :]
                probs = jnp.exp(scores - lse_t[at_row : at_row + 1, :])
                grad_probs = dot_t(value, do_pair)
                grad_scores = (probs * (grad_probs - delta_t[at_row : at_row + 1, :])).astype(BF16)
                term_v = dot(probs.astype(BF16), grad_o)
                term_k = dot(grad_scores, query)
                grad_v = term_v if grad_v is None else grad_v + term_v
                grad_k = term_k if grad_k is None else grad_k + term_k
                grad_q = grad_q + t_dot(grad_scores, key)
            dk_ref[at, :] = grad_k.astype(dk_ref.dtype)
            dv_ref[at, :] = grad_v.astype(dv_ref.dtype)
    grad_q = grad_q * (1.0 / math.sqrt(HDIM))
    gq_ref[...] = (grad_q * cos_ref[...] - swap_halves(grad_q) * sin_ref[...]).astype(BF16)


def attend_back(q, kv_own, kv_other, grad_o, o, lse, col, col_other, row, cosine, sine, after=()):
    rows, cols = q.shape
    pairs = cols // LANES
    tok = pl.BlockSpec((rows, LANES), lambda p: (0, p))
    fixed = pl.BlockSpec((rows, LANES), lambda p: (0, 0))
    return pl.pallas_call(
        functools.partial(ordered, attend_back_kernel, len(after)),
        grid=(pairs,),
        out_shape=(
            jax.ShapeDtypeStruct((rows, cols), BF16),
            jax.ShapeDtypeStruct((rows, cols), F32),
            jax.ShapeDtypeStruct((rows, cols), F32),
            jax.ShapeDtypeStruct((2, rows, cols), BF16),
        ),
        in_specs=[ANYSPEC] * len(after)
        + [
            tok, tok, tok, tok, tok, tok, tok, tok, fixed, fixed,
            pl.BlockSpec((8, rows), lambda p: (0, 0)), fixed, fixed,
        ],
        out_specs=[tok] * 3 + [pl.BlockSpec((2, rows, LANES), lambda p: (0, 0, p))],
        scratch_shapes=[pltpu.VMEM((rows, rows), F32), pltpu.VMEM((rows, rows), F32)],
        compiler_params=params(semantics=("arbitrary",)),
        cost_estimate=cost(True),
        name="attend_back",
    )(*after, q, *kv_own, *kv_other, grad_o, o, lse, col, col_other, row, cosine, sine)


def middle_kernel(
    place_ref, x_ref, atto_ref, attx_ref, cot_ref, col_ref, gain_ref, wo_ref, wi_ref, wd_ref,
    p0, p1i, p1r, p2, p3i, p3r,
    out_ref, gm_ref, gao_ref, gax_ref, ak_ref, as_ref, gain_grad_ref, g_s, gml_s, hid_s,
    wi_s, wd_s, wo_s, b_s, gu_s, gg_s,
):
    rows, width = x_ref.shape
    units, cols = wd_ref.shape[0], wo_ref.shape[0]
    both = 2 * units
    wi_s[0:units, :] = wi_ref[0:units, :]
    wi_s[both : both + units, :] = wi_ref[units:both, :]
    wd_s[0:units, :] = wd_ref[...]
    wo_s[0:cols, :] = wo_ref[...]
    n_i, n_d, n_o = both // 4, units // 4, cols // 4
    n_r = n_d + n_o
    cut = (p0.at[0:n_i], p1i, p2.at[0:n_i], p3i)
    rest = (p0.at[n_i : n_i + n_r], p1r, p2.at[n_i : n_i + n_r], p3r)
    for step, piece_i, piece in zip((0, 2, 1, 3), cut, rest):
        at = place_ref[PIECE] ^ step
        to_i = units + (at % 2) * n_i + (at // 2) * both
        wi_s[pl.ds(aligned(to_i, 16), n_i), :] = piece_i[...]
        at = place_ref[PIECE_NEXT] ^ step
        wd_s[pl.ds(aligned(units + at * n_d, 16), n_d), :] = piece[0:n_d, :]
        wo_s[pl.ds(aligned(cols + at * n_o, 16), n_o), :] = piece[n_d:, :]
    tile = min(256, rows)
    gain = gain_ref[...]
    gain_grad = jnp.zeros((1, width), F32)
    for begin in range(0, rows, tile):
        at = pl.ds(begin, tile)
        mixed = x_ref[at, :].astype(F32) + dot(atto_ref[at, :], wo_s[0:cols, :]) + dot(attx_ref[at, :], wo_s[cols:, :])
        normed, scale = norm_parts(mixed)
        low = (normed * gain).astype(BF16)
        live = col_ref[at, 0:1] >= 0
        cot = cot_ref[at, :]
        grad_low = jnp.where(live, cot, jnp.zeros_like(cot))
        b_s[at, :] = low
        g_s[at, :] = grad_low
        up = dot_t(low, wi_s[0:both, :])
        gate = dot_t(low, wi_s[both:, :])
        cdf = 0.5 * (1.0 + lax.erf(up * (1.0 / math.sqrt(2.0))))
        act = up * cdf
        hid = (act * gate).astype(BF16)
        slope = cdf + up * (jnp.exp(-0.5 * up * up) * (1.0 / math.sqrt(2.0 * math.pi)))
        grad_hid = dot_t(grad_low, wd_s[...])
        grad_up = (grad_hid * gate * slope).astype(BF16)
        grad_gate = (grad_hid * act).astype(BF16)
        out_ref[at, :] = (mixed + dot(hid, wd_s[...])).astype(BF16)
        grad_b = dot(grad_up, wi_s[0:both, :]) + dot(grad_gate, wi_s[both:, :])
        hid_s[at, :] = hid
        gu_s[at, :] = grad_up
        gg_s[at, :] = grad_gate
        gain_grad = gain_grad + jnp.sum(grad_b * normed, axis=0, keepdims=True)
        scaled = grad_b * gain
        grad_mixed = grad_low.astype(F32) + scale * (
            scaled
            - jnp.mean(scaled, axis=-1, keepdims=True)
            - normed * jnp.mean(scaled * normed, axis=-1, keepdims=True)
        )
        gm_ref[at, :] = grad_mixed
        grad_mixed_low = grad_mixed.astype(BF16)
        gml_s[at, :] = grad_mixed_low
        gao_ref[at, :] = dot_t(grad_mixed_low, wo_s[0:cols, :]).astype(BF16)
        gax_ref[at, :] = dot_t(grad_mixed_low, wo_s[cols:, :]).astype(BF16)
    gain_grad_ref[...] = jnp.broadcast_to(gain_grad, gain_grad_ref.shape)
    half = width // 2
    core = place_ref[CORE]
    for a_ref, which in ((as_ref, 1 - core), (ak_ref, core)):
        low = b_s[:, pl.ds(aligned(which * half, LANES), half)]
        for row, src in ((0, gu_s), (units, gg_s)):
            grad = t_dot(src[...], low).astype(BF16)
            for side in range(2):
                for quarter in range(2):
                    at = side_block(which, side, row // n_i + quarter) * n_i
                    begin = side * units + quarter * n_i
                    a_ref[pl.ds(aligned(at, 16), n_i), :] = grad[begin : begin + n_i]


def outer_kernel(place_ref, atto_ref, attx_ref, hid_ref, g_ref, gml_ref, bk_ref, bs_ref):
    half = g_ref.shape[1] // 2
    units, cols = hid_ref.shape[1] // 2, atto_ref.shape[1]
    n_d, n_o = units // 4, cols // 4
    n_b = n_d + n_o
    core = place_ref[CORE]
    for b_ref, which in ((bs_ref, 1 - core), (bk_ref, core)):
        part = pl.ds(aligned(which * half, LANES), half)
        grad = t_dot(hid_ref[...], g_ref[:, part]).astype(BF16)
        grad_mixed_low = gml_ref[:, part]
        for side, att_ref in enumerate((atto_ref, attx_ref)):
            grad_o = t_dot(att_ref[...], grad_mixed_low).astype(BF16)
            for quarter in range(4):
                to = side_block(which, side, quarter) * n_b
                begin = side * units + quarter * n_d
                b_ref[pl.ds(aligned(to, 16), n_d), :] = grad[begin : begin + n_d]
                b_ref[pl.ds(aligned(to + n_d, 16), n_o), :] = grad_o[quarter * n_o : (quarter + 1) * n_o]


def outer(place, att_own, att_other, hid, g, gml):
    rows, width = g.shape
    size = hid.shape[1] + 2 * att_own.shape[1]
    return pl.pallas_call(
        outer_kernel,
        out_shape=(jax.ShapeDtypeStruct((size, width // 2), BF16),) * 2,
        in_specs=[SSPEC] + [VSPEC] * 5,
        out_specs=[VSPEC] * 2,
        compiler_params=params(),
        cost_estimate=cost(True),
        name="outer",
    )(place, att_own, att_other, hid, g, gml)


def middle(place, x, att_own, att_other, cot, col, gain, wo, wi, wd, pieces):
    rows, width = x.shape
    units, cols = wd.shape[0], wo.shape[0]
    size = 2 * cols * width + 6 * units * width
    half = width // 2
    return pl.pallas_call(
        middle_kernel,
        out_shape=(
            jax.ShapeDtypeStruct((rows, width), BF16),
            jax.ShapeDtypeStruct((rows, width), F32),
            jax.ShapeDtypeStruct((rows, cols), BF16),
            jax.ShapeDtypeStruct((rows, cols), BF16),
            jax.ShapeDtypeStruct((4 * units, half), BF16),
            jax.ShapeDtypeStruct((4 * units, half), BF16),
            jax.ShapeDtypeStruct((8, width), F32),
            jax.ShapeDtypeStruct((rows, width), BF16),
            jax.ShapeDtypeStruct((rows, width), BF16),
            jax.ShapeDtypeStruct((rows, 2 * units), BF16),
        ),
        in_specs=[SSPEC] + [VSPEC] * 15,
        out_specs=[VSPEC] * 10,
        scratch_shapes=[
            pltpu.VMEM((4 * units, width), BF16),
            pltpu.VMEM((2 * units, width), BF16),
            pltpu.VMEM((2 * cols, width), BF16),
            pltpu.VMEM((rows, width), BF16),
            pltpu.VMEM((rows, 2 * units), BF16),
            pltpu.VMEM((rows, 2 * units), BF16),
        ],
        compiler_params=params(34),
        cost_estimate=cost(True),
        name="middle",
    )(place, x, att_own, att_other, cot, col, gain, wo, wi, wd, *pieces)


def qkv_grads(place_ref, x_ref, gain_ref, gq_ref, dk_ref, dv_ref, recv_ref, cos_ref, sin_ref,
              keep_ref, send_ref, gk_ref, gv_ref, low_s):
    rows, width = x_ref.shape
    cols = gq_ref.shape[1]
    tile = min(256, rows)
    for begin in range(0, rows, tile):
        at = pl.ds(begin, tile)
        normed, _ = norm_parts(x_ref[at, :].astype(F32))
        low_s[at, :] = (normed * gain_ref[...]).astype(BF16)
        cosine, sine = cos_ref[at, :], sin_ref[at, :]
        for col in range(0, cols, LANES):
            part = slice(col, col + LANES)
            grad_k = dk_ref[at, part] + recv_ref[0, at, part].astype(F32)
            gk_ref[at, part] = (grad_k * cosine - swap_halves(grad_k) * sine).astype(BF16)
        gv_ref[at, :] = (dv_ref[at, :] + recv_ref[1, at, :].astype(F32)).astype(BF16)
    half = width // 2
    size = half // 4
    core = place_ref[CORE]
    for to_ref, which in ((send_ref, 1 - core), (keep_ref, core)):
        low = low_s[:, pl.ds(aligned(which * half, LANES), half)]
        for item, src in enumerate((gq_ref, gk_ref, gv_ref)):
            grad = t_dot(low, src[...]).astype(BF16)
            for quarter in range(4):
                to = (quarter * 3 + item) * size
                to_ref[to : to + size, :] = grad[quarter * size : (quarter + 1) * size]


def project_grads(place, x, gain, gq, dk, dv, received, cosine, sine, after=()):
    rows, width = x.shape
    cols = gq.shape[1]
    operands = [x, gain, gq, dk, dv, received, cosine, sine]
    return pl.pallas_call(
        functools.partial(ordered, qkv_grads, len(after)),
        out_shape=(jax.ShapeDtypeStruct((3 * width // 2, cols), BF16),) * 2
        + (jax.ShapeDtypeStruct((rows, cols), BF16),) * 2,
        in_specs=[ANYSPEC] * len(after) + [SSPEC] + [VSPEC] * len(operands),
        out_specs=[VSPEC] * 4,
        scratch_shapes=[pltpu.VMEM((rows, width), BF16)],
        compiler_params=params(24),
        cost_estimate=cost(True),
        name="project_grads",
    )(*after, place, *operands)


def project_back_kernel(
    place_ref, x_ref, gain_ref, gq_ref, dk_ref, dv_ref, recv_ref, cos_ref, sin_ref, w_ref,
    gqx_ref, gkx_ref, gvx_ref, w0, w1, w2, gm_ref,
    keep_ref, send_ref, gx_ref, gain_grad_ref, low_s, gk_s, gv_s, wx_s,
):
    qkv_grads(place_ref, x_ref, gain_ref, gq_ref, dk_ref, dv_ref, recv_ref, cos_ref, sin_ref,
              keep_ref, send_ref, gk_s, gv_s, low_s)
    load_pieces(place_ref, (w0, w1, w2), wx_s)
    rows, width = x_ref.shape
    tile = min(256, rows)
    gain = gain_ref[...]
    gain_grad = jnp.zeros((1, width), F32)
    for begin in range(0, rows, tile):
        at = pl.ds(begin, tile)
        normed, scale = norm_parts(x_ref[at, :].astype(F32))
        total = jnp.zeros((tile, width), F32)
        for item, (own, other) in enumerate(((gq_ref, gqx_ref), (gk_s, gkx_ref), (gv_s, gvx_ref))):
            part = slice(item * width, (item + 1) * width)
            total = total + dot_t(own[at, :], w_ref[part, :]) + dot_t(other[at, :], wx_s[part, :])
        gain_grad = gain_grad + jnp.sum(total * normed, axis=0, keepdims=True)
        scaled = total * gain
        gx_ref[at, :] = (
            gm_ref[at, :]
            + scale
            * (
                scaled
                - jnp.mean(scaled, axis=-1, keepdims=True)
                - normed * jnp.mean(scaled * normed, axis=-1, keepdims=True)
            )
        ).astype(BF16)
    gain_grad_ref[...] = jnp.broadcast_to(gain_grad, gain_grad_ref.shape)


def project_back(place, x, gain, gq, dk, dv, received, cosine, sine, weight, others, pieces, grad_mixed, after):
    rows, width = x.shape
    cols = gq.shape[1]
    operands = [x, gain, gq, dk, dv, received, cosine, sine, weight, *others, *pieces, grad_mixed]
    return pl.pallas_call(
        functools.partial(ordered, project_back_kernel, len(after)),
        out_shape=(
            jax.ShapeDtypeStruct((3 * width // 2, cols), BF16),
            jax.ShapeDtypeStruct((3 * width // 2, cols), BF16),
            jax.ShapeDtypeStruct((rows, width), BF16),
            jax.ShapeDtypeStruct((8, width), F32),
        ),
        in_specs=[ANYSPEC] * len(after) + [SSPEC] + [VSPEC] * len(operands),
        out_specs=[VSPEC] * 4,
        scratch_shapes=[
            pltpu.VMEM((rows, width), BF16),
            pltpu.VMEM((rows, cols), BF16),
            pltpu.VMEM((rows, cols), BF16),
            pltpu.VMEM((3 * width, cols), BF16),
        ],
        compiler_params=params(32),
        cost_estimate=cost(True),
        name="project_back",
    )(*after, place, *operands)


def pack(place, weights, after=(), entries=None):
    sizes = [value.shape[0] // 4 for value in weights]
    width = weights[0].shape[1]
    entries = entries or [PIECE] * len(weights)

    def spec(size, entry):
        return pl.BlockSpec((size, width), lambda _, at: (at[entry], 0))

    def kernel(place_ref, *refs):
        begin = 0
        for ref, size in zip(refs[len(after) :], sizes):
            refs[-1][begin : begin + size, :] = ref[...]
            begin += size

    return pl.pallas_call(
        kernel,
        grid_spec=pltpu.PrefetchScalarGridSpec(
            num_scalar_prefetch=1,
            grid=(1,),
            in_specs=[ANYSPEC] * len(after)
            + [spec(size, entry) for size, entry in zip(sizes, entries)],
            out_specs=pl.BlockSpec((sum(sizes), width), lambda _, at: (0, 0)),
        ),
        out_shape=jax.ShapeDtypeStruct((sum(sizes), width), BF16),
        compiler_params=params(semantics=("arbitrary",)),
        cost_estimate=cost(False),
        name="pack",
    )(place, *after, *weights)


def merge_kernel(jobs, after, place_ref, *refs):
    ins = list(refs[after : after + sum(job["count"] for job in jobs)])
    outs = list(refs[after + len(ins) :])
    for job in jobs:
        mine, ins = ins[: job["count"]], ins[job["count"] :]
        which = job["which"]
        if which is None:
            out_ref, outs = outs[0], outs[1:]
            out_ref[...] = sum(ref[...].astype(F32) for ref in mine).astype(out_ref.dtype)
            continue
        size = outs[0].shape[0]
        bit = place_ref[which]
        for out_ref, half in ((outs[0], 1 - bit), (outs[1], bit)):
            at = pl.ds(aligned(half * size, 16), size)
            total = sum(ref[at, :].astype(F32) for ref in (mine[:-2] if which == FIRST else mine))
            if which == FIRST:
                total = total + jnp.where(half == 0, mine[-2][...], mine[-1][...]).astype(F32)
            out_ref[...] = total.astype(BF16)
        outs = outs[2:]


def merge(place, *jobs, after=(), covers=True):
    arrays, shapes, notes = [], [], []
    for values, which in jobs:
        rows, cols = values[0].shape
        parts = 1 if which is None else 2
        shapes += [jax.ShapeDtypeStruct((rows // parts, cols), values[0].dtype)] * parts
        notes.append({"count": len(values), "which": which})
        arrays += values
    out = pl.pallas_call(
        functools.partial(merge_kernel, notes, len(after)),
        out_shape=tuple(shapes),
        in_specs=[SSPEC] + [ANYSPEC] * len(after) + [VSPEC] * len(arrays),
        out_specs=[VSPEC] * len(shapes),
        compiler_params=params(),
        cost_estimate=cost(covers),
        name="merge",
    )(place, *after, *arrays)
    return out


def join_kernel(counts, after, *refs):
    ins, outs = list(refs[after : after + sum(counts)]), refs[after + sum(counts) :]
    for count, out_ref in zip(counts, outs):
        size = out_ref.shape[0] // count
        for step in range(count):
            out_ref[step * size : (step + 1) * size, :] = ins[step][...]
        ins = ins[count:]


def join(*groups, after=(), covers=True):
    values = [value for group in groups for value in group]
    return pl.pallas_call(
        functools.partial(join_kernel, [len(group) for group in groups], len(after)),
        out_shape=tuple(
            jax.ShapeDtypeStruct((len(group) * group[0].shape[0], group[0].shape[1]), BF16) for group in groups
        ),
        in_specs=[ANYSPEC] * len(after) + [VSPEC] * len(values),
        out_specs=[VSPEC] * len(groups),
        compiler_params=params(),
        cost_estimate=cost(covers),
        name="join",
    )(*after, *values)


def assemble_kernel(kind, after, place_ref, *refs):
    pieces, outs = list(refs[after : after + 4]), refs[after + 5 : -1]
    refs[-1][...] = jnp.zeros(refs[-1].shape, F32)
    core = place_ref[CORE]
    size = pieces[0].shape[0]
    pieces += [refs[after + 4].at[step * size : (step + 1) * size] for step in range(4)]
    for step, piece in enumerate(pieces):
        mine = step < 4
        quarter = place_ref[MINE if mine else THEIRS] ^ (step % 4)
        side = core if mine else 1 - core
        if kind == "qkv":
            rows = size // 3
            for item in range(3):
                at = pl.ds(aligned((side * 4 + quarter) * rows, 8), rows)
                outs[0][item, at, :] = piece[item * rows : (item + 1) * rows, :].astype(F32)
            continue
        half = outs[0].shape[1] // 2
        part = pl.ds(aligned(side * half, LANES), half)
        begin = 0
        for out_ref in outs:
            rows = out_ref.shape[0] // 4
            at = pl.ds(aligned(quarter * rows, 8), rows)
            out_ref[at, part] = piece[begin : begin + rows, :].astype(F32)
            begin += rows


def assemble(kind, place, pieces, shapes, after=()):
    total = sum(math.prod(shape) for shape in shapes)
    return pl.pallas_call(
        functools.partial(assemble_kernel, kind, len(after)),
        out_shape=tuple(jax.ShapeDtypeStruct(shape, F32) for shape in [*shapes, (8, LANES)]),
        in_specs=[SSPEC] + [ANYSPEC] * len(after) + [VSPEC] * 5,
        out_specs=[VSPEC] * (len(shapes) + 1),
        compiler_params=params(),
        cost_estimate=cost(True),
        name="assemble",
    )(place, *after, *pieces)


def per_device(
    axis_sizes,
    hidden,
    seq_ids,
    cotangent,
    qkv_weight,
    attn_out_weight,
    mlp_in_weight,
    mlp_out_weight,
    norm1_gain,
    norm2_gain,
):
    dp_size, tensor_size = axis_sizes
    devices = dp_size * tensor_size
    chips = devices // 4
    chip_bits = chips.bit_length() - 1
    rows, width = hidden.shape
    cols = qkv_weight.shape[2]
    units = mlp_out_weight.shape[0]
    dp_at = lax.axis_index("dp")
    core = dp_at % 2
    chip = dp_at // 2

    def move(value, target):
        return lax.ppermute(value, ("dp", "tensor"), [(i, target(i)) for i in range(devices)])

    def swapped(i):
        return (i & ~3) | ((i & 1) << 1) | ((i >> 1) & 1)

    def to_tensor(i):
        return i ^ 1

    def to_core(i):
        return i ^ 2

    def to_near(i):
        return i ^ 4

    def to_next(i):
        return i ^ 8

    def masked(first, second):
        return lambda i: i ^ (second if i & 2 else first)

    near, next_near = chip % 2, (chip // 2) % 2
    quarters = [near * 2 + next_near, next_near * 2 + near]
    place = jnp.stack(
        [
            core,
            near * 2 + core,
            next_near * 2 + core,
            jnp.where(core == 0, quarters[0], quarters[1]),
            jnp.where(core == 0, quarters[1], quarters[0]),
            jnp.where(core == 0, 0, next_near),
            jnp.where(core == 0, near, 0),
            jnp.where(core == 0, next_near, near),
            jnp.where(core == 0, near, next_near),
            jnp.where(core == 0, next_near, near),
        ]
    ).astype(jnp.int32)

    x = move(hidden, swapped)
    ids = jnp.where(core == lax.axis_index("tensor"), seq_ids, move(seq_ids, to_core))
    ids_own = lax.dynamic_slice_in_dim(ids, core * rows, rows)
    ids_other = lax.dynamic_slice_in_dim(ids, (1 - core) * rows, rows)

    index = jnp.arange(ids.shape[0], dtype=jnp.int32)
    begins = jnp.zeros((rows,), jnp.int32)
    for number in (-1, 0, 1, 2):
        start = jnp.min(jnp.where(ids == number, index, ids.shape[0]))
        begins = jnp.where(ids_own == number, start, begins)
    pos = core * rows + jnp.arange(rows, dtype=jnp.int32) - begins
    frequency = jnp.power(ROPE_BASE, -2.0 * jnp.arange(HDIM // 2, dtype=F32) / HDIM)
    angles = pos.astype(F32)[:, None] * frequency[None, :]
    cosine, sine = jnp.cos(angles), jnp.sin(angles)
    cosine = jnp.concatenate([cosine] * 4, axis=1)
    sine = jnp.concatenate([-sine, sine] * 2, axis=1)
    col_own = jnp.broadcast_to(ids_own[:, None], (rows, LANES))
    col_other = jnp.broadcast_to(ids_other[:, None], (rows, LANES))
    row_own = jnp.broadcast_to(ids_own[None, :], (8, rows))
    row_other = jnp.broadcast_to(ids_other[None, :], (8, rows))

    w_qkv = qkv_weight.reshape(3 * width, cols)
    w_in = jnp.swapaxes(mlp_in_weight, 1, 2).reshape(2 * units, width)
    w_qkv_part = pack(place, [w_qkv])
    w_part = pack(
        place, [w_in, mlp_out_weight, attn_out_weight], [w_qkv_part], entries=[PIECE, PIECE_NEXT, PIECE_NEXT]
    )
    w_qkv_one = move(w_qkv_part, to_tensor)
    w_one = move(w_part, to_tensor)
    cot = move(cotangent, swapped)
    gain1, gain2 = norm1_gain[None, :], norm2_gain[None, :]

    (sent,) = join([w_qkv_one], after=[w_part], covers=False)
    w_qkv_two = move(sent, to_near)
    q_a, *kv_a = project(place, x, gain1, [w_qkv], cosine, sine, after=[sent])
    kv_a_x = [move(value, to_core) for value in kv_a]
    o_a, lse_a = attend(q_a, kv_a, kv_a_x, col_own, row_own, row_other)
    sent, both = join([w_one], [w_qkv_one, w_qkv_two], after=[o_a], covers=False)
    in_rows = w_in.shape[0] // 4
    w_in_two, w_rest_two = move(sent[:in_rows], to_near), move(sent[in_rows:], to_next)
    w_qkv_x = [w_qkv_one, w_qkv_two, move(both, to_core)]
    q_b, *kv_b = project(place, x, gain1, w_qkv_x, cosine, sine, after=[sent])
    kv_b_x = [move(value, to_core) for value in kv_b]
    o_b, lse_b = attend(q_b, kv_b, kv_b_x, col_own, row_own, row_other)
    in_sent, rest_sent = join([w_in_two], [w_rest_two], after=[o_b], covers=False)
    w_x = [w_one, w_in_two, w_rest_two] + [move(value, to_core) for value in (w_one, in_sent, rest_sent)]
    out, grad_mixed, go_a, go_b, in_keep, in_send, gain2_part, grad_low, grad_mixed_low, hid = middle(
        place, x, o_a, o_b, cot, col_own, gain2, attn_out_weight, w_in, mlp_out_weight, w_x
    )
    rest_keep, rest_send = outer(place, o_a, o_b, hid, grad_low, grad_mixed_low)

    plain = range(2, chip_bits)

    def spread(total, after=()):
        one = move(total, masked(8, 4))
        two = move(total, masked(4, 8))
        mine = [total, one, two, move(one, masked(4, 8))]
        return mine + [move(join(mine, after=after)[0], to_core)]

    def back(q, kv, kv_x, go, o, lse, after):
        gq, dk, dv, dx = attend_back(q, kv, kv_x, go, o, lse, col_own, col_other, row_own, cosine, sine, after)
        return gq, dk, dv, move(dx, to_core)

    def pair(value, mask):
        return [value, move(value, masked(mask, mask))]

    target_1, target_2, target_3 = masked(1, 8), masked(4, 1), masked(8, 4)
    in_got = move(in_send, to_core)
    rest_got = move(rest_send, to_core)
    in_sent, in_kept = merge(place, ([in_keep, in_got], ONE))
    gq_b, dk_b, dv_b, recv_b = back(q_b, kv_b, kv_b_x, go_b, o_b, lse_b, [in_sent])
    in_got = move(in_sent, target_1)
    in_sent, in_kept, rest_sent, rest_kept = merge(
        place, ([in_kept, in_got], TWO), ([rest_keep, rest_got], ONE), after=[gq_b]
    )
    keep_b, send_b, gk_b, gv_b = project_grads(place, x, gain1, gq_b, dk_b, dv_b, recv_b, cosine, sine, [in_sent])
    (qkv_sum,) = merge(place, ([keep_b, move(send_b, to_core)], None), covers=False)
    half = qkv_sum.shape[0] // 2
    low_got = move(qkv_sum[:half], to_tensor)
    gq_a, dk_a, dv_a, recv_a = back(q_a, kv_a, kv_a_x, go_a, o_a, lse_a, [qkv_sum])
    in_got = move(in_sent, target_2)
    rest_got = move(rest_sent, target_1)
    in_sent, in_kept, rest_sent, rest_kept = merge(
        place, ([in_kept, in_got], THREE), ([rest_kept, rest_got], TWO), after=[gq_a, low_got]
    )
    in_got = move(in_sent, target_3)
    rest_got = move(rest_sent, target_2)
    high_got = move(qkv_sum[half:], to_tensor)
    keep_a, send_a, input_grad, gain1_part = project_back(
        place, x, gain1, gq_a, dk_a, dv_a, recv_a, cosine, sine, w_qkv, [gq_b, gk_b, gv_b], w_qkv_x, grad_mixed,
        [in_sent],
    )
    in_total, rest_sent, rest_kept = merge(
        place, ([in_kept, in_got], None), ([rest_kept, rest_got], THREE), after=[keep_a, high_got]
    )
    rest_got = move(rest_sent, target_3)
    out, input_grad = move(out, swapped), move(input_grad, swapped)
    gains = jnp.concatenate([gain1_part, gain2_part])
    sent, kept, gains = merge(
        place,
        ([keep_a, move(send_a, to_core), low_got, high_got], FIRST),
        (pair(gains, 2), None),
        after=[in_total],
    )
    sent, kept, gains, rest_total = merge(
        place,
        ([kept, move(sent, masked(4, 8))], SECOND),
        (pair(gains, 4), None),
        ([rest_kept, rest_got], None),
    )
    for b in plain:
        (in_total,) = merge(place, (pair(in_total, 4 << b), None), after=[sent])
    in_pieces = spread(in_total)
    qkv_total, gains = merge(
        place, ([kept, move(sent, masked(8, 4))], None), (pair(gains, 8), None), after=[in_total]
    )
    for b in plain:
        (rest_total,) = merge(place, (pair(rest_total, 4 << b), None), after=[qkv_total])
    rest_pieces = spread(rest_total)
    g_in, in_done = assemble("in", place, in_pieces, [(2 * units, width)])
    out, input_grad = join([out], [input_grad], covers=False)
    for b in plain:
        qkv_total, gains = merge(
            place, (pair(qkv_total, 4 << b), None), (pair(gains, 4 << b), None), after=[input_grad, in_pieces[3]]
        )
    qkv_pieces = spread(qkv_total, [in_done])
    gains = sum(pair(gains, 1))
    g_down, g_out, _ = assemble("rest", place, rest_pieces, [(units, width), (cols, width)], after=[qkv_total])
    g_qkv, _ = assemble("qkv", place, qkv_pieces, [(3, width, cols)])
    return (
        out,
        input_grad,
        gains[0],
        gains[8],
        g_qkv,
        g_out,
        jnp.swapaxes(g_in.reshape(2, units, width), 1, 2),
        g_down,
    )


def solution(mesh):
    in_specs = (
        P(("dp", "tensor"), None),
        P("dp"),
        P(("dp", "tensor"), None),
        P(None, None, "tensor"),
        P("tensor", None),
        P(None, None, "tensor"),
        P("tensor", None),
        P(),
        P(),
    )
    out_specs = (
        P(("dp", "tensor"), None),
        P(("dp", "tensor"), None),
        P(),
        P(),
        P(None, None, "tensor"),
        P("tensor", None),
        P(None, None, "tensor"),
        P("tensor", None),
    )
    return jax.shard_map(
        functools.partial(per_device, (mesh.shape["dp"], mesh.shape["tensor"])),
        mesh=mesh,
        in_specs=in_specs,
        out_specs=out_specs,
        check_vma=False,
    )
```

```python
import functools
import math

import jax
import jax.numpy as jnp
from jax import lax
from jax.experimental import pallas as pl
from jax.experimental.pallas import tpu as pltpu
from jax.sharding import PartitionSpec as P

HDIM = 64
LANES = 128
EPSILON = 1e-05
ROPE_BASE = 160000.0
MASKED = -1e30
F32 = jnp.float32
BF16 = jnp.bfloat16
MIB = 1024 * 1024


def dot(left, right):
    return jnp.dot(left, right, preferred_element_type=F32)


def dot_t(left, right):
    return lax.dot_general(left, right, (((1,), (1,)), ((), ())), preferred_element_type=F32)


def t_dot(left, right):
    return lax.dot_general(left, right, (((0,), (0,)), ((), ())), preferred_element_type=F32)


def norm_parts(values):
    center = values - jnp.mean(values, axis=-1, keepdims=True)
    spread = jnp.mean(center * center, axis=-1, keepdims=True)
    scale = lax.rsqrt(spread + EPSILON)
    return center * scale, scale


def swap_halves(values):
    lane = lax.broadcasted_iota(jnp.int32, values.shape, 1) % HDIM
    return jnp.where(
        lane < HDIM // 2,
        pltpu.roll(values, LANES - HDIM // 2, 1),
        pltpu.roll(values, HDIM // 2, 1),
    )


def low_lanes(shape):
    return lax.broadcasted_iota(jnp.int32, shape, 1) < HDIM


def cost(covers):
    return pl.CostEstimate(flops=20_000_000_000 if covers else 1_000, bytes_accessed=1_024, transcendentals=0)


def params(mib=20, semantics=None):
    return pltpu.CompilerParams(vmem_limit_bytes=mib * MIB, dimension_semantics=semantics)


VSPEC = pl.BlockSpec(memory_space=pltpu.VMEM)
SSPEC = pl.BlockSpec(memory_space=pltpu.SMEM)
ANYSPEC = pl.BlockSpec(memory_space=pl.ANY)
CORE, PIECE, PIECE_NEXT, MINE, THEIRS, ONE, TWO, THREE, FIRST, SECOND = range(10)


def aligned(value, by):
    return pl.multiple_of(value, by)


def side_block(core, side, quarter):
    return jnp.where(core == 0, side * 4 + quarter, (quarter // 2) * 4 + side * 2 + quarter % 2)


def ordered(kernel, count, *refs):
    kernel(*refs[count:])


def quarters_of(place_ref, pieces):
    one, two, others = pieces
    size = one.shape[0]
    for step, piece in ((0, one), (2, two), (1, others.at[0:size]), (3, others.at[size : 2 * size])):
        yield place_ref[PIECE] ^ step, piece


def load_pieces(place_ref, pieces, w_s):
    size = pieces[0].shape[0]
    for at, piece in quarters_of(place_ref, pieces):
        w_s[pl.ds(aligned(at * size, 16), size), :] = piece[...]


def project_kernel(gathered, *refs):
    if gathered:
        place_ref, x_ref, gain_ref, w0, w1, w2, cos_ref, sin_ref, q_ref, k_ref, v_ref, w_ref = refs
        load_pieces(place_ref, (w0, w1, w2), w_ref)
    else:
        place_ref, x_ref, gain_ref, w_ref, cos_ref, sin_ref, q_ref, k_ref, v_ref = refs
    rows, width = x_ref.shape
    cols = q_ref.shape[1]
    tile = min(256, rows)
    for begin in range(0, rows, tile):
        at = pl.ds(begin, tile)
        normed, _ = norm_parts(x_ref[at, :].astype(F32))
        low = (normed * gain_ref[...]).astype(BF16)
        cosine, sine = cos_ref[at, :], sin_ref[at, :]
        q_raw = dot(low, w_ref[0:width, :])
        k_raw = dot(low, w_ref[width : 2 * width, :])
        v_ref[at, :] = dot(low, w_ref[2 * width : 3 * width, :]).astype(BF16)
        for col in range(0, cols, LANES):
            part = slice(col, col + LANES)
            q_part, k_part = q_raw[:, part], k_raw[:, part]
            q_ref[at, part] = (
                (q_part * cosine + swap_halves(q_part) * sine).astype(BF16) * (1.0 / math.sqrt(HDIM))
            ).astype(BF16)
            k_ref[at, part] = (k_part * cosine + swap_halves(k_part) * sine).astype(BF16)


def project(place, x, gain, weights, cosine, sine, after=()):
    rows, width = x.shape
    cols = weights[0].shape[1]
    gathered = len(weights) > 1
    operands = [place, x, gain, *weights, cosine, sine]
    return pl.pallas_call(
        functools.partial(ordered, functools.partial(project_kernel, gathered), len(after)),
        out_shape=(
            jax.ShapeDtypeStruct((rows, cols), BF16),
            jax.ShapeDtypeStruct((rows, cols), BF16),
            jax.ShapeDtypeStruct((rows, cols), BF16),
        ),
        in_specs=[ANYSPEC] * len(after) + [SSPEC] + [VSPEC] * (len(operands) - 1),
        out_specs=[VSPEC] * 3,
        scratch_shapes=[pltpu.VMEM((3 * width, cols), BF16)] if gathered else [],
        compiler_params=params(),
        cost_estimate=cost(gathered),
        name="project",
    )(*after, *operands)


def attend_kernel(q_ref, ko_ref, vo_ref, kx_ref, vx_ref, col_ref, row_ref, rowx_ref, o_ref, lse_ref, bo_ref, bx_ref):
    rows = q_ref.shape[0]
    tile = min(256, rows)

    @pl.when(pl.program_id(0) == 0)
    def _():
        col = col_ref[...][:, 0:1]
        bo_ref[...] = jnp.where(col == row_ref[0:1, :], 0.0, MASKED)
        bx_ref[...] = jnp.where(col == rowx_ref[0:1, :], 0.0, MASKED)

    for begin in range(0, rows, tile):
        at = pl.ds(begin, tile)
        low = low_lanes((tile, LANES))
        q_pair = q_ref[at, :]
        results, logs = [], []
        for head in range(2):
            chosen = low if head == 0 else jnp.logical_not(low)
            query = jnp.where(chosen, q_pair, jnp.zeros_like(q_pair))
            own = dot_t(query, ko_ref[...]) + bo_ref[at, :]
            other = dot_t(query, kx_ref[...]) + bx_ref[at, :]
            highest = jnp.maximum(
                jnp.max(own, axis=-1, keepdims=True), jnp.max(other, axis=-1, keepdims=True)
            )
            own = jnp.exp(own - highest)
            other = jnp.exp(other - highest)
            totals = jnp.sum(own, axis=-1, keepdims=True) + jnp.sum(other, axis=-1, keepdims=True)
            value = dot(own.astype(BF16), vo_ref[...]) + dot(other.astype(BF16), vx_ref[...])
            results.append(value / totals)
            logs.append(highest + jnp.log(totals))
        o_ref[at, :] = jnp.where(low, results[0], results[1]).astype(BF16)
        lse_ref[at, :] = jnp.where(low, logs[0], logs[1])


def attend(q, kv_own, kv_other, col, row, row_other, after=()):
    rows, cols = q.shape
    pairs = cols // LANES
    tok = pl.BlockSpec((rows, LANES), lambda p: (0, p))
    return pl.pallas_call(
        functools.partial(ordered, attend_kernel, len(after)),
        grid=(pairs,),
        out_shape=(
            jax.ShapeDtypeStruct((rows, cols), BF16),
            jax.ShapeDtypeStruct((rows, cols), F32),
        ),
        in_specs=[ANYSPEC] * len(after)
        + [
            tok,
            tok,
            tok,
            tok,
            tok,
            pl.BlockSpec((rows, LANES), lambda p: (0, 0)),
            pl.BlockSpec((8, rows), lambda p: (0, 0)),
            pl.BlockSpec((8, rows), lambda p: (0, 0)),
        ],
        out_specs=[tok, tok],
        scratch_shapes=[pltpu.VMEM((rows, rows), F32), pltpu.VMEM((rows, rows), F32)],
        compiler_params=params(semantics=("arbitrary",)),
        cost_estimate=cost(False),
        name="attend",
    )(*after, q, *kv_own, *kv_other, col, row, row_other)


def attend_back_kernel(
    q_ref, ko_ref, vo_ref, kx_ref, vx_ref, do_ref, o_ref, lse_ref, col_ref, colx_ref, row_ref, cos_ref, sin_ref,
    gq_ref, dko_ref, dvo_ref, dx_ref, bo_ref, bx_ref,
):
    rows = q_ref.shape[0]
    tile = min(256, rows)

    @pl.when(pl.program_id(0) == 0)
    def _():
        row = row_ref[0:1, :]
        bo_ref[...] = jnp.where(col_ref[...][:, 0:1] == row, 0.0, MASKED)
        bx_ref[...] = jnp.where(colx_ref[...][:, 0:1] == row, 0.0, MASKED)

    low = low_lanes((rows, LANES))
    q_pair, do_pair = q_ref[...], do_ref[...]
    product = do_pair.astype(F32) * o_ref[...].astype(F32)
    first = jnp.sum(jnp.where(low, product, 0.0), axis=-1, keepdims=True)
    second = jnp.sum(jnp.where(low, 0.0, product), axis=-1, keepdims=True)
    delta_t = jnp.transpose(jnp.where(low, first, second))
    lse_t = jnp.transpose(lse_ref[...])
    low_tile = low_lanes((tile, LANES))
    grad_q = jnp.zeros((rows, LANES), F32)
    for k_ref, v_ref, bias_ref, dk_ref, dv_ref in (
        (ko_ref, vo_ref, bo_ref, dko_ref, dvo_ref),
        (kx_ref, vx_ref, bx_ref, dx_ref.at[0], dx_ref.at[1]),
    ):
        for begin in range(0, rows, tile):
            at = pl.ds(begin, tile)
            k_pair, v_pair = k_ref[at, :], v_ref[at, :]
            grad_k = grad_v = None
            for head in range(2):
                chosen = low_tile if head == 0 else jnp.logical_not(low_tile)
                chosen_q = low if head == 0 else jnp.logical_not(low)
                key = jnp.where(chosen, k_pair, jnp.zeros_like(k_pair))
                value = jnp.where(chosen, v_pair, jnp.zeros_like(v_pair))
                query = jnp.where(chosen_q, q_pair, jnp.zeros_like(q_pair))
                grad_o = jnp.where(chosen_q, do_pair, jnp.zeros_like(do_pair))
                at_row = head * HDIM
                scores = dot_t(key, q_pair) + bias_ref[at, :]
                probs = jnp.exp(scores - lse_t[at_row : at_row + 1, :])
                grad_probs = dot_t(value, do_pair)
                grad_scores = (probs * (grad_probs - delta_t[at_row : at_row + 1, :])).astype(BF16)
                term_v = dot(probs.astype(BF16), grad_o)
                term_k = dot(grad_scores, query)
                grad_v = term_v if grad_v is None else grad_v + term_v
                grad_k = term_k if grad_k is None else grad_k + term_k
                grad_q = grad_q + t_dot(grad_scores, key)
            dk_ref[at, :] = grad_k.astype(dk_ref.dtype)
            dv_ref[at, :] = grad_v.astype(dv_ref.dtype)
    grad_q = grad_q * (1.0 / math.sqrt(HDIM))
    gq_ref[...] = (grad_q * cos_ref[...] - swap_halves(grad_q) * sin_ref[...]).astype(BF16)


def attend_back(q, kv_own, kv_other, grad_o, o, lse, col, col_other, row, cosine, sine, after=()):
    rows, cols = q.shape
    pairs = cols // LANES
    tok = pl.BlockSpec((rows, LANES), lambda p: (0, p))
    fixed = pl.BlockSpec((rows, LANES), lambda p: (0, 0))
    return pl.pallas_call(
        functools.partial(ordered, attend_back_kernel, len(after)),
        grid=(pairs,),
        out_shape=(
            jax.ShapeDtypeStruct((rows, cols), BF16),
            jax.ShapeDtypeStruct((rows, cols), F32),
            jax.ShapeDtypeStruct((rows, cols), F32),
            jax.ShapeDtypeStruct((2, rows, cols), BF16),
        ),
        in_specs=[ANYSPEC] * len(after)
        + [
            tok, tok, tok, tok, tok, tok, tok, tok, fixed, fixed,
            pl.BlockSpec((8, rows), lambda p: (0, 0)), fixed, fixed,
        ],
        out_specs=[tok] * 3 + [pl.BlockSpec((2, rows, LANES), lambda p: (0, 0, p))],
        scratch_shapes=[pltpu.VMEM((rows, rows), F32), pltpu.VMEM((rows, rows), F32)],
        compiler_params=params(semantics=("arbitrary",)),
        cost_estimate=cost(True),
        name="attend_back",
    )(*after, q, *kv_own, *kv_other, grad_o, o, lse, col, col_other, row, cosine, sine)


def middle_kernel(
    place_ref, x_ref, atto_ref, attx_ref, cot_ref, col_ref, gain_ref, wo_ref, wi_ref, wd_ref,
    p0, p1i, p1r, p2, p3i, p3r,
    out_ref, gm_ref, gao_ref, gax_ref, ak_ref, as_ref, gain_grad_ref, g_s, gml_s, hid_s,
    wi_s, wd_s, wo_s, b_s, gu_s, gg_s,
):
    rows, width = x_ref.shape
    units, cols = wd_ref.shape[0], wo_ref.shape[0]
    both = 2 * units
    wi_s[0:units, :] = wi_ref[0:units, :]
    wi_s[both : both + units, :] = wi_ref[units:both, :]
    wd_s[0:units, :] = wd_ref[...]
    wo_s[0:cols, :] = wo_ref[...]
    n_i, n_d, n_o = both // 4, units // 4, cols // 4
    n_r = n_d + n_o
    cut = (p0.at[0:n_i], p1i, p2.at[0:n_i], p3i)
    rest = (p0.at[n_i : n_i + n_r], p1r, p2.at[n_i : n_i + n_r], p3r)
    for step, piece_i, piece in zip((0, 2, 1, 3), cut, rest):
        at = place_ref[PIECE] ^ step
        to_i = units + (at % 2) * n_i + (at // 2) * both
        wi_s[pl.ds(aligned(to_i, 16), n_i), :] = piece_i[...]
        at = place_ref[PIECE_NEXT] ^ step
        wd_s[pl.ds(aligned(units + at * n_d, 16), n_d), :] = piece[0:n_d, :]
        wo_s[pl.ds(aligned(cols + at * n_o, 16), n_o), :] = piece[n_d:, :]
    tile = min(256, rows)
    gain = gain_ref[...]
    gain_grad = jnp.zeros((1, width), F32)
    for begin in range(0, rows, tile):
        at = pl.ds(begin, tile)
        mixed = x_ref[at, :].astype(F32) + dot(atto_ref[at, :], wo_s[0:cols, :]) + dot(attx_ref[at, :], wo_s[cols:, :])
        normed, scale = norm_parts(mixed)
        low = (normed * gain).astype(BF16)
        live = col_ref[at, 0:1] >= 0
        cot = cot_ref[at, :]
        grad_low = jnp.where(live, cot, jnp.zeros_like(cot))
        b_s[at, :] = low
        g_s[at, :] = grad_low
        up = dot_t(low, wi_s[0:both, :])
        gate = dot_t(low, wi_s[both:, :])
        cdf = 0.5 * (1.0 + lax.erf(up * (1.0 / math.sqrt(2.0))))
        act = up * cdf
        hid = (act * gate).astype(BF16)
        slope = cdf + up * (jnp.exp(-0.5 * up * up) * (1.0 / math.sqrt(2.0 * math.pi)))
        grad_hid = dot_t(grad_low, wd_s[...])
        grad_up = (grad_hid * gate * slope).astype(BF16)
        grad_gate = (grad_hid * act).astype(BF16)
        out_ref[at, :] = (mixed + dot(hid, wd_s[...])).astype(BF16)
        grad_b = dot(grad_up, wi_s[0:both, :]) + dot(grad_gate, wi_s[both:, :])
        hid_s[at, :] = hid
        gu_s[at, :] = grad_up
        gg_s[at, :] = grad_gate
        gain_grad = gain_grad + jnp.sum(grad_b * normed, axis=0, keepdims=True)
        scaled = grad_b * gain
        grad_mixed = grad_low.astype(F32) + scale * (
            scaled
            - jnp.mean(scaled, axis=-1, keepdims=True)
            - normed * jnp.mean(scaled * normed, axis=-1, keepdims=True)
        )
        gm_ref[at, :] = grad_mixed
        grad_mixed_low = grad_mixed.astype(BF16)
        gml_s[at, :] = grad_mixed_low
        gao_ref[at, :] = dot_t(grad_mixed_low, wo_s[0:cols, :]).astype(BF16)
        gax_ref[at, :] = dot_t(grad_mixed_low, wo_s[cols:, :]).astype(BF16)
    gain_grad_ref[...] = jnp.broadcast_to(gain_grad, gain_grad_ref.shape)
    half = width // 2
    core = place_ref[CORE]
    for a_ref, which in ((as_ref, 1 - core), (ak_ref, core)):
        low = b_s[:, pl.ds(aligned(which * half, LANES), half)]
        for row, src in ((0, gu_s), (units, gg_s)):
            grad = t_dot(src[...], low).astype(BF16)
            for side in range(2):
                for quarter in range(2):
                    at = side_block(which, side, row // n_i + quarter) * n_i
                    begin = side * units + quarter * n_i
                    a_ref[pl.ds(aligned(at, 16), n_i), :] = grad[begin : begin + n_i]


def outer_kernel(place_ref, atto_ref, attx_ref, hid_ref, g_ref, gml_ref, bk_ref, bs_ref):
    half = g_ref.shape[1] // 2
    units, cols = hid_ref.shape[1] // 2, atto_ref.shape[1]
    n_d, n_o = units // 4, cols // 4
    n_b = n_d + n_o
    core = place_ref[CORE]
    for b_ref, which in ((bs_ref, 1 - core), (bk_ref, core)):
        part = pl.ds(aligned(which * half, LANES), half)
        grad = t_dot(hid_ref[...], g_ref[:, part]).astype(BF16)
        grad_mixed_low = gml_ref[:, part]
        for side, att_ref in enumerate((atto_ref, attx_ref)):
            grad_o = t_dot(att_ref[...], grad_mixed_low).astype(BF16)
            for quarter in range(4):
                to = side_block(which, side, quarter) * n_b
                begin = side * units + quarter * n_d
                b_ref[pl.ds(aligned(to, 16), n_d), :] = grad[begin : begin + n_d]
                b_ref[pl.ds(aligned(to + n_d, 16), n_o), :] = grad_o[quarter * n_o : (quarter + 1) * n_o]


def outer(place, att_own, att_other, hid, g, gml):
    rows, width = g.shape
    size = hid.shape[1] + 2 * att_own.shape[1]
    return pl.pallas_call(
        outer_kernel,
        out_shape=(jax.ShapeDtypeStruct((size, width // 2), BF16),) * 2,
        in_specs=[SSPEC] + [VSPEC] * 5,
        out_specs=[VSPEC] * 2,
        compiler_params=params(),
        cost_estimate=cost(True),
        name="outer",
    )(place, att_own, att_other, hid, g, gml)


def middle(place, x, att_own, att_other, cot, col, gain, wo, wi, wd, pieces):
    rows, width = x.shape
    units, cols = wd.shape[0], wo.shape[0]
    size = 2 * cols * width + 6 * units * width
    half = width // 2
    return pl.pallas_call(
        middle_kernel,
        out_shape=(
            jax.ShapeDtypeStruct((rows, width), BF16),
            jax.ShapeDtypeStruct((rows, width), F32),
            jax.ShapeDtypeStruct((rows, cols), BF16),
            jax.ShapeDtypeStruct((rows, cols), BF16),
            jax.ShapeDtypeStruct((4 * units, half), BF16),
            jax.ShapeDtypeStruct((4 * units, half), BF16),
            jax.ShapeDtypeStruct((8, width), F32),
            jax.ShapeDtypeStruct((rows, width), BF16),
            jax.ShapeDtypeStruct((rows, width), BF16),
            jax.ShapeDtypeStruct((rows, 2 * units), BF16),
        ),
        in_specs=[SSPEC] + [VSPEC] * 15,
        out_specs=[VSPEC] * 10,
        scratch_shapes=[
            pltpu.VMEM((4 * units, width), BF16),
            pltpu.VMEM((2 * units, width), BF16),
            pltpu.VMEM((2 * cols, width), BF16),
            pltpu.VMEM((rows, width), BF16),
            pltpu.VMEM((rows, 2 * units), BF16),
            pltpu.VMEM((rows, 2 * units), BF16),
        ],
        compiler_params=params(34),
        cost_estimate=cost(True),
        name="middle",
    )(place, x, att_own, att_other, cot, col, gain, wo, wi, wd, *pieces)


def qkv_grads(place_ref, x_ref, gain_ref, gq_ref, dk_ref, dv_ref, recv_ref, cos_ref, sin_ref,
              keep_ref, send_ref, gk_ref, gv_ref, low_s):
    rows, width = x_ref.shape
    cols = gq_ref.shape[1]
    tile = min(256, rows)
    for begin in range(0, rows, tile):
        at = pl.ds(begin, tile)
        normed, _ = norm_parts(x_ref[at, :].astype(F32))
        low_s[at, :] = (normed * gain_ref[...]).astype(BF16)
        cosine, sine = cos_ref[at, :], sin_ref[at, :]
        for col in range(0, cols, LANES):
            part = slice(col, col + LANES)
            grad_k = dk_ref[at, part] + recv_ref[0, at, part].astype(F32)
            gk_ref[at, part] = (grad_k * cosine - swap_halves(grad_k) * sine).astype(BF16)
        gv_ref[at, :] = (dv_ref[at, :] + recv_ref[1, at, :].astype(F32)).astype(BF16)
    half = width // 2
    size = half // 4
    core = place_ref[CORE]
    for to_ref, which in ((send_ref, 1 - core), (keep_ref, core)):
        low = low_s[:, pl.ds(aligned(which * half, LANES), half)]
        for item, src in enumerate((gq_ref, gk_ref, gv_ref)):
            grad = t_dot(low, src[...]).astype(BF16)
            for quarter in range(4):
                to = (quarter * 3 + item) * size
                to_ref[to : to + size, :] = grad[quarter * size : (quarter + 1) * size]


def project_grads(place, x, gain, gq, dk, dv, received, cosine, sine, after=()):
    rows, width = x.shape
    cols = gq.shape[1]
    operands = [x, gain, gq, dk, dv, received, cosine, sine]
    return pl.pallas_call(
        functools.partial(ordered, qkv_grads, len(after)),
        out_shape=(jax.ShapeDtypeStruct((3 * width // 2, cols), BF16),) * 2
        + (jax.ShapeDtypeStruct((rows, cols), BF16),) * 2,
        in_specs=[ANYSPEC] * len(after) + [SSPEC] + [VSPEC] * len(operands),
        out_specs=[VSPEC] * 4,
        scratch_shapes=[pltpu.VMEM((rows, width), BF16)],
        compiler_params=params(24),
        cost_estimate=cost(True),
        name="project_grads",
    )(*after, place, *operands)


def project_back_kernel(
    place_ref, x_ref, gain_ref, gq_ref, dk_ref, dv_ref, recv_ref, cos_ref, sin_ref, w_ref,
    gqx_ref, gkx_ref, gvx_ref, w0, w1, w2, gm_ref,
    keep_ref, send_ref, gx_ref, gain_grad_ref, low_s, gk_s, gv_s, wx_s,
):
    qkv_grads(place_ref, x_ref, gain_ref, gq_ref, dk_ref, dv_ref, recv_ref, cos_ref, sin_ref,
              keep_ref, send_ref, gk_s, gv_s, low_s)
    load_pieces(place_ref, (w0, w1, w2), wx_s)
    rows, width = x_ref.shape
    tile = min(256, rows)
    gain = gain_ref[...]
    gain_grad = jnp.zeros((1, width), F32)
    for begin in range(0, rows, tile):
        at = pl.ds(begin, tile)
        normed, scale = norm_parts(x_ref[at, :].astype(F32))
        total = jnp.zeros((tile, width), F32)
        for item, (own, other) in enumerate(((gq_ref, gqx_ref), (gk_s, gkx_ref), (gv_s, gvx_ref))):
            part = slice(item * width, (item + 1) * width)
            total = total + dot_t(own[at, :], w_ref[part, :]) + dot_t(other[at, :], wx_s[part, :])
        gain_grad = gain_grad + jnp.sum(total * normed, axis=0, keepdims=True)
        scaled = total * gain
        gx_ref[at, :] = (
            gm_ref[at, :]
            + scale
            * (
                scaled
                - jnp.mean(scaled, axis=-1, keepdims=True)
                - normed * jnp.mean(scaled * normed, axis=-1, keepdims=True)
            )
        ).astype(BF16)
    gain_grad_ref[...] = jnp.broadcast_to(gain_grad, gain_grad_ref.shape)


def project_back(place, x, gain, gq, dk, dv, received, cosine, sine, weight, others, pieces, grad_mixed, after):
    rows, width = x.shape
    cols = gq.shape[1]
    operands = [x, gain, gq, dk, dv, received, cosine, sine, weight, *others, *pieces, grad_mixed]
    return pl.pallas_call(
        functools.partial(ordered, project_back_kernel, len(after)),
        out_shape=(
            jax.ShapeDtypeStruct((3 * width // 2, cols), BF16),
            jax.ShapeDtypeStruct((3 * width // 2, cols), BF16),
            jax.ShapeDtypeStruct((rows, width), BF16),
            jax.ShapeDtypeStruct((8, width), F32),
        ),
        in_specs=[ANYSPEC] * len(after) + [SSPEC] + [VSPEC] * len(operands),
        out_specs=[VSPEC] * 4,
        scratch_shapes=[
            pltpu.VMEM((rows, width), BF16),
            pltpu.VMEM((rows, cols), BF16),
            pltpu.VMEM((rows, cols), BF16),
            pltpu.VMEM((3 * width, cols), BF16),
        ],
        compiler_params=params(32),
        cost_estimate=cost(True),
        name="project_back",
    )(*after, place, *operands)


def pack(place, weights, after=(), entries=None):
    sizes = [value.shape[0] // 4 for value in weights]
    width = weights[0].shape[1]
    entries = entries or [PIECE] * len(weights)

    def spec(size, entry):
        return pl.BlockSpec((size, width), lambda _, at: (at[entry], 0))

    def kernel(place_ref, *refs):
        begin = 0
        for ref, size in zip(refs[len(after) :], sizes):
            refs[-1][begin : begin + size, :] = ref[...]
            begin += size

    return pl.pallas_call(
        kernel,
        grid_spec=pltpu.PrefetchScalarGridSpec(
            num_scalar_prefetch=1,
            grid=(1,),
            in_specs=[ANYSPEC] * len(after)
            + [spec(size, entry) for size, entry in zip(sizes, entries)],
            out_specs=pl.BlockSpec((sum(sizes), width), lambda _, at: (0, 0)),
        ),
        out_shape=jax.ShapeDtypeStruct((sum(sizes), width), BF16),
        compiler_params=params(semantics=("arbitrary",)),
        cost_estimate=cost(False),
        name="pack",
    )(place, *after, *weights)


def merge_kernel(jobs, after, place_ref, *refs):
    ins = list(refs[after : after + sum(job["count"] for job in jobs)])
    outs = list(refs[after + len(ins) :])
    for job in jobs:
        mine, ins = ins[: job["count"]], ins[job["count"] :]
        which = job["which"]
        if which is None:
            out_ref, outs = outs[0], outs[1:]
            out_ref[...] = sum(ref[...].astype(F32) for ref in mine).astype(out_ref.dtype)
            continue
        size = outs[0].shape[0]
        bit = place_ref[which]
        for out_ref, half in ((outs[0], 1 - bit), (outs[1], bit)):
            at = pl.ds(aligned(half * size, 16), size)
            total = sum(ref[at, :].astype(F32) for ref in (mine[:-2] if which == FIRST else mine))
            if which == FIRST:
                total = total + jnp.where(half == 0, mine[-2][...], mine[-1][...]).astype(F32)
            out_ref[...] = total.astype(BF16)
        outs = outs[2:]


def merge(place, *jobs, after=(), covers=True):
    arrays, shapes, notes = [], [], []
    for values, which in jobs:
        rows, cols = values[0].shape
        parts = 1 if which is None else 2
        shapes += [jax.ShapeDtypeStruct((rows // parts, cols), values[0].dtype)] * parts
        notes.append({"count": len(values), "which": which})
        arrays += values
    out = pl.pallas_call(
        functools.partial(merge_kernel, notes, len(after)),
        out_shape=tuple(shapes),
        in_specs=[SSPEC] + [ANYSPEC] * len(after) + [VSPEC] * len(arrays),
        out_specs=[VSPEC] * len(shapes),
        compiler_params=params(),
        cost_estimate=cost(covers),
        name="merge",
    )(place, *after, *arrays)
    return out


def join_kernel(counts, after, *refs):
    ins, outs = list(refs[after : after + sum(counts)]), refs[after + sum(counts) :]
    for count, out_ref in zip(counts, outs):
        size = out_ref.shape[0] // count
        for step in range(count):
            out_ref[step * size : (step + 1) * size, :] = ins[step][...]
        ins = ins[count:]


def join(*groups, after=(), covers=True):
    values = [value for group in groups for value in group]
    return pl.pallas_call(
        functools.partial(join_kernel, [len(group) for group in groups], len(after)),
        out_shape=tuple(
            jax.ShapeDtypeStruct((len(group) * group[0].shape[0], group[0].shape[1]), BF16) for group in groups
        ),
        in_specs=[ANYSPEC] * len(after) + [VSPEC] * len(values),
        out_specs=[VSPEC] * len(groups),
        compiler_params=params(),
        cost_estimate=cost(covers),
        name="join",
    )(*after, *values)


def assemble_kernel(kind, after, place_ref, *refs):
    pieces, outs = list(refs[after : after + 4]), refs[after + 5 : -1]
    refs[-1][...] = jnp.zeros(refs[-1].shape, F32)
    core = place_ref[CORE]
    size = pieces[0].shape[0]
    pieces += [refs[after + 4].at[step * size : (step + 1) * size] for step in range(4)]
    for step, piece in enumerate(pieces):
        mine = step < 4
        quarter = place_ref[MINE if mine else THEIRS] ^ (step % 4)
        side = core if mine else 1 - core
        if kind == "qkv":
            rows = size // 3
            for item in range(3):
                at = pl.ds(aligned((side * 4 + quarter) * rows, 8), rows)
                outs[0][item, at, :] = piece[item * rows : (item + 1) * rows, :].astype(F32)
            continue
        half = outs[0].shape[1] // 2
        part = pl.ds(aligned(side * half, LANES), half)
        begin = 0
        for out_ref in outs:
            rows = out_ref.shape[0] // 4
            at = pl.ds(aligned(quarter * rows, 8), rows)
            out_ref[at, part] = piece[begin : begin + rows, :].astype(F32)
            begin += rows


def assemble(kind, place, pieces, shapes, after=()):
    total = sum(math.prod(shape) for shape in shapes)
    return pl.pallas_call(
        functools.partial(assemble_kernel, kind, len(after)),
        out_shape=tuple(jax.ShapeDtypeStruct(shape, F32) for shape in [*shapes, (8, LANES)]),
        in_specs=[SSPEC] + [ANYSPEC] * len(after) + [VSPEC] * 5,
        out_specs=[VSPEC] * (len(shapes) + 1),
        compiler_params=params(),
        cost_estimate=cost(True),
        name="assemble",
    )(place, *after, *pieces)


def per_device(
    axis_sizes,
    hidden,
    seq_ids,
    cotangent,
    qkv_weight,
    attn_out_weight,
    mlp_in_weight,
    mlp_out_weight,
    norm1_gain,
    norm2_gain,
):
    dp_size, tensor_size = axis_sizes
    devices = dp_size * tensor_size
    chips = devices // 4
    chip_bits = chips.bit_length() - 1
    rows, width = hidden.shape
    cols = qkv_weight.shape[2]
    units = mlp_out_weight.shape[0]
    dp_at = lax.axis_index("dp")
    core = dp_at % 2
    chip = dp_at // 2

    def move(value, target):
        return lax.ppermute(value, ("dp", "tensor"), [(i, target(i)) for i in range(devices)])

    def swapped(i):
        return (i & ~3) | ((i & 1) << 1) | ((i >> 1) & 1)

    def to_tensor(i):
        return i ^ 1

    def to_core(i):
        return i ^ 2

    def to_near(i):
        return i ^ 4

    def to_next(i):
        return i ^ 8

    def masked(first, second):
        return lambda i: i ^ (second if i & 2 else first)

    near, next_near = chip % 2, (chip // 2) % 2
    quarters = [near * 2 + next_near, next_near * 2 + near]
    place = jnp.stack(
        [
            core,
            near * 2 + core,
            next_near * 2 + core,
            jnp.where(core == 0, quarters[0], quarters[1]),
            jnp.where(core == 0, quarters[1], quarters[0]),
            jnp.where(core == 0, 0, next_near),
            jnp.where(core == 0, near, 0),
            jnp.where(core == 0, next_near, near),
            jnp.where(core == 0, near, next_near),
            jnp.where(core == 0, next_near, near),
        ]
    ).astype(jnp.int32)

    x = move(hidden, swapped)
    ids = jnp.where(core == lax.axis_index("tensor"), seq_ids, move(seq_ids, to_core))
    ids_own = lax.dynamic_slice_in_dim(ids, core * rows, rows)
    ids_other = lax.dynamic_slice_in_dim(ids, (1 - core) * rows, rows)

    index = jnp.arange(ids.shape[0], dtype=jnp.int32)
    begins = jnp.zeros((rows,), jnp.int32)
    for number in (-1, 0, 1, 2):
        start = jnp.min(jnp.where(ids == number, index, ids.shape[0]))
        begins = jnp.where(ids_own == number, start, begins)
    pos = core * rows + jnp.arange(rows, dtype=jnp.int32) - begins
    frequency = jnp.power(ROPE_BASE, -2.0 * jnp.arange(HDIM // 2, dtype=F32) / HDIM)
    angles = pos.astype(F32)[:, None] * frequency[None, :]
    cosine, sine = jnp.cos(angles), jnp.sin(angles)
    cosine = jnp.concatenate([cosine] * 4, axis=1)
    sine = jnp.concatenate([-sine, sine] * 2, axis=1)
    col_own = jnp.broadcast_to(ids_own[:, None], (rows, LANES))
    col_other = jnp.broadcast_to(ids_other[:, None], (rows, LANES))
    row_own = jnp.broadcast_to(ids_own[None, :], (8, rows))
    row_other = jnp.broadcast_to(ids_other[None, :], (8, rows))

    w_qkv = qkv_weight.reshape(3 * width, cols)
    w_in = jnp.swapaxes(mlp_in_weight, 1, 2).reshape(2 * units, width)
    w_qkv_part = pack(place, [w_qkv])
    w_qkv_one = move(w_qkv_part, to_tensor)
    w_part = pack(
        place, [w_in, mlp_out_weight, attn_out_weight], [w_qkv_one], entries=[PIECE, PIECE_NEXT, PIECE_NEXT]
    )
    w_one = move(w_part, to_tensor)
    cot = move(cotangent, swapped)
    gain1, gain2 = norm1_gain[None, :], norm2_gain[None, :]

    (sent,) = join([w_qkv_one], covers=False)
    w_qkv_two = move(sent, to_near)
    q_a, *kv_a = project(place, x, gain1, [w_qkv], cosine, sine, after=[sent])
    kv_a_x = [move(value, to_core) for value in kv_a]
    o_a, lse_a = attend(q_a, kv_a, kv_a_x, col_own, row_own, row_other)
    sent, both = join([w_one], [w_qkv_one, w_qkv_two], after=[o_a], covers=False)
    in_rows = w_in.shape[0] // 4
    w_in_two, w_rest_two = move(sent[:in_rows], to_near), move(sent[in_rows:], to_next)
    w_qkv_x = [w_qkv_one, w_qkv_two, move(both, to_core)]
    q_b, *kv_b = project(place, x, gain1, w_qkv_x, cosine, sine, after=[sent])
    kv_b_x = [move(value, to_core) for value in kv_b]
    o_b, lse_b = attend(q_b, kv_b, kv_b_x, col_own, row_own, row_other)
    in_sent, rest_sent = join([w_in_two], [w_rest_two], after=[o_b], covers=False)
    w_x = [w_one, w_in_two, w_rest_two] + [move(value, to_core) for value in (w_one, in_sent, rest_sent)]
    out, grad_mixed, go_a, go_b, in_keep, in_send, gain2_part, grad_low, grad_mixed_low, hid = middle(
        place, x, o_a, o_b, cot, col_own, gain2, attn_out_weight, w_in, mlp_out_weight, w_x
    )
    rest_keep, rest_send = outer(place, o_a, o_b, hid, grad_low, grad_mixed_low)

    plain = range(2, chip_bits)

    def spread(total, after=()):
        one = move(total, masked(8, 4))
        two = move(total, masked(4, 8))
        mine = [total, one, two, move(one, masked(4, 8))]
        return mine + [move(join(mine, after=after)[0], to_core)]

    def back(q, kv, kv_x, go, o, lse, after):
        gq, dk, dv, dx = attend_back(q, kv, kv_x, go, o, lse, col_own, col_other, row_own, cosine, sine, after)
        return gq, dk, dv, move(dx, to_core)

    def pair(value, mask):
        return [value, move(value, masked(mask, mask))]

    target_1, target_2, target_3 = masked(1, 8), masked(4, 1), masked(8, 4)
    in_got = move(in_send, to_core)
    rest_got = move(rest_send, to_core)
    in_sent, in_kept = merge(place, ([in_keep, in_got], ONE))
    gq_b, dk_b, dv_b, recv_b = back(q_b, kv_b, kv_b_x, go_b, o_b, lse_b, [in_sent])
    in_got = move(in_sent, target_1)
    in_sent, in_kept, rest_sent, rest_kept = merge(
        place, ([in_kept, in_got], TWO), ([rest_keep, rest_got], ONE), after=[gq_b]
    )
    keep_b, send_b, gk_b, gv_b = project_grads(place, x, gain1, gq_b, dk_b, dv_b, recv_b, cosine, sine, [in_sent])
    (qkv_sum,) = merge(place, ([keep_b, move(send_b, to_core)], None), covers=False)
    half = qkv_sum.shape[0] // 2
    low_got = move(qkv_sum[:half], to_tensor)
    gq_a, dk_a, dv_a, recv_a = back(q_a, kv_a, kv_a_x, go_a, o_a, lse_a, [qkv_sum])
    in_got = move(in_sent, target_2)
    rest_got = move(rest_sent, target_1)
    in_sent, in_kept, rest_sent, rest_kept = merge(
        place, ([in_kept, in_got], THREE), ([rest_kept, rest_got], TWO), after=[gq_a, low_got]
    )
    in_got = move(in_sent, target_3)
    rest_got = move(rest_sent, target_2)
    high_got = move(qkv_sum[half:], to_tensor)
    keep_a, send_a, input_grad, gain1_part = project_back(
        place, x, gain1, gq_a, dk_a, dv_a, recv_a, cosine, sine, w_qkv, [gq_b, gk_b, gv_b], w_qkv_x, grad_mixed,
        [in_sent],
    )
    in_total, rest_sent, rest_kept = merge(
        place, ([in_kept, in_got], None), ([rest_kept, rest_got], THREE), after=[keep_a, high_got]
    )
    rest_got = move(rest_sent, target_3)
    out, input_grad = move(out, swapped), move(input_grad, swapped)
    gains = jnp.concatenate([gain1_part, gain2_part])
    sent, kept, gains = merge(
        place,
        ([keep_a, move(send_a, to_core), low_got, high_got], FIRST),
        (pair(gains, 2), None),
        after=[in_total],
    )
    sent, kept, gains, rest_total = merge(
        place,
        ([kept, move(sent, masked(4, 8))], SECOND),
        (pair(gains, 4), None),
        ([rest_kept, rest_got], None),
    )
    for b in plain:
        (in_total,) = merge(place, (pair(in_total, 4 << b), None), after=[sent])
    in_pieces = spread(in_total)
    qkv_total, gains = merge(
        place, ([kept, move(sent, masked(8, 4))], None), (pair(gains, 8), None), after=[in_total]
    )
    for b in plain:
        (rest_total,) = merge(place, (pair(rest_total, 4 << b), None), after=[qkv_total])
    rest_pieces = spread(rest_total)
    g_in, in_done = assemble("in", place, in_pieces, [(2 * units, width)])
    out, input_grad = join([out], [input_grad], covers=False)
    for b in plain:
        qkv_total, gains = merge(
            place, (pair(qkv_total, 4 << b), None), (pair(gains, 4 << b), None), after=[input_grad, in_pieces[3]]
        )
    qkv_pieces = spread(qkv_total, [in_done])
    gains = sum(pair(gains, 1))
    g_down, g_out, _ = assemble("rest", place, rest_pieces, [(units, width), (cols, width)], after=[qkv_total])
    g_qkv, _ = assemble("qkv", place, qkv_pieces, [(3, width, cols)])
    return (
        out,
        input_grad,
        gains[0],
        gains[8],
        g_qkv,
        g_out,
        jnp.swapaxes(g_in.reshape(2, units, width), 1, 2),
        g_down,
    )


def solution(mesh):
    in_specs = (
        P(("dp", "tensor"), None),
        P("dp"),
        P(("dp", "tensor"), None),
        P(None, None, "tensor"),
        P("tensor", None),
        P(None, None, "tensor"),
        P("tensor", None),
        P(),
        P(),
    )
    out_specs = (
        P(("dp", "tensor"), None),
        P(("dp", "tensor"), None),
        P(),
        P(),
        P(None, None, "tensor"),
        P("tensor", None),
        P(None, None, "tensor"),
        P("tensor", None),
    )
    return jax.shard_map(
        functools.partial(per_device, (mesh.shape["dp"], mesh.shape["tensor"])),
        mesh=mesh,
        in_specs=in_specs,
        out_specs=out_specs,
        check_vma=False,
    )
```

```python
import functools
import math

import jax
import jax.numpy as jnp
from jax import lax
from jax.experimental import pallas as pl
from jax.experimental.pallas import tpu as pltpu
from jax.sharding import PartitionSpec as P

HDIM = 64
LANES = 128
EPSILON = 1e-05
ROPE_BASE = 160000.0
MASKED = -1e30
F32 = jnp.float32
BF16 = jnp.bfloat16
MIB = 1024 * 1024


def dot(left, right):
    return jnp.dot(left, right, preferred_element_type=F32)


def dot_t(left, right):
    return lax.dot_general(left, right, (((1,), (1,)), ((), ())), preferred_element_type=F32)


def t_dot(left, right):
    return lax.dot_general(left, right, (((0,), (0,)), ((), ())), preferred_element_type=F32)


def norm_parts(values):
    center = values - jnp.mean(values, axis=-1, keepdims=True)
    spread = jnp.mean(center * center, axis=-1, keepdims=True)
    scale = lax.rsqrt(spread + EPSILON)
    return center * scale, scale


def swap_halves(values):
    lane = lax.broadcasted_iota(jnp.int32, values.shape, 1) % HDIM
    return jnp.where(
        lane < HDIM // 2,
        pltpu.roll(values, LANES - HDIM // 2, 1),
        pltpu.roll(values, HDIM // 2, 1),
    )


def low_lanes(shape):
    return lax.broadcasted_iota(jnp.int32, shape, 1) < HDIM


def cost(covers):
    return pl.CostEstimate(flops=20_000_000_000 if covers else 1_000, bytes_accessed=1_024, transcendentals=0)


def params(mib=20, semantics=None):
    return pltpu.CompilerParams(vmem_limit_bytes=mib * MIB, dimension_semantics=semantics)


VSPEC = pl.BlockSpec(memory_space=pltpu.VMEM)
SSPEC = pl.BlockSpec(memory_space=pltpu.SMEM)
ANYSPEC = pl.BlockSpec(memory_space=pl.ANY)
CORE, PIECE, PIECE_NEXT, MINE, THEIRS, ONE, TWO, THREE, FIRST, SECOND = range(10)


def aligned(value, by):
    return pl.multiple_of(value, by)


def side_block(core, side, quarter):
    return jnp.where(core == 0, side * 4 + quarter, (quarter // 2) * 4 + side * 2 + quarter % 2)


def ordered(kernel, count, *refs):
    kernel(*refs[count:])


def quarters_of(place_ref, pieces):
    one, two, others = pieces
    size = one.shape[0]
    for step, piece in ((0, one), (2, two), (1, others.at[0:size]), (3, others.at[size : 2 * size])):
        yield place_ref[PIECE] ^ step, piece


def load_pieces(place_ref, pieces, w_s):
    size = pieces[0].shape[0]
    for at, piece in quarters_of(place_ref, pieces):
        w_s[pl.ds(aligned(at * size, 16), size), :] = piece[...]


def project_kernel(gathered, *refs):
    if gathered:
        place_ref, x_ref, gain_ref, w0, w1, w2, cos_ref, sin_ref, q_ref, k_ref, v_ref, w_ref = refs
        load_pieces(place_ref, (w0, w1, w2), w_ref)
    else:
        place_ref, x_ref, gain_ref, w_ref, cos_ref, sin_ref, q_ref, k_ref, v_ref = refs
    rows, width = x_ref.shape
    cols = q_ref.shape[1]
    tile = min(256, rows)
    for begin in range(0, rows, tile):
        at = pl.ds(begin, tile)
        normed, _ = norm_parts(x_ref[at, :].astype(F32))
        low = (normed * gain_ref[...]).astype(BF16)
        cosine, sine = cos_ref[at, :], sin_ref[at, :]
        q_raw = dot(low, w_ref[0:width, :])
        k_raw = dot(low, w_ref[width : 2 * width, :])
        v_ref[at, :] = dot(low, w_ref[2 * width : 3 * width, :]).astype(BF16)
        for col in range(0, cols, LANES):
            part = slice(col, col + LANES)
            q_part, k_part = q_raw[:, part], k_raw[:, part]
            q_ref[at, part] = (
                (q_part * cosine + swap_halves(q_part) * sine).astype(BF16) * (1.0 / math.sqrt(HDIM))
            ).astype(BF16)
            k_ref[at, part] = (k_part * cosine + swap_halves(k_part) * sine).astype(BF16)


def project(place, x, gain, weights, cosine, sine, after=()):
    rows, width = x.shape
    cols = weights[0].shape[1]
    gathered = len(weights) > 1
    operands = [place, x, gain, *weights, cosine, sine]
    return pl.pallas_call(
        functools.partial(ordered, functools.partial(project_kernel, gathered), len(after)),
        out_shape=(
            jax.ShapeDtypeStruct((rows, cols), BF16),
            jax.ShapeDtypeStruct((rows, cols), BF16),
            jax.ShapeDtypeStruct((rows, cols), BF16),
        ),
        in_specs=[ANYSPEC] * len(after) + [SSPEC] + [VSPEC] * (len(operands) - 1),
        out_specs=[VSPEC] * 3,
        scratch_shapes=[pltpu.VMEM((3 * width, cols), BF16)] if gathered else [],
        compiler_params=params(),
        cost_estimate=cost(gathered),
        name="project",
    )(*after, *operands)


def attend_kernel(q_ref, ko_ref, vo_ref, kx_ref, vx_ref, col_ref, row_ref, rowx_ref, o_ref, lse_ref, bo_ref, bx_ref):
    rows = q_ref.shape[0]
    tile = min(256, rows)

    @pl.when(pl.program_id(0) == 0)
    def _():
        col = col_ref[...][:, 0:1]
        bo_ref[...] = jnp.where(col == row_ref[0:1, :], 0.0, MASKED)
        bx_ref[...] = jnp.where(col == rowx_ref[0:1, :], 0.0, MASKED)

    for begin in range(0, rows, tile):
        at = pl.ds(begin, tile)
        low = low_lanes((tile, LANES))
        q_pair = q_ref[at, :]
        results, logs = [], []
        for head in range(2):
            chosen = low if head == 0 else jnp.logical_not(low)
            query = jnp.where(chosen, q_pair, jnp.zeros_like(q_pair))
            own = dot_t(query, ko_ref[...]) + bo_ref[at, :]
            other = dot_t(query, kx_ref[...]) + bx_ref[at, :]
            highest = jnp.maximum(
                jnp.max(own, axis=-1, keepdims=True), jnp.max(other, axis=-1, keepdims=True)
            )
            own = jnp.exp(own - highest)
            other = jnp.exp(other - highest)
            totals = jnp.sum(own, axis=-1, keepdims=True) + jnp.sum(other, axis=-1, keepdims=True)
            value = dot(own.astype(BF16), vo_ref[...]) + dot(other.astype(BF16), vx_ref[...])
            results.append(value / totals)
            logs.append(highest + jnp.log(totals))
        o_ref[at, :] = jnp.where(low, results[0], results[1]).astype(BF16)
        lse_ref[at, :] = jnp.where(low, logs[0], logs[1])


def attend(q, kv_own, kv_other, col, row, row_other, after=()):
    rows, cols = q.shape
    pairs = cols // LANES
    tok = pl.BlockSpec((rows, LANES), lambda p: (0, p))
    return pl.pallas_call(
        functools.partial(ordered, attend_kernel, len(after)),
        grid=(pairs,),
        out_shape=(
            jax.ShapeDtypeStruct((rows, cols), BF16),
            jax.ShapeDtypeStruct((rows, cols), F32),
        ),
        in_specs=[ANYSPEC] * len(after)
        + [
            tok,
            tok,
            tok,
            tok,
            tok,
            pl.BlockSpec((rows, LANES), lambda p: (0, 0)),
            pl.BlockSpec((8, rows), lambda p: (0, 0)),
            pl.BlockSpec((8, rows), lambda p: (0, 0)),
        ],
        out_specs=[tok, tok],
        scratch_shapes=[pltpu.VMEM((rows, rows), F32), pltpu.VMEM((rows, rows), F32)],
        compiler_params=params(semantics=("arbitrary",)),
        cost_estimate=cost(False),
        name="attend",
    )(*after, q, *kv_own, *kv_other, col, row, row_other)


def attend_back_kernel(
    q_ref, ko_ref, vo_ref, kx_ref, vx_ref, do_ref, o_ref, lse_ref, col_ref, colx_ref, row_ref, cos_ref, sin_ref,
    gq_ref, dko_ref, dvo_ref, dx_ref, bo_ref, bx_ref,
):
    rows = q_ref.shape[0]
    tile = min(256, rows)

    @pl.when(pl.program_id(0) == 0)
    def _():
        row = row_ref[0:1, :]
        bo_ref[...] = jnp.where(col_ref[...][:, 0:1] == row, 0.0, MASKED)
        bx_ref[...] = jnp.where(colx_ref[...][:, 0:1] == row, 0.0, MASKED)

    low = low_lanes((rows, LANES))
    q_pair, do_pair = q_ref[...], do_ref[...]
    product = do_pair.astype(F32) * o_ref[...].astype(F32)
    first = jnp.sum(jnp.where(low, product, 0.0), axis=-1, keepdims=True)
    second = jnp.sum(jnp.where(low, 0.0, product), axis=-1, keepdims=True)
    delta_t = jnp.transpose(jnp.where(low, first, second))
    lse_t = jnp.transpose(lse_ref[...])
    low_tile = low_lanes((tile, LANES))
    grad_q = jnp.zeros((rows, LANES), F32)
    for k_ref, v_ref, bias_ref, dk_ref, dv_ref in (
        (ko_ref, vo_ref, bo_ref, dko_ref, dvo_ref),
        (kx_ref, vx_ref, bx_ref, dx_ref.at[0], dx_ref.at[1]),
    ):
        for begin in range(0, rows, tile):
            at = pl.ds(begin, tile)
            k_pair, v_pair = k_ref[at, :], v_ref[at, :]
            grad_k = grad_v = None
            for head in range(2):
                chosen = low_tile if head == 0 else jnp.logical_not(low_tile)
                chosen_q = low if head == 0 else jnp.logical_not(low)
                key = jnp.where(chosen, k_pair, jnp.zeros_like(k_pair))
                value = jnp.where(chosen, v_pair, jnp.zeros_like(v_pair))
                query = jnp.where(chosen_q, q_pair, jnp.zeros_like(q_pair))
                grad_o = jnp.where(chosen_q, do_pair, jnp.zeros_like(do_pair))
                at_row = head * HDIM
                scores = dot_t(key, q_pair) + bias_ref[at, :]
                probs = jnp.exp(scores - lse_t[at_row : at_row + 1, :])
                grad_probs = dot_t(value, do_pair)
                grad_scores = (probs * (grad_probs - delta_t[at_row : at_row + 1, :])).astype(BF16)
                term_v = dot(probs.astype(BF16), grad_o)
                term_k = dot(grad_scores, query)
                grad_v = term_v if grad_v is None else grad_v + term_v
                grad_k = term_k if grad_k is None else grad_k + term_k
                grad_q = grad_q + t_dot(grad_scores, key)
            dk_ref[at, :] = grad_k.astype(dk_ref.dtype)
            dv_ref[at, :] = grad_v.astype(dv_ref.dtype)
    grad_q = grad_q * (1.0 / math.sqrt(HDIM))
    gq_ref[...] = (grad_q * cos_ref[...] - swap_halves(grad_q) * sin_ref[...]).astype(BF16)


def attend_back(q, kv_own, kv_other, grad_o, o, lse, col, col_other, row, cosine, sine, after=()):
    rows, cols = q.shape
    pairs = cols // LANES
    tok = pl.BlockSpec((rows, LANES), lambda p: (0, p))
    fixed = pl.BlockSpec((rows, LANES), lambda p: (0, 0))
    return pl.pallas_call(
        functools.partial(ordered, attend_back_kernel, len(after)),
        grid=(pairs,),
        out_shape=(
            jax.ShapeDtypeStruct((rows, cols), BF16),
            jax.ShapeDtypeStruct((rows, cols), F32),
            jax.ShapeDtypeStruct((rows, cols), F32),
            jax.ShapeDtypeStruct((2, rows, cols), BF16),
        ),
        in_specs=[ANYSPEC] * len(after)
        + [
            tok, tok, tok, tok, tok, tok, tok, tok, fixed, fixed,
            pl.BlockSpec((8, rows), lambda p: (0, 0)), fixed, fixed,
        ],
        out_specs=[tok] * 3 + [pl.BlockSpec((2, rows, LANES), lambda p: (0, 0, p))],
        scratch_shapes=[pltpu.VMEM((rows, rows), F32), pltpu.VMEM((rows, rows), F32)],
        compiler_params=params(semantics=("arbitrary",)),
        cost_estimate=cost(True),
        name="attend_back",
    )(*after, q, *kv_own, *kv_other, grad_o, o, lse, col, col_other, row, cosine, sine)


def middle_kernel(
    place_ref, x_ref, atto_ref, attx_ref, cot_ref, col_ref, gain_ref, wo_ref, wi_ref, wd_ref,
    p0, p1i, p1r, p2, p3i, p3r,
    out_ref, gm_ref, gao_ref, gax_ref, ak_ref, as_ref, gain_grad_ref, g_s, gml_s, hid_s,
    wi_s, wd_s, wo_s, b_s, gu_s, gg_s,
):
    rows, width = x_ref.shape
    units, cols = wd_ref.shape[0], wo_ref.shape[0]
    both = 2 * units
    wi_s[0:units, :] = wi_ref[0:units, :]
    wi_s[both : both + units, :] = wi_ref[units:both, :]
    wd_s[0:units, :] = wd_ref[...]
    wo_s[0:cols, :] = wo_ref[...]
    n_i, n_d, n_o = both // 4, units // 4, cols // 4
    n_r = n_d + n_o
    cut = (p0.at[0:n_i], p1i, p2.at[0:n_i], p3i)
    rest = (p0.at[n_i : n_i + n_r], p1r, p2.at[n_i : n_i + n_r], p3r)
    for step, piece_i, piece in zip((0, 2, 1, 3), cut, rest):
        at = place_ref[PIECE] ^ step
        to_i = units + (at % 2) * n_i + (at // 2) * both
        wi_s[pl.ds(aligned(to_i, 16), n_i), :] = piece_i[...]
        at = place_ref[PIECE_NEXT] ^ step
        wd_s[pl.ds(aligned(units + at * n_d, 16), n_d), :] = piece[0:n_d, :]
        wo_s[pl.ds(aligned(cols + at * n_o, 16), n_o), :] = piece[n_d:, :]
    tile = min(256, rows)
    gain = gain_ref[...]
    gain_grad = jnp.zeros((1, width), F32)
    for begin in range(0, rows, tile):
        at = pl.ds(begin, tile)
        mixed = x_ref[at, :].astype(F32) + dot(atto_ref[at, :], wo_s[0:cols, :]) + dot(attx_ref[at, :], wo_s[cols:, :])
        normed, scale = norm_parts(mixed)
        low = (normed * gain).astype(BF16)
        live = col_ref[at, 0:1] >= 0
        cot = cot_ref[at, :]
        grad_low = jnp.where(live, cot, jnp.zeros_like(cot))
        b_s[at, :] = low
        g_s[at, :] = grad_low
        up = dot_t(low, wi_s[0:both, :])
        gate = dot_t(low, wi_s[both:, :])
        cdf = 0.5 * (1.0 + lax.erf(up * (1.0 / math.sqrt(2.0))))
        act = up * cdf
        hid = (act * gate).astype(BF16)
        slope = cdf + up * (jnp.exp(-0.5 * up * up) * (1.0 / math.sqrt(2.0 * math.pi)))
        grad_hid = dot_t(grad_low, wd_s[...])
        grad_up = (grad_hid * gate * slope).astype(BF16)
        grad_gate = (grad_hid * act).astype(BF16)
        out_ref[at, :] = (mixed + dot(hid, wd_s[...])).astype(BF16)
        grad_b = dot(grad_up, wi_s[0:both, :]) + dot(grad_gate, wi_s[both:, :])
        hid_s[at, :] = hid
        gu_s[at, :] = grad_up
        gg_s[at, :] = grad_gate
        gain_grad = gain_grad + jnp.sum(grad_b * normed, axis=0, keepdims=True)
        scaled = grad_b * gain
        grad_mixed = grad_low.astype(F32) + scale * (
            scaled
            - jnp.mean(scaled, axis=-1, keepdims=True)
            - normed * jnp.mean(scaled * normed, axis=-1, keepdims=True)
        )
        gm_ref[at, :] = grad_mixed
        grad_mixed_low = grad_mixed.astype(BF16)
        gml_s[at, :] = grad_mixed_low
        gao_ref[at, :] = dot_t(grad_mixed_low, wo_s[0:cols, :]).astype(BF16)
        gax_ref[at, :] = dot_t(grad_mixed_low, wo_s[cols:, :]).astype(BF16)
    gain_grad_ref[...] = jnp.broadcast_to(gain_grad, gain_grad_ref.shape)
    half = width // 2
    core = place_ref[CORE]
    for a_ref, which in ((as_ref, 1 - core), (ak_ref, core)):
        low = b_s[:, pl.ds(aligned(which * half, LANES), half)]
        for row, src in ((0, gu_s), (units, gg_s)):
            grad = t_dot(src[...], low).astype(BF16)
            for side in range(2):
                for quarter in range(2):
                    at = side_block(which, side, row // n_i + quarter) * n_i
                    begin = side * units + quarter * n_i
                    a_ref[pl.ds(aligned(at, 16), n_i), :] = grad[begin : begin + n_i]


def outer_kernel(place_ref, atto_ref, attx_ref, hid_ref, g_ref, gml_ref, bk_ref, bs_ref):
    half = g_ref.shape[1] // 2
    units, cols = hid_ref.shape[1] // 2, atto_ref.shape[1]
    n_d, n_o = units // 4, cols // 4
    n_b = n_d + n_o
    core = place_ref[CORE]
    for b_ref, which in ((bs_ref, 1 - core), (bk_ref, core)):
        part = pl.ds(aligned(which * half, LANES), half)
        grad = t_dot(hid_ref[...], g_ref[:, part]).astype(BF16)
        grad_mixed_low = gml_ref[:, part]
        for side, att_ref in enumerate((atto_ref, attx_ref)):
            grad_o = t_dot(att_ref[...], grad_mixed_low).astype(BF16)
            for quarter in range(4):
                to = side_block(which, side, quarter) * n_b
                begin = side * units + quarter * n_d
                b_ref[pl.ds(aligned(to, 16), n_d), :] = grad[begin : begin + n_d]
                b_ref[pl.ds(aligned(to + n_d, 16), n_o), :] = grad_o[quarter * n_o : (quarter + 1) * n_o]


def outer(place, att_own, att_other, hid, g, gml):
    rows, width = g.shape
    size = hid.shape[1] + 2 * att_own.shape[1]
    return pl.pallas_call(
        outer_kernel,
        out_shape=(jax.ShapeDtypeStruct((size, width // 2), BF16),) * 2,
        in_specs=[SSPEC] + [VSPEC] * 5,
        out_specs=[VSPEC] * 2,
        compiler_params=params(),
        cost_estimate=cost(True),
        name="outer",
    )(place, att_own, att_other, hid, g, gml)


def middle(place, x, att_own, att_other, cot, col, gain, wo, wi, wd, pieces):
    rows, width = x.shape
    units, cols = wd.shape[0], wo.shape[0]
    size = 2 * cols * width + 6 * units * width
    half = width // 2
    return pl.pallas_call(
        middle_kernel,
        out_shape=(
            jax.ShapeDtypeStruct((rows, width), BF16),
            jax.ShapeDtypeStruct((rows, width), F32),
            jax.ShapeDtypeStruct((rows, cols), BF16),
            jax.ShapeDtypeStruct((rows, cols), BF16),
            jax.ShapeDtypeStruct((4 * units, half), BF16),
            jax.ShapeDtypeStruct((4 * units, half), BF16),
            jax.ShapeDtypeStruct((8, width), F32),
            jax.ShapeDtypeStruct((rows, width), BF16),
            jax.ShapeDtypeStruct((rows, width), BF16),
            jax.ShapeDtypeStruct((rows, 2 * units), BF16),
        ),
        in_specs=[SSPEC] + [VSPEC] * 15,
        out_specs=[VSPEC] * 10,
        scratch_shapes=[
            pltpu.VMEM((4 * units, width), BF16),
            pltpu.VMEM((2 * units, width), BF16),
            pltpu.VMEM((2 * cols, width), BF16),
            pltpu.VMEM((rows, width), BF16),
            pltpu.VMEM((rows, 2 * units), BF16),
            pltpu.VMEM((rows, 2 * units), BF16),
        ],
        compiler_params=params(34),
        cost_estimate=cost(True),
        name="middle",
    )(place, x, att_own, att_other, cot, col, gain, wo, wi, wd, *pieces)


def qkv_grads(place_ref, x_ref, gain_ref, gq_ref, dk_ref, dv_ref, recv_ref, cos_ref, sin_ref,
              keep_ref, send_ref, gk_ref, gv_ref, low_s):
    rows, width = x_ref.shape
    cols = gq_ref.shape[1]
    tile = min(256, rows)
    for begin in range(0, rows, tile):
        at = pl.ds(begin, tile)
        normed, _ = norm_parts(x_ref[at, :].astype(F32))
        low_s[at, :] = (normed * gain_ref[...]).astype(BF16)
        cosine, sine = cos_ref[at, :], sin_ref[at, :]
        for col in range(0, cols, LANES):
            part = slice(col, col + LANES)
            grad_k = dk_ref[at, part] + recv_ref[0, at, part].astype(F32)
            gk_ref[at, part] = (grad_k * cosine - swap_halves(grad_k) * sine).astype(BF16)
        gv_ref[at, :] = (dv_ref[at, :] + recv_ref[1, at, :].astype(F32)).astype(BF16)
    half = width // 2
    size = half // 4
    core = place_ref[CORE]
    for to_ref, which in ((send_ref, 1 - core), (keep_ref, core)):
        low = low_s[:, pl.ds(aligned(which * half, LANES), half)]
        for item, src in enumerate((gq_ref, gk_ref, gv_ref)):
            grad = t_dot(low, src[...]).astype(BF16)
            for quarter in range(4):
                to = (quarter * 3 + item) * size
                to_ref[to : to + size, :] = grad[quarter * size : (quarter + 1) * size]


def project_grads(place, x, gain, gq, dk, dv, received, cosine, sine, after=()):
    rows, width = x.shape
    cols = gq.shape[1]
    operands = [x, gain, gq, dk, dv, received, cosine, sine]
    return pl.pallas_call(
        functools.partial(ordered, qkv_grads, len(after)),
        out_shape=(jax.ShapeDtypeStruct((3 * width // 2, cols), BF16),) * 2
        + (jax.ShapeDtypeStruct((rows, cols), BF16),) * 2,
        in_specs=[ANYSPEC] * len(after) + [SSPEC] + [VSPEC] * len(operands),
        out_specs=[VSPEC] * 4,
        scratch_shapes=[pltpu.VMEM((rows, width), BF16)],
        compiler_params=params(24),
        cost_estimate=cost(True),
        name="project_grads",
    )(*after, place, *operands)


def project_back_kernel(
    place_ref, x_ref, gain_ref, gq_ref, dk_ref, dv_ref, recv_ref, cos_ref, sin_ref, w_ref,
    gqx_ref, gkx_ref, gvx_ref, w0, w1, w2, gm_ref, out_ref,
    keep_ref, send_ref, gx_ref, gain_grad_ref, low_s, gk_s, gv_s, wx_s,
):
    qkv_grads(place_ref, x_ref, gain_ref, gq_ref, dk_ref, dv_ref, recv_ref, cos_ref, sin_ref,
              keep_ref, send_ref, gk_s, gv_s, low_s)
    load_pieces(place_ref, (w0, w1, w2), wx_s)
    rows, width = x_ref.shape
    tile = min(256, rows)
    gain = gain_ref[...]
    gain_grad = jnp.zeros((1, width), F32)
    gx_ref[0:rows, :] = out_ref[...]
    for begin in range(0, rows, tile):
        at = pl.ds(begin, tile)
        normed, scale = norm_parts(x_ref[at, :].astype(F32))
        total = jnp.zeros((tile, width), F32)
        for item, (own, other) in enumerate(((gq_ref, gqx_ref), (gk_s, gkx_ref), (gv_s, gvx_ref))):
            part = slice(item * width, (item + 1) * width)
            total = total + dot_t(own[at, :], w_ref[part, :]) + dot_t(other[at, :], wx_s[part, :])
        gain_grad = gain_grad + jnp.sum(total * normed, axis=0, keepdims=True)
        scaled = total * gain
        gx_ref[pl.ds(rows + begin, tile), :] = (
            gm_ref[at, :]
            + scale
            * (
                scaled
                - jnp.mean(scaled, axis=-1, keepdims=True)
                - normed * jnp.mean(scaled * normed, axis=-1, keepdims=True)
            )
        ).astype(BF16)
    gain_grad_ref[...] = jnp.broadcast_to(gain_grad, gain_grad_ref.shape)


def project_back(place, x, gain, gq, dk, dv, received, cosine, sine, weight, others, pieces, grad_mixed, out, after):
    rows, width = x.shape
    cols = gq.shape[1]
    operands = [x, gain, gq, dk, dv, received, cosine, sine, weight, *others, *pieces, grad_mixed, out]
    return pl.pallas_call(
        functools.partial(ordered, project_back_kernel, len(after)),
        out_shape=(
            jax.ShapeDtypeStruct((3 * width // 2, cols), BF16),
            jax.ShapeDtypeStruct((3 * width // 2, cols), BF16),
            jax.ShapeDtypeStruct((2 * rows, width), BF16),
            jax.ShapeDtypeStruct((8, width), F32),
        ),
        in_specs=[ANYSPEC] * len(after) + [SSPEC] + [VSPEC] * len(operands),
        out_specs=[VSPEC] * 4,
        scratch_shapes=[
            pltpu.VMEM((rows, width), BF16),
            pltpu.VMEM((rows, cols), BF16),
            pltpu.VMEM((rows, cols), BF16),
            pltpu.VMEM((3 * width, cols), BF16),
        ],
        compiler_params=params(32),
        cost_estimate=cost(True),
        name="project_back",
    )(*after, place, *operands)


def pack(place, weights, after=(), entries=None):
    sizes = [value.shape[0] // 4 for value in weights]
    width = weights[0].shape[1]
    entries = entries or [PIECE] * len(weights)

    def spec(size, entry):
        return pl.BlockSpec((size, width), lambda _, at: (at[entry], 0))

    def kernel(place_ref, *refs):
        begin = 0
        for ref, size in zip(refs[len(after) :], sizes):
            refs[-1][begin : begin + size, :] = ref[...]
            begin += size

    return pl.pallas_call(
        kernel,
        grid_spec=pltpu.PrefetchScalarGridSpec(
            num_scalar_prefetch=1,
            grid=(1,),
            in_specs=[ANYSPEC] * len(after)
            + [spec(size, entry) for size, entry in zip(sizes, entries)],
            out_specs=pl.BlockSpec((sum(sizes), width), lambda _, at: (0, 0)),
        ),
        out_shape=jax.ShapeDtypeStruct((sum(sizes), width), BF16),
        compiler_params=params(semantics=("arbitrary",)),
        cost_estimate=cost(False),
        name="pack",
    )(place, *after, *weights)


def merge_kernel(jobs, after, place_ref, *refs):
    ins = list(refs[after : after + sum(job["count"] for job in jobs)])
    outs = list(refs[after + len(ins) :])
    for job in jobs:
        mine, ins = ins[: job["count"]], ins[job["count"] :]
        which = job["which"]
        if which is None:
            out_ref, outs = outs[0], outs[1:]
            out_ref[...] = sum(ref[...].astype(F32) for ref in mine).astype(out_ref.dtype)
            continue
        size = outs[0].shape[0]
        bit = place_ref[which]
        for out_ref, half in ((outs[0], 1 - bit), (outs[1], bit)):
            at = pl.ds(aligned(half * size, 16), size)
            total = sum(ref[at, :].astype(F32) for ref in (mine[:-2] if which == FIRST else mine))
            if which == FIRST:
                total = total + jnp.where(half == 0, mine[-2][...], mine[-1][...]).astype(F32)
            out_ref[...] = total.astype(BF16)
        outs = outs[2:]


def merge(place, *jobs, after=(), covers=True):
    arrays, shapes, notes = [], [], []
    for values, which in jobs:
        rows, cols = values[0].shape
        parts = 1 if which is None else 2
        shapes += [jax.ShapeDtypeStruct((rows // parts, cols), values[0].dtype)] * parts
        notes.append({"count": len(values), "which": which})
        arrays += values
    out = pl.pallas_call(
        functools.partial(merge_kernel, notes, len(after)),
        out_shape=tuple(shapes),
        in_specs=[SSPEC] + [ANYSPEC] * len(after) + [VSPEC] * len(arrays),
        out_specs=[VSPEC] * len(shapes),
        compiler_params=params(),
        cost_estimate=cost(covers),
        name="merge",
    )(place, *after, *arrays)
    return out


def join_kernel(counts, after, *refs):
    ins, outs = list(refs[after : after + sum(counts)]), refs[after + sum(counts) :]
    for count, out_ref in zip(counts, outs):
        size = out_ref.shape[0] // count
        for step in range(count):
            out_ref[step * size : (step + 1) * size, :] = ins[step][...]
        ins = ins[count:]


def join(*groups, after=(), covers=True):
    values = [value for group in groups for value in group]
    return pl.pallas_call(
        functools.partial(join_kernel, [len(group) for group in groups], len(after)),
        out_shape=tuple(
            jax.ShapeDtypeStruct((len(group) * group[0].shape[0], group[0].shape[1]), BF16) for group in groups
        ),
        in_specs=[ANYSPEC] * len(after) + [VSPEC] * len(values),
        out_specs=[VSPEC] * len(groups),
        compiler_params=params(),
        cost_estimate=cost(covers),
        name="join",
    )(*after, *values)


def split_kernel(both_ref, first_ref, second_ref):
    rows = first_ref.shape[0]
    first_ref[...] = both_ref[0:rows, :]
    second_ref[...] = both_ref[rows:, :]


def split(both):
    rows, width = both.shape[0] // 2, both.shape[1]
    return pl.pallas_call(
        split_kernel,
        out_shape=(jax.ShapeDtypeStruct((rows, width), both.dtype),) * 2,
        in_specs=[VSPEC],
        out_specs=[VSPEC] * 2,
        compiler_params=params(),
        cost_estimate=cost(False),
        name="split",
    )(both)


def assemble_kernel(kind, after, place_ref, *refs):
    pieces, outs = list(refs[after : after + 4]), refs[after + 5 : -1]
    refs[-1][...] = jnp.zeros(refs[-1].shape, F32)
    core = place_ref[CORE]
    size = pieces[0].shape[0]
    pieces += [refs[after + 4].at[step * size : (step + 1) * size] for step in range(4)]
    for step, piece in enumerate(pieces):
        mine = step < 4
        quarter = place_ref[MINE if mine else THEIRS] ^ (step % 4)
        side = core if mine else 1 - core
        if kind == "qkv":
            rows = size // 3
            for item in range(3):
                at = pl.ds(aligned((side * 4 + quarter) * rows, 8), rows)
                outs[0][item, at, :] = piece[item * rows : (item + 1) * rows, :].astype(F32)
            continue
        half = outs[0].shape[1] // 2
        part = pl.ds(aligned(side * half, LANES), half)
        begin = 0
        for out_ref in outs:
            rows = out_ref.shape[0] // 4
            at = pl.ds(aligned(quarter * rows, 8), rows)
            out_ref[at, part] = piece[begin : begin + rows, :].astype(F32)
            begin += rows


def assemble(kind, place, pieces, shapes, after=()):
    total = sum(math.prod(shape) for shape in shapes)
    return pl.pallas_call(
        functools.partial(assemble_kernel, kind, len(after)),
        out_shape=tuple(jax.ShapeDtypeStruct(shape, F32) for shape in [*shapes, (8, LANES)]),
        in_specs=[SSPEC] + [ANYSPEC] * len(after) + [VSPEC] * 5,
        out_specs=[VSPEC] * (len(shapes) + 1),
        compiler_params=params(),
        cost_estimate=cost(True),
        name="assemble",
    )(place, *after, *pieces)


def per_device(
    axis_sizes,
    hidden,
    seq_ids,
    cotangent,
    qkv_weight,
    attn_out_weight,
    mlp_in_weight,
    mlp_out_weight,
    norm1_gain,
    norm2_gain,
):
    dp_size, tensor_size = axis_sizes
    devices = dp_size * tensor_size
    chips = devices // 4
    chip_bits = chips.bit_length() - 1
    rows, width = hidden.shape
    cols = qkv_weight.shape[2]
    units = mlp_out_weight.shape[0]
    dp_at = lax.axis_index("dp")
    core = dp_at % 2
    chip = dp_at // 2

    def move(value, target):
        return lax.ppermute(value, ("dp", "tensor"), [(i, target(i)) for i in range(devices)])

    def swapped(i):
        return (i & ~3) | ((i & 1) << 1) | ((i >> 1) & 1)

    def to_tensor(i):
        return i ^ 1

    def to_core(i):
        return i ^ 2

    def to_near(i):
        return i ^ 4

    def to_next(i):
        return i ^ 8

    def masked(first, second):
        return lambda i: i ^ (second if i & 2 else first)

    near, next_near = chip % 2, (chip // 2) % 2
    quarters = [near * 2 + next_near, next_near * 2 + near]
    place = jnp.stack(
        [
            core,
            near * 2 + core,
            next_near * 2 + core,
            jnp.where(core == 0, quarters[0], quarters[1]),
            jnp.where(core == 0, quarters[1], quarters[0]),
            jnp.where(core == 0, 0, next_near),
            jnp.where(core == 0, near, 0),
            jnp.where(core == 0, next_near, near),
            jnp.where(core == 0, near, next_near),
            jnp.where(core == 0, next_near, near),
        ]
    ).astype(jnp.int32)

    x = move(hidden, swapped)
    ids = jnp.where(core == lax.axis_index("tensor"), seq_ids, move(seq_ids, to_core))
    ids_own = lax.dynamic_slice_in_dim(ids, core * rows, rows)
    ids_other = lax.dynamic_slice_in_dim(ids, (1 - core) * rows, rows)

    index = jnp.arange(ids.shape[0], dtype=jnp.int32)
    begins = jnp.zeros((rows,), jnp.int32)
    for number in (-1, 0, 1, 2):
        start = jnp.min(jnp.where(ids == number, index, ids.shape[0]))
        begins = jnp.where(ids_own == number, start, begins)
    pos = core * rows + jnp.arange(rows, dtype=jnp.int32) - begins
    frequency = jnp.power(ROPE_BASE, -2.0 * jnp.arange(HDIM // 2, dtype=F32) / HDIM)
    angles = pos.astype(F32)[:, None] * frequency[None, :]
    cosine, sine = jnp.cos(angles), jnp.sin(angles)
    cosine = jnp.concatenate([cosine] * 4, axis=1)
    sine = jnp.concatenate([-sine, sine] * 2, axis=1)
    col_own = jnp.broadcast_to(ids_own[:, None], (rows, LANES))
    col_other = jnp.broadcast_to(ids_other[:, None], (rows, LANES))
    row_own = jnp.broadcast_to(ids_own[None, :], (8, rows))
    row_other = jnp.broadcast_to(ids_other[None, :], (8, rows))

    w_qkv = qkv_weight.reshape(3 * width, cols)
    w_in = jnp.swapaxes(mlp_in_weight, 1, 2).reshape(2 * units, width)
    w_qkv_part = pack(place, [w_qkv])
    w_qkv_one = move(w_qkv_part, to_tensor)
    w_part = pack(
        place, [w_in, mlp_out_weight, attn_out_weight], [w_qkv_one], entries=[PIECE, PIECE_NEXT, PIECE_NEXT]
    )
    w_one = move(w_part, to_tensor)
    cot = move(cotangent, swapped)
    gain1, gain2 = norm1_gain[None, :], norm2_gain[None, :]

    (sent,) = join([w_qkv_one], covers=False)
    w_qkv_two = move(sent, to_near)
    q_a, *kv_a = project(place, x, gain1, [w_qkv], cosine, sine, after=[sent])
    kv_a_x = [move(value, to_core) for value in kv_a]
    o_a, lse_a = attend(q_a, kv_a, kv_a_x, col_own, row_own, row_other)
    sent, both = join([w_one], [w_qkv_one, w_qkv_two], after=[o_a], covers=False)
    in_rows = w_in.shape[0] // 4
    w_in_two, w_rest_two = move(sent[:in_rows], to_near), move(sent[in_rows:], to_next)
    w_qkv_x = [w_qkv_one, w_qkv_two, move(both, to_core)]
    q_b, *kv_b = project(place, x, gain1, w_qkv_x, cosine, sine, after=[sent])
    kv_b_x = [move(value, to_core) for value in kv_b]
    o_b, lse_b = attend(q_b, kv_b, kv_b_x, col_own, row_own, row_other)
    in_sent, rest_sent = join([w_in_two], [w_rest_two], after=[o_b], covers=False)
    w_x = [w_one, w_in_two, w_rest_two] + [move(value, to_core) for value in (w_one, in_sent, rest_sent)]
    out, grad_mixed, go_a, go_b, in_keep, in_send, gain2_part, grad_low, grad_mixed_low, hid = middle(
        place, x, o_a, o_b, cot, col_own, gain2, attn_out_weight, w_in, mlp_out_weight, w_x
    )
    rest_keep, rest_send = outer(place, o_a, o_b, hid, grad_low, grad_mixed_low)

    plain = range(2, chip_bits)

    def spread(total, after=()):
        one = move(total, masked(8, 4))
        two = move(total, masked(4, 8))
        mine = [total, one, two, move(one, masked(4, 8))]
        return mine + [move(join(mine, after=after)[0], to_core)]

    def back(q, kv, kv_x, go, o, lse, after):
        gq, dk, dv, dx = attend_back(q, kv, kv_x, go, o, lse, col_own, col_other, row_own, cosine, sine, after)
        return gq, dk, dv, move(dx, to_core)

    def pair(value, mask):
        return [value, move(value, masked(mask, mask))]

    target_1, target_2, target_3 = masked(1, 8), masked(4, 1), masked(8, 4)
    in_got = move(in_send, to_core)
    rest_got = move(rest_send, to_core)
    in_sent, in_kept = merge(place, ([in_keep, in_got], ONE))
    gq_b, dk_b, dv_b, recv_b = back(q_b, kv_b, kv_b_x, go_b, o_b, lse_b, [in_sent])
    in_got = move(in_sent, target_1)
    in_sent, in_kept, rest_sent, rest_kept = merge(
        place, ([in_kept, in_got], TWO), ([rest_keep, rest_got], ONE), after=[gq_b]
    )
    keep_b, send_b, gk_b, gv_b = project_grads(place, x, gain1, gq_b, dk_b, dv_b, recv_b, cosine, sine, [in_sent])
    (qkv_sum,) = merge(place, ([keep_b, move(send_b, to_core)], None), covers=False)
    half = qkv_sum.shape[0] // 2
    low_got = move(qkv_sum[:half], to_tensor)
    gq_a, dk_a, dv_a, recv_a = back(q_a, kv_a, kv_a_x, go_a, o_a, lse_a, [qkv_sum])
    in_got = move(in_sent, target_2)
    rest_got = move(rest_sent, target_1)
    in_sent, in_kept, rest_sent, rest_kept = merge(
        place, ([in_kept, in_got], THREE), ([rest_kept, rest_got], TWO), after=[gq_a, low_got]
    )
    in_got = move(in_sent, target_3)
    rest_got = move(rest_sent, target_2)
    high_got = move(qkv_sum[half:], to_tensor)
    keep_a, send_a, results, gain1_part = project_back(
        place, x, gain1, gq_a, dk_a, dv_a, recv_a, cosine, sine, w_qkv, [gq_b, gk_b, gv_b], w_qkv_x, grad_mixed,
        out, [in_sent],
    )
    in_total, rest_sent, rest_kept = merge(
        place, ([in_kept, in_got], None), ([rest_kept, rest_got], THREE), after=[keep_a, high_got]
    )
    rest_got = move(rest_sent, target_3)
    results = move(results, swapped)
    gains = jnp.concatenate([gain1_part, gain2_part])
    sent, kept, gains = merge(
        place,
        ([keep_a, move(send_a, to_core), low_got, high_got], FIRST),
        (pair(gains, 2), None),
        after=[in_total],
    )
    sent, kept, gains, rest_total = merge(
        place,
        ([kept, move(sent, masked(4, 8))], SECOND),
        (pair(gains, 4), None),
        ([rest_kept, rest_got], None),
    )
    for b in plain:
        (in_total,) = merge(place, (pair(in_total, 4 << b), None), after=[sent])
    in_pieces = spread(in_total)
    qkv_total, gains = merge(
        place, ([kept, move(sent, masked(8, 4))], None), (pair(gains, 8), None), after=[in_total]
    )
    for b in plain:
        (rest_total,) = merge(place, (pair(rest_total, 4 << b), None), after=[qkv_total])
    rest_pieces = spread(rest_total)
    g_in, in_done = assemble("in", place, in_pieces, [(2 * units, width)])
    out, input_grad = split(results)
    for b in plain:
        qkv_total, gains = merge(
            place, (pair(qkv_total, 4 << b), None), (pair(gains, 4 << b), None), after=[input_grad, in_pieces[3]]
        )
    qkv_pieces = spread(qkv_total, [in_done])
    gains = sum(pair(gains, 1))
    g_down, g_out, _ = assemble("rest", place, rest_pieces, [(units, width), (cols, width)], after=[qkv_total])
    g_qkv, _ = assemble("qkv", place, qkv_pieces, [(3, width, cols)])
    return (
        out,
        input_grad,
        gains[0],
        gains[8],
        g_qkv,
        g_out,
        jnp.swapaxes(g_in.reshape(2, units, width), 1, 2),
        g_down,
    )


def solution(mesh):
    in_specs = (
        P(("dp", "tensor"), None),
        P("dp"),
        P(("dp", "tensor"), None),
        P(None, None, "tensor"),
        P("tensor", None),
        P(None, None, "tensor"),
        P("tensor", None),
        P(),
        P(),
    )
    out_specs = (
        P(("dp", "tensor"), None),
        P(("dp", "tensor"), None),
        P(),
        P(),
        P(None, None, "tensor"),
        P("tensor", None),
        P(None, None, "tensor"),
        P("tensor", None),
    )
    return jax.shard_map(
        functools.partial(per_device, (mesh.shape["dp"], mesh.shape["tensor"])),
        mesh=mesh,
        in_specs=in_specs,
        out_specs=out_specs,
        check_vma=False,
    )
```

```python
import functools
import math

import jax
import jax.numpy as jnp
from jax import lax
from jax.experimental import pallas as pl
from jax.experimental.pallas import tpu as pltpu
from jax.sharding import PartitionSpec as P

HDIM = 64
LANES = 128
EPSILON = 1e-05
ROPE_BASE = 160000.0
MASKED = -1e30
F32 = jnp.float32
BF16 = jnp.bfloat16
MIB = 1024 * 1024


def dot(left, right):
    return jnp.dot(left, right, preferred_element_type=F32)


def dot_t(left, right):
    return lax.dot_general(left, right, (((1,), (1,)), ((), ())), preferred_element_type=F32)


def t_dot(left, right):
    return lax.dot_general(left, right, (((0,), (0,)), ((), ())), preferred_element_type=F32)


def norm_parts(values):
    center = values - jnp.mean(values, axis=-1, keepdims=True)
    spread = jnp.mean(center * center, axis=-1, keepdims=True)
    scale = lax.rsqrt(spread + EPSILON)
    return center * scale, scale


def swap_halves(values):
    lane = lax.broadcasted_iota(jnp.int32, values.shape, 1) % HDIM
    return jnp.where(
        lane < HDIM // 2,
        pltpu.roll(values, LANES - HDIM // 2, 1),
        pltpu.roll(values, HDIM // 2, 1),
    )


def low_lanes(shape):
    return lax.broadcasted_iota(jnp.int32, shape, 1) < HDIM


def cost(covers):
    return pl.CostEstimate(flops=20_000_000_000 if covers else 1_000, bytes_accessed=1_024, transcendentals=0)


def params(mib=20, semantics=None):
    return pltpu.CompilerParams(vmem_limit_bytes=mib * MIB, dimension_semantics=semantics)


VSPEC = pl.BlockSpec(memory_space=pltpu.VMEM)
SSPEC = pl.BlockSpec(memory_space=pltpu.SMEM)
ANYSPEC = pl.BlockSpec(memory_space=pl.ANY)
CORE, PIECE, PIECE_NEXT, MINE, THEIRS, ONE, TWO, THREE, FIRST, SECOND = range(10)


def aligned(value, by):
    return pl.multiple_of(value, by)


def side_block(core, side, quarter):
    return jnp.where(core == 0, side * 4 + quarter, (quarter // 2) * 4 + side * 2 + quarter % 2)


def ordered(kernel, count, *refs):
    kernel(*refs[count:])


def quarters_of(place_ref, pieces):
    one, two, others = pieces
    size = one.shape[0]
    for step, piece in ((0, one), (2, two), (1, others.at[0:size]), (3, others.at[size : 2 * size])):
        yield place_ref[PIECE] ^ step, piece


def load_pieces(place_ref, pieces, w_s):
    size = pieces[0].shape[0]
    for at, piece in quarters_of(place_ref, pieces):
        w_s[pl.ds(aligned(at * size, 16), size), :] = piece[...]


def project_kernel(gathered, *refs):
    if gathered:
        place_ref, x_ref, gain_ref, w0, w1, w2, cos_ref, sin_ref, q_ref, k_ref, v_ref, w_ref = refs
        load_pieces(place_ref, (w0, w1, w2), w_ref)
    else:
        place_ref, x_ref, gain_ref, w_ref, cos_ref, sin_ref, q_ref, k_ref, v_ref = refs
    rows, width = x_ref.shape
    cols = q_ref.shape[1]
    tile = min(256, rows)
    for begin in range(0, rows, tile):
        at = pl.ds(begin, tile)
        normed, _ = norm_parts(x_ref[at, :].astype(F32))
        low = (normed * gain_ref[...]).astype(BF16)
        cosine, sine = cos_ref[at, :], sin_ref[at, :]
        q_raw = dot(low, w_ref[0:width, :])
        k_raw = dot(low, w_ref[width : 2 * width, :])
        v_ref[at, :] = dot(low, w_ref[2 * width : 3 * width, :]).astype(BF16)
        for col in range(0, cols, LANES):
            part = slice(col, col + LANES)
            q_part, k_part = q_raw[:, part], k_raw[:, part]
            q_ref[at, part] = (
                (q_part * cosine + swap_halves(q_part) * sine).astype(BF16) * (1.0 / math.sqrt(HDIM))
            ).astype(BF16)
            k_ref[at, part] = (k_part * cosine + swap_halves(k_part) * sine).astype(BF16)


def project(place, x, gain, weights, cosine, sine, after=()):
    rows, width = x.shape
    cols = weights[0].shape[1]
    gathered = len(weights) > 1
    operands = [place, x, gain, *weights, cosine, sine]
    return pl.pallas_call(
        functools.partial(ordered, functools.partial(project_kernel, gathered), len(after)),
        out_shape=(
            jax.ShapeDtypeStruct((rows, cols), BF16),
            jax.ShapeDtypeStruct((rows, cols), BF16),
            jax.ShapeDtypeStruct((rows, cols), BF16),
        ),
        in_specs=[ANYSPEC] * len(after) + [SSPEC] + [VSPEC] * (len(operands) - 1),
        out_specs=[VSPEC] * 3,
        scratch_shapes=[pltpu.VMEM((3 * width, cols), BF16)] if gathered else [],
        compiler_params=params(),
        cost_estimate=cost(gathered),
        name="project",
    )(*after, *operands)


def attend_kernel(q_ref, ko_ref, vo_ref, kx_ref, vx_ref, col_ref, row_ref, rowx_ref, o_ref, lse_ref, bo_ref, bx_ref):
    rows = q_ref.shape[0]
    tile = min(256, rows)

    @pl.when(pl.program_id(0) == 0)
    def _():
        col = col_ref[...][:, 0:1]
        bo_ref[...] = jnp.where(col == row_ref[0:1, :], 0.0, MASKED)
        bx_ref[...] = jnp.where(col == rowx_ref[0:1, :], 0.0, MASKED)

    for begin in range(0, rows, tile):
        at = pl.ds(begin, tile)
        low = low_lanes((tile, LANES))
        q_pair = q_ref[at, :]
        results, logs = [], []
        for head in range(2):
            chosen = low if head == 0 else jnp.logical_not(low)
            query = jnp.where(chosen, q_pair, jnp.zeros_like(q_pair))
            own = dot_t(query, ko_ref[...]) + bo_ref[at, :]
            other = dot_t(query, kx_ref[...]) + bx_ref[at, :]
            highest = jnp.maximum(
                jnp.max(own, axis=-1, keepdims=True), jnp.max(other, axis=-1, keepdims=True)
            )
            own = jnp.exp(own - highest)
            other = jnp.exp(other - highest)
            totals = jnp.sum(own, axis=-1, keepdims=True) + jnp.sum(other, axis=-1, keepdims=True)
            value = dot(own.astype(BF16), vo_ref[...]) + dot(other.astype(BF16), vx_ref[...])
            results.append(value / totals)
            logs.append(highest + jnp.log(totals))
        o_ref[at, :] = jnp.where(low, results[0], results[1]).astype(BF16)
        lse_ref[at, :] = jnp.where(low, logs[0], logs[1])


def attend(q, kv_own, kv_other, col, row, row_other, after=()):
    rows, cols = q.shape
    pairs = cols // LANES
    tok = pl.BlockSpec((rows, LANES), lambda p: (0, p))
    return pl.pallas_call(
        functools.partial(ordered, attend_kernel, len(after)),
        grid=(pairs,),
        out_shape=(
            jax.ShapeDtypeStruct((rows, cols), BF16),
            jax.ShapeDtypeStruct((rows, cols), F32),
        ),
        in_specs=[ANYSPEC] * len(after)
        + [
            tok,
            tok,
            tok,
            tok,
            tok,
            pl.BlockSpec((rows, LANES), lambda p: (0, 0)),
            pl.BlockSpec((8, rows), lambda p: (0, 0)),
            pl.BlockSpec((8, rows), lambda p: (0, 0)),
        ],
        out_specs=[tok, tok],
        scratch_shapes=[pltpu.VMEM((rows, rows), F32), pltpu.VMEM((rows, rows), F32)],
        compiler_params=params(semantics=("arbitrary",)),
        cost_estimate=cost(False),
        name="attend",
    )(*after, q, *kv_own, *kv_other, col, row, row_other)


def attend_back_kernel(
    q_ref, ko_ref, vo_ref, kx_ref, vx_ref, do_ref, o_ref, lse_ref, col_ref, colx_ref, row_ref, cos_ref, sin_ref,
    gq_ref, dko_ref, dvo_ref, dx_ref, bo_ref, bx_ref,
):
    rows = q_ref.shape[0]
    tile = min(256, rows)

    @pl.when(pl.program_id(0) == 0)
    def _():
        row = row_ref[0:1, :]
        bo_ref[...] = jnp.where(col_ref[...][:, 0:1] == row, 0.0, MASKED)
        bx_ref[...] = jnp.where(colx_ref[...][:, 0:1] == row, 0.0, MASKED)

    low = low_lanes((rows, LANES))
    q_pair, do_pair = q_ref[...], do_ref[...]
    product = do_pair.astype(F32) * o_ref[...].astype(F32)
    first = jnp.sum(jnp.where(low, product, 0.0), axis=-1, keepdims=True)
    second = jnp.sum(jnp.where(low, 0.0, product), axis=-1, keepdims=True)
    delta_t = jnp.transpose(jnp.where(low, first, second))
    lse_t = jnp.transpose(lse_ref[...])
    low_tile = low_lanes((tile, LANES))
    grad_q = jnp.zeros((rows, LANES), F32)
    for k_ref, v_ref, bias_ref, dk_ref, dv_ref in (
        (ko_ref, vo_ref, bo_ref, dko_ref, dvo_ref),
        (kx_ref, vx_ref, bx_ref, dx_ref.at[0], dx_ref.at[1]),
    ):
        for begin in range(0, rows, tile):
            at = pl.ds(begin, tile)
            k_pair, v_pair = k_ref[at, :], v_ref[at, :]
            grad_k = grad_v = None
            for head in range(2):
                chosen = low_tile if head == 0 else jnp.logical_not(low_tile)
                chosen_q = low if head == 0 else jnp.logical_not(low)
                key = jnp.where(chosen, k_pair, jnp.zeros_like(k_pair))
                value = jnp.where(chosen, v_pair, jnp.zeros_like(v_pair))
                query = jnp.where(chosen_q, q_pair, jnp.zeros_like(q_pair))
                grad_o = jnp.where(chosen_q, do_pair, jnp.zeros_like(do_pair))
                at_row = head * HDIM
                scores = dot_t(key, q_pair) + bias_ref[at, :]
                probs = jnp.exp(scores - lse_t[at_row : at_row + 1, :])
                grad_probs = dot_t(value, do_pair)
                grad_scores = (probs * (grad_probs - delta_t[at_row : at_row + 1, :])).astype(BF16)
                term_v = dot(probs.astype(BF16), grad_o)
                term_k = dot(grad_scores, query)
                grad_v = term_v if grad_v is None else grad_v + term_v
                grad_k = term_k if grad_k is None else grad_k + term_k
                grad_q = grad_q + t_dot(grad_scores, key)
            dk_ref[at, :] = grad_k.astype(dk_ref.dtype)
            dv_ref[at, :] = grad_v.astype(dv_ref.dtype)
    grad_q = grad_q * (1.0 / math.sqrt(HDIM))
    gq_ref[...] = (grad_q * cos_ref[...] - swap_halves(grad_q) * sin_ref[...]).astype(BF16)


def attend_back(q, kv_own, kv_other, grad_o, o, lse, col, col_other, row, cosine, sine, after=()):
    rows, cols = q.shape
    pairs = cols // LANES
    tok = pl.BlockSpec((rows, LANES), lambda p: (0, p))
    fixed = pl.BlockSpec((rows, LANES), lambda p: (0, 0))
    return pl.pallas_call(
        functools.partial(ordered, attend_back_kernel, len(after)),
        grid=(pairs,),
        out_shape=(
            jax.ShapeDtypeStruct((rows, cols), BF16),
            jax.ShapeDtypeStruct((rows, cols), F32),
            jax.ShapeDtypeStruct((rows, cols), F32),
            jax.ShapeDtypeStruct((2, rows, cols), BF16),
        ),
        in_specs=[ANYSPEC] * len(after)
        + [
            tok, tok, tok, tok, tok, tok, tok, tok, fixed, fixed,
            pl.BlockSpec((8, rows), lambda p: (0, 0)), fixed, fixed,
        ],
        out_specs=[tok] * 3 + [pl.BlockSpec((2, rows, LANES), lambda p: (0, 0, p))],
        scratch_shapes=[pltpu.VMEM((rows, rows), F32), pltpu.VMEM((rows, rows), F32)],
        compiler_params=params(semantics=("arbitrary",)),
        cost_estimate=cost(True),
        name="attend_back",
    )(*after, q, *kv_own, *kv_other, grad_o, o, lse, col, col_other, row, cosine, sine)


def middle_kernel(
    place_ref, x_ref, atto_ref, attx_ref, cot_ref, col_ref, gain_ref, wo_ref, wi_ref, wd_ref,
    p0, p1i, p1r, p2, p3i, p3r,
    out_ref, gm_ref, gao_ref, gax_ref, ak_ref, as_ref, gain_grad_ref, g_s, gml_s, hid_s,
    wi_s, wd_s, wo_s, b_s, gu_s, gg_s,
):
    rows, width = x_ref.shape
    units, cols = wd_ref.shape[0], wo_ref.shape[0]
    both = 2 * units
    wi_s[0:units, :] = wi_ref[0:units, :]
    wi_s[both : both + units, :] = wi_ref[units:both, :]
    wd_s[0:units, :] = wd_ref[...]
    wo_s[0:cols, :] = wo_ref[...]
    n_i, n_d, n_o = both // 4, units // 4, cols // 4
    n_r = n_d + n_o
    cut = (p0.at[0:n_i], p1i, p2.at[0:n_i], p3i)
    rest = (p0.at[n_i : n_i + n_r], p1r, p2.at[n_i : n_i + n_r], p3r)
    for step, piece_i, piece in zip((0, 2, 1, 3), cut, rest):
        at = place_ref[PIECE] ^ step
        to_i = units + (at % 2) * n_i + (at // 2) * both
        wi_s[pl.ds(aligned(to_i, 16), n_i), :] = piece_i[...]
        at = place_ref[PIECE_NEXT] ^ step
        wd_s[pl.ds(aligned(units + at * n_d, 16), n_d), :] = piece[0:n_d, :]
        wo_s[pl.ds(aligned(cols + at * n_o, 16), n_o), :] = piece[n_d:, :]
    tile = min(256, rows)
    gain = gain_ref[...]
    gain_grad = jnp.zeros((1, width), F32)
    for begin in range(0, rows, tile):
        at = pl.ds(begin, tile)
        mixed = x_ref[at, :].astype(F32) + dot(atto_ref[at, :], wo_s[0:cols, :]) + dot(attx_ref[at, :], wo_s[cols:, :])
        normed, scale = norm_parts(mixed)
        low = (normed * gain).astype(BF16)
        live = col_ref[at, 0:1] >= 0
        cot = cot_ref[at, :]
        grad_low = jnp.where(live, cot, jnp.zeros_like(cot))
        b_s[at, :] = low
        g_s[at, :] = grad_low
        up = dot_t(low, wi_s[0:both, :])
        gate = dot_t(low, wi_s[both:, :])
        cdf = 0.5 * (1.0 + lax.erf(up * (1.0 / math.sqrt(2.0))))
        act = up * cdf
        hid = (act * gate).astype(BF16)
        slope = cdf + up * (jnp.exp(-0.5 * up * up) * (1.0 / math.sqrt(2.0 * math.pi)))
        grad_hid = dot_t(grad_low, wd_s[...])
        grad_up = (grad_hid * gate * slope).astype(BF16)
        grad_gate = (grad_hid * act).astype(BF16)
        out_ref[at, :] = (mixed + dot(hid, wd_s[...])).astype(BF16)
        grad_b = dot(grad_up, wi_s[0:both, :]) + dot(grad_gate, wi_s[both:, :])
        hid_s[at, :] = hid
        gu_s[at, :] = grad_up
        gg_s[at, :] = grad_gate
        gain_grad = gain_grad + jnp.sum(grad_b * normed, axis=0, keepdims=True)
        scaled = grad_b * gain
        grad_mixed = grad_low.astype(F32) + scale * (
            scaled
            - jnp.mean(scaled, axis=-1, keepdims=True)
            - normed * jnp.mean(scaled * normed, axis=-1, keepdims=True)
        )
        gm_ref[at, :] = grad_mixed
        grad_mixed_low = grad_mixed.astype(BF16)
        gml_s[at, :] = grad_mixed_low
        gao_ref[at, :] = dot_t(grad_mixed_low, wo_s[0:cols, :]).astype(BF16)
        gax_ref[at, :] = dot_t(grad_mixed_low, wo_s[cols:, :]).astype(BF16)
    gain_grad_ref[...] = jnp.broadcast_to(gain_grad, gain_grad_ref.shape)
    half = width // 2
    core = place_ref[CORE]
    for a_ref, which in ((as_ref, 1 - core), (ak_ref, core)):
        low = b_s[:, pl.ds(aligned(which * half, LANES), half)]
        for row, src in ((0, gu_s), (units, gg_s)):
            grad = t_dot(src[...], low).astype(BF16)
            for side in range(2):
                for quarter in range(2):
                    at = side_block(which, side, row // n_i + quarter) * n_i
                    begin = side * units + quarter * n_i
                    a_ref[pl.ds(aligned(at, 16), n_i), :] = grad[begin : begin + n_i]


def outer_kernel(place_ref, atto_ref, attx_ref, hid_ref, g_ref, gml_ref, bk_ref, bs_ref):
    half = g_ref.shape[1] // 2
    units, cols = hid_ref.shape[1] // 2, atto_ref.shape[1]
    n_d, n_o = units // 4, cols // 4
    n_b = n_d + n_o
    core = place_ref[CORE]
    for b_ref, which in ((bs_ref, 1 - core), (bk_ref, core)):
        part = pl.ds(aligned(which * half, LANES), half)
        grad = t_dot(hid_ref[...], g_ref[:, part]).astype(BF16)
        grad_mixed_low = gml_ref[:, part]
        for side, att_ref in enumerate((atto_ref, attx_ref)):
            grad_o = t_dot(att_ref[...], grad_mixed_low).astype(BF16)
            for quarter in range(4):
                to = side_block(which, side, quarter) * n_b
                begin = side * units + quarter * n_d
                b_ref[pl.ds(aligned(to, 16), n_d), :] = grad[begin : begin + n_d]
                b_ref[pl.ds(aligned(to + n_d, 16), n_o), :] = grad_o[quarter * n_o : (quarter + 1) * n_o]


def outer(place, att_own, att_other, hid, g, gml):
    rows, width = g.shape
    size = hid.shape[1] + 2 * att_own.shape[1]
    return pl.pallas_call(
        outer_kernel,
        out_shape=(jax.ShapeDtypeStruct((size, width // 2), BF16),) * 2,
        in_specs=[SSPEC] + [VSPEC] * 5,
        out_specs=[VSPEC] * 2,
        compiler_params=params(),
        cost_estimate=cost(True),
        name="outer",
    )(place, att_own, att_other, hid, g, gml)


def middle(place, x, att_own, att_other, cot, col, gain, wo, wi, wd, pieces):
    rows, width = x.shape
    units, cols = wd.shape[0], wo.shape[0]
    size = 2 * cols * width + 6 * units * width
    half = width // 2
    return pl.pallas_call(
        middle_kernel,
        out_shape=(
            jax.ShapeDtypeStruct((rows, width), BF16),
            jax.ShapeDtypeStruct((rows, width), F32),
            jax.ShapeDtypeStruct((rows, cols), BF16),
            jax.ShapeDtypeStruct((rows, cols), BF16),
            jax.ShapeDtypeStruct((4 * units, half), BF16),
            jax.ShapeDtypeStruct((4 * units, half), BF16),
            jax.ShapeDtypeStruct((8, width), F32),
            jax.ShapeDtypeStruct((rows, width), BF16),
            jax.ShapeDtypeStruct((rows, width), BF16),
            jax.ShapeDtypeStruct((rows, 2 * units), BF16),
        ),
        in_specs=[SSPEC] + [VSPEC] * 15,
        out_specs=[VSPEC] * 10,
        scratch_shapes=[
            pltpu.VMEM((4 * units, width), BF16),
            pltpu.VMEM((2 * units, width), BF16),
            pltpu.VMEM((2 * cols, width), BF16),
            pltpu.VMEM((rows, width), BF16),
            pltpu.VMEM((rows, 2 * units), BF16),
            pltpu.VMEM((rows, 2 * units), BF16),
        ],
        compiler_params=params(34),
        cost_estimate=cost(True),
        name="middle",
    )(place, x, att_own, att_other, cot, col, gain, wo, wi, wd, *pieces)


def qkv_grads(place_ref, x_ref, gain_ref, gq_ref, dk_ref, dv_ref, recv_ref, cos_ref, sin_ref,
              keep_ref, send_ref, gk_ref, gv_ref, low_s):
    rows, width = x_ref.shape
    cols = gq_ref.shape[1]
    tile = min(256, rows)
    for begin in range(0, rows, tile):
        at = pl.ds(begin, tile)
        normed, _ = norm_parts(x_ref[at, :].astype(F32))
        low_s[at, :] = (normed * gain_ref[...]).astype(BF16)
        cosine, sine = cos_ref[at, :], sin_ref[at, :]
        for col in range(0, cols, LANES):
            part = slice(col, col + LANES)
            grad_k = dk_ref[at, part] + recv_ref[0, at, part].astype(F32)
            gk_ref[at, part] = (grad_k * cosine - swap_halves(grad_k) * sine).astype(BF16)
        gv_ref[at, :] = (dv_ref[at, :] + recv_ref[1, at, :].astype(F32)).astype(BF16)
    half = width // 2
    size = half // 4
    core = place_ref[CORE]
    for to_ref, which in ((send_ref, 1 - core), (keep_ref, core)):
        low = low_s[:, pl.ds(aligned(which * half, LANES), half)]
        for item, src in enumerate((gq_ref, gk_ref, gv_ref)):
            grad = t_dot(low, src[...]).astype(BF16)
            for quarter in range(4):
                to = (quarter * 3 + item) * size
                to_ref[to : to + size, :] = grad[quarter * size : (quarter + 1) * size]


def project_grads(place, x, gain, gq, dk, dv, received, cosine, sine, after=()):
    rows, width = x.shape
    cols = gq.shape[1]
    operands = [x, gain, gq, dk, dv, received, cosine, sine]
    return pl.pallas_call(
        functools.partial(ordered, qkv_grads, len(after)),
        out_shape=(jax.ShapeDtypeStruct((3 * width // 2, cols), BF16),) * 2
        + (jax.ShapeDtypeStruct((rows, cols), BF16),) * 2,
        in_specs=[ANYSPEC] * len(after) + [SSPEC] + [VSPEC] * len(operands),
        out_specs=[VSPEC] * 4,
        scratch_shapes=[pltpu.VMEM((rows, width), BF16)],
        compiler_params=params(24),
        cost_estimate=cost(True),
        name="project_grads",
    )(*after, place, *operands)


def project_back_kernel(
    place_ref, x_ref, gain_ref, gq_ref, dk_ref, dv_ref, recv_ref, cos_ref, sin_ref, w_ref,
    gqx_ref, gkx_ref, gvx_ref, w0, w1, w2, gm_ref, out_ref,
    keep_ref, send_ref, gx_ref, gain_grad_ref, low_s, gk_s, gv_s, wx_s,
):
    qkv_grads(place_ref, x_ref, gain_ref, gq_ref, dk_ref, dv_ref, recv_ref, cos_ref, sin_ref,
              keep_ref, send_ref, gk_s, gv_s, low_s)
    load_pieces(place_ref, (w0, w1, w2), wx_s)
    rows, width = x_ref.shape
    tile = min(256, rows)
    gain = gain_ref[...]
    gain_grad = jnp.zeros((1, width), F32)
    gx_ref[0:rows, :] = out_ref[...]
    for begin in range(0, rows, tile):
        at = pl.ds(begin, tile)
        normed, scale = norm_parts(x_ref[at, :].astype(F32))
        total = jnp.zeros((tile, width), F32)
        for item, (own, other) in enumerate(((gq_ref, gqx_ref), (gk_s, gkx_ref), (gv_s, gvx_ref))):
            part = slice(item * width, (item + 1) * width)
            total = total + dot_t(own[at, :], w_ref[part, :]) + dot_t(other[at, :], wx_s[part, :])
        gain_grad = gain_grad + jnp.sum(total * normed, axis=0, keepdims=True)
        scaled = total * gain
        gx_ref[pl.ds(rows + begin, tile), :] = (
            gm_ref[at, :]
            + scale
            * (
                scaled
                - jnp.mean(scaled, axis=-1, keepdims=True)
                - normed * jnp.mean(scaled * normed, axis=-1, keepdims=True)
            )
        ).astype(BF16)
    gain_grad_ref[...] = jnp.broadcast_to(gain_grad, gain_grad_ref.shape)


def project_back(place, x, gain, gq, dk, dv, received, cosine, sine, weight, others, pieces, grad_mixed, out, after):
    rows, width = x.shape
    cols = gq.shape[1]
    operands = [x, gain, gq, dk, dv, received, cosine, sine, weight, *others, *pieces, grad_mixed, out]
    return pl.pallas_call(
        functools.partial(ordered, project_back_kernel, len(after)),
        out_shape=(
            jax.ShapeDtypeStruct((3 * width // 2, cols), BF16),
            jax.ShapeDtypeStruct((3 * width // 2, cols), BF16),
            jax.ShapeDtypeStruct((2 * rows, width), BF16),
            jax.ShapeDtypeStruct((8, width), F32),
        ),
        in_specs=[ANYSPEC] * len(after) + [SSPEC] + [VSPEC] * len(operands),
        out_specs=[VSPEC] * 4,
        scratch_shapes=[
            pltpu.VMEM((rows, width), BF16),
            pltpu.VMEM((rows, cols), BF16),
            pltpu.VMEM((rows, cols), BF16),
            pltpu.VMEM((3 * width, cols), BF16),
        ],
        compiler_params=params(32),
        cost_estimate=cost(True),
        name="project_back",
    )(*after, place, *operands)


def pack(place, weights, after=(), entries=None):
    sizes = [value.shape[0] // 4 for value in weights]
    width = weights[0].shape[1]
    entries = entries or [PIECE] * len(weights)

    def spec(size, entry):
        return pl.BlockSpec((size, width), lambda _, at: (at[entry], 0))

    def kernel(place_ref, *refs):
        begin = 0
        for ref, size in zip(refs[len(after) :], sizes):
            refs[-1][begin : begin + size, :] = ref[...]
            begin += size

    return pl.pallas_call(
        kernel,
        grid_spec=pltpu.PrefetchScalarGridSpec(
            num_scalar_prefetch=1,
            grid=(1,),
            in_specs=[ANYSPEC] * len(after)
            + [spec(size, entry) for size, entry in zip(sizes, entries)],
            out_specs=pl.BlockSpec((sum(sizes), width), lambda _, at: (0, 0)),
        ),
        out_shape=jax.ShapeDtypeStruct((sum(sizes), width), BF16),
        compiler_params=params(semantics=("arbitrary",)),
        cost_estimate=cost(False),
        name="pack",
    )(place, *after, *weights)


def merge_kernel(jobs, after, place_ref, *refs):
    ins = list(refs[after : after + sum(job["count"] for job in jobs)])
    outs = list(refs[after + len(ins) :])
    for job in jobs:
        mine, ins = ins[: job["count"]], ins[job["count"] :]
        which = job["which"]
        if which is None:
            out_ref, outs = outs[0], outs[1:]
            out_ref[...] = sum(ref[...].astype(F32) for ref in mine).astype(out_ref.dtype)
            continue
        size = outs[0].shape[0]
        bit = place_ref[which]
        for out_ref, half in ((outs[0], 1 - bit), (outs[1], bit)):
            at = pl.ds(aligned(half * size, 16), size)
            total = sum(ref[at, :].astype(F32) for ref in (mine[:-2] if which == FIRST else mine))
            if which == FIRST:
                total = total + jnp.where(half == 0, mine[-2][...], mine[-1][...]).astype(F32)
            out_ref[...] = total.astype(BF16)
        outs = outs[2:]


def merge(place, *jobs, after=(), covers=True):
    arrays, shapes, notes = [], [], []
    for values, which in jobs:
        rows, cols = values[0].shape
        parts = 1 if which is None else 2
        shapes += [jax.ShapeDtypeStruct((rows // parts, cols), values[0].dtype)] * parts
        notes.append({"count": len(values), "which": which})
        arrays += values
    out = pl.pallas_call(
        functools.partial(merge_kernel, notes, len(after)),
        out_shape=tuple(shapes),
        in_specs=[SSPEC] + [ANYSPEC] * len(after) + [VSPEC] * len(arrays),
        out_specs=[VSPEC] * len(shapes),
        compiler_params=params(),
        cost_estimate=cost(covers),
        name="merge",
    )(place, *after, *arrays)
    return out


def join_kernel(counts, after, *refs):
    ins, outs = list(refs[after : after + sum(counts)]), refs[after + sum(counts) :]
    for count, out_ref in zip(counts, outs):
        size = out_ref.shape[0] // count
        for step in range(count):
            out_ref[step * size : (step + 1) * size, :] = ins[step][...]
        ins = ins[count:]


def join(*groups, after=(), covers=True):
    values = [value for group in groups for value in group]
    return pl.pallas_call(
        functools.partial(join_kernel, [len(group) for group in groups], len(after)),
        out_shape=tuple(
            jax.ShapeDtypeStruct((len(group) * group[0].shape[0], group[0].shape[1]), BF16) for group in groups
        ),
        in_specs=[ANYSPEC] * len(after) + [VSPEC] * len(values),
        out_specs=[VSPEC] * len(groups),
        compiler_params=params(),
        cost_estimate=cost(covers),
        name="join",
    )(*after, *values)


def split_kernel(both_ref, first_ref, second_ref):
    rows = first_ref.shape[0]
    first_ref[...] = both_ref[0:rows, :]
    second_ref[...] = both_ref[rows:, :]


def split(both):
    rows, width = both.shape[0] // 2, both.shape[1]
    return pl.pallas_call(
        split_kernel,
        out_shape=(jax.ShapeDtypeStruct((rows, width), both.dtype),) * 2,
        in_specs=[VSPEC],
        out_specs=[VSPEC] * 2,
        compiler_params=params(),
        cost_estimate=cost(False),
        name="split",
    )(both)


def assemble_kernel(kind, after, place_ref, *refs):
    pieces, outs = list(refs[after : after + 4]), refs[after + 5 : -1]
    refs[-1][...] = jnp.zeros(refs[-1].shape, F32)
    core = place_ref[CORE]
    size = pieces[0].shape[0]
    pieces += [refs[after + 4].at[step * size : (step + 1) * size] for step in range(4)]
    for step, piece in enumerate(pieces):
        mine = step < 4
        quarter = place_ref[MINE if mine else THEIRS] ^ (step % 4)
        side = core if mine else 1 - core
        if kind == "qkv":
            rows = size // 3
            for item in range(3):
                at = pl.ds(aligned((side * 4 + quarter) * rows, 8), rows)
                outs[0][item, at, :] = piece[item * rows : (item + 1) * rows, :].astype(F32)
            continue
        half = outs[0].shape[1] // 2
        part = pl.ds(aligned(side * half, LANES), half)
        begin = 0
        for out_ref in outs:
            rows = out_ref.shape[0] // 4
            at = pl.ds(aligned(quarter * rows, 8), rows)
            out_ref[at, part] = piece[begin : begin + rows, :].astype(F32)
            begin += rows


def assemble(kind, place, pieces, shapes, after=()):
    total = sum(math.prod(shape) for shape in shapes)
    return pl.pallas_call(
        functools.partial(assemble_kernel, kind, len(after)),
        out_shape=tuple(jax.ShapeDtypeStruct(shape, F32) for shape in [*shapes, (8, LANES)]),
        in_specs=[SSPEC] + [ANYSPEC] * len(after) + [VSPEC] * 5,
        out_specs=[VSPEC] * (len(shapes) + 1),
        compiler_params=params(),
        cost_estimate=cost(True),
        name="assemble",
    )(place, *after, *pieces)


def per_device(
    axis_sizes,
    hidden,
    seq_ids,
    cotangent,
    qkv_weight,
    attn_out_weight,
    mlp_in_weight,
    mlp_out_weight,
    norm1_gain,
    norm2_gain,
):
    dp_size, tensor_size = axis_sizes
    devices = dp_size * tensor_size
    chips = devices // 4
    chip_bits = chips.bit_length() - 1
    rows, width = hidden.shape
    cols = qkv_weight.shape[2]
    units = mlp_out_weight.shape[0]
    dp_at = lax.axis_index("dp")
    core = dp_at % 2
    chip = dp_at // 2

    def move(value, target):
        return lax.ppermute(value, ("dp", "tensor"), [(i, target(i)) for i in range(devices)])

    def swapped(i):
        return (i & ~3) | ((i & 1) << 1) | ((i >> 1) & 1)

    def to_tensor(i):
        return i ^ 1

    def to_core(i):
        return i ^ 2

    def to_near(i):
        return i ^ 4

    def to_next(i):
        return i ^ 8

    def masked(first, second):
        return lambda i: i ^ (second if i & 2 else first)

    near, next_near = chip % 2, (chip // 2) % 2
    quarters = [near * 2 + next_near, next_near * 2 + near]
    place = jnp.stack(
        [
            core,
            near * 2 + core,
            next_near * 2 + core,
            jnp.where(core == 0, quarters[0], quarters[1]),
            jnp.where(core == 0, quarters[1], quarters[0]),
            jnp.where(core == 0, 0, next_near),
            jnp.where(core == 0, near, 0),
            jnp.where(core == 0, next_near, near),
            jnp.where(core == 0, near, next_near),
            jnp.where(core == 0, next_near, near),
        ]
    ).astype(jnp.int32)

    x = move(hidden, swapped)
    ids = jnp.where(core == lax.axis_index("tensor"), seq_ids, move(seq_ids, to_core))
    ids_own = lax.dynamic_slice_in_dim(ids, core * rows, rows)
    ids_other = lax.dynamic_slice_in_dim(ids, (1 - core) * rows, rows)

    index = jnp.arange(ids.shape[0], dtype=jnp.int32)
    begins = jnp.zeros((rows,), jnp.int32)
    for number in (-1, 0, 1, 2):
        start = jnp.min(jnp.where(ids == number, index, ids.shape[0]))
        begins = jnp.where(ids_own == number, start, begins)
    pos = core * rows + jnp.arange(rows, dtype=jnp.int32) - begins
    frequency = jnp.power(ROPE_BASE, -2.0 * jnp.arange(HDIM // 2, dtype=F32) / HDIM)
    angles = pos.astype(F32)[:, None] * frequency[None, :]
    cosine, sine = jnp.cos(angles), jnp.sin(angles)
    cosine = jnp.concatenate([cosine] * 4, axis=1)
    sine = jnp.concatenate([-sine, sine] * 2, axis=1)
    col_own = jnp.broadcast_to(ids_own[:, None], (rows, LANES))
    col_other = jnp.broadcast_to(ids_other[:, None], (rows, LANES))
    row_own = jnp.broadcast_to(ids_own[None, :], (8, rows))
    row_other = jnp.broadcast_to(ids_other[None, :], (8, rows))

    w_qkv = qkv_weight.reshape(3 * width, cols)
    w_in = jnp.swapaxes(mlp_in_weight, 1, 2).reshape(2 * units, width)
    w_qkv_part = pack(place, [w_qkv])
    w_qkv_one = move(w_qkv_part, to_tensor)
    w_part = pack(
        place, [w_in, mlp_out_weight, attn_out_weight], [w_qkv_one], entries=[PIECE, PIECE_NEXT, PIECE_NEXT]
    )
    w_one = move(w_part, to_tensor)
    cot = move(cotangent, swapped)
    gain1, gain2 = norm1_gain[None, :], norm2_gain[None, :]

    (sent,) = join([w_qkv_one], covers=False)
    w_qkv_two = move(sent, to_near)
    q_a, *kv_a = project(place, x, gain1, [w_qkv], cosine, sine, after=[sent])
    kv_a_x = [move(value, to_core) for value in kv_a]
    o_a, lse_a = attend(q_a, kv_a, kv_a_x, col_own, row_own, row_other)
    sent, both = join([w_one], [w_qkv_one, w_qkv_two], after=[o_a], covers=False)
    in_rows = w_in.shape[0] // 4
    w_in_two, w_rest_two = move(sent[:in_rows], to_near), move(sent[in_rows:], to_next)
    w_qkv_x = [w_qkv_one, w_qkv_two, move(both, to_core)]
    q_b, *kv_b = project(place, x, gain1, w_qkv_x, cosine, sine, after=[sent])
    kv_b_x = [move(value, to_core) for value in kv_b]
    o_b, lse_b = attend(q_b, kv_b, kv_b_x, col_own, row_own, row_other)
    in_sent, rest_sent = join([w_in_two], [w_rest_two], after=[o_b], covers=False)
    w_x = [w_one, w_in_two, w_rest_two] + [move(value, to_core) for value in (w_one, in_sent, rest_sent)]
    out, grad_mixed, go_a, go_b, in_keep, in_send, gain2_part, grad_low, grad_mixed_low, hid = middle(
        place, x, o_a, o_b, cot, col_own, gain2, attn_out_weight, w_in, mlp_out_weight, w_x
    )
    rest_keep, rest_send = outer(place, o_a, o_b, hid, grad_low, grad_mixed_low)

    plain = range(2, chip_bits)

    def spread(total, after=()):
        one = move(total, masked(8, 4))
        two = move(total, masked(4, 8))
        mine = [total, one, two, move(one, masked(4, 8))]
        return mine + [move(join(mine, after=after)[0], to_core)]

    def back(q, kv, kv_x, go, o, lse, after):
        gq, dk, dv, dx = attend_back(q, kv, kv_x, go, o, lse, col_own, col_other, row_own, cosine, sine, after)
        return gq, dk, dv, move(dx, to_core)

    def pair(value, mask):
        return [value, move(value, masked(mask, mask))]

    target_1, target_2, target_3 = masked(1, 8), masked(4, 1), masked(8, 4)
    in_got = move(in_send, to_core)
    rest_got = move(rest_send, to_core)
    in_sent, in_kept = merge(place, ([in_keep, in_got], ONE))
    gq_b, dk_b, dv_b, recv_b = back(q_b, kv_b, kv_b_x, go_b, o_b, lse_b, [in_sent])
    in_got = move(in_sent, target_1)
    in_sent, in_kept, rest_sent, rest_kept = merge(
        place, ([in_kept, in_got], TWO), ([rest_keep, rest_got], ONE), after=[gq_b]
    )
    keep_b, send_b, gk_b, gv_b = project_grads(place, x, gain1, gq_b, dk_b, dv_b, recv_b, cosine, sine, [in_sent])
    (qkv_sum,) = merge(place, ([keep_b, move(send_b, to_core)], None), covers=False)
    half = qkv_sum.shape[0] // 2
    low_got = move(qkv_sum[:half], to_tensor)
    gq_a, dk_a, dv_a, recv_a = back(q_a, kv_a, kv_a_x, go_a, o_a, lse_a, [qkv_sum])
    in_got = move(in_sent, target_2)
    rest_got = move(rest_sent, target_1)
    in_sent, in_kept, rest_sent, rest_kept = merge(
        place, ([in_kept, in_got], THREE), ([rest_kept, rest_got], TWO), after=[gq_a, low_got]
    )
    in_got = move(in_sent, target_3)
    rest_got = move(rest_sent, target_2)
    high_got = move(qkv_sum[half:], to_tensor)
    keep_a, send_a, results, gain1_part = project_back(
        place, x, gain1, gq_a, dk_a, dv_a, recv_a, cosine, sine, w_qkv, [gq_b, gk_b, gv_b], w_qkv_x, grad_mixed,
        out, [in_sent],
    )
    in_total, rest_sent, rest_kept = merge(
        place, ([in_kept, in_got], None), ([rest_kept, rest_got], THREE), after=[keep_a, high_got]
    )
    rest_got = move(rest_sent, target_3)
    results = move(results, swapped)
    gains = jnp.concatenate([gain1_part, gain2_part])
    sent, kept, gains = merge(
        place,
        ([keep_a, move(send_a, to_core), low_got, high_got], FIRST),
        (pair(gains, 2), None),
        after=[in_total],
    )
    sent, kept, gains, rest_total = merge(
        place,
        ([kept, move(sent, masked(4, 8))], SECOND),
        (pair(gains, 4), None),
        ([rest_kept, rest_got], None),
    )
    for b in plain:
        (in_total,) = merge(place, (pair(in_total, 4 << b), None), after=[sent])
    in_pieces = spread(in_total)
    qkv_total, gains = merge(
        place, ([kept, move(sent, masked(8, 4))], None), (pair(gains, 8), None), after=[in_total]
    )
    for b in plain:
        rest_total, gains = merge(
            place, (pair(rest_total, 4 << b), None), (pair(gains, 4 << b), None), after=[qkv_total]
        )
    rest_pieces = spread(rest_total)
    g_in, in_done = assemble("in", place, in_pieces, [(2 * units, width)])
    out, input_grad = split(results)
    gains_got = pair(gains, 1)
    for b in plain:
        qkv_total, gains = merge(
            place, (pair(qkv_total, 4 << b), None), (gains_got, None), after=[input_grad, in_pieces[3]]
        )
    qkv_pieces = spread(qkv_total, [in_done])
    g_down, g_out, _ = assemble("rest", place, rest_pieces, [(units, width), (cols, width)], after=[qkv_total])
    g_qkv, _ = assemble("qkv", place, qkv_pieces, [(3, width, cols)])
    return (
        out,
        input_grad,
        gains[0],
        gains[8],
        g_qkv,
        g_out,
        jnp.swapaxes(g_in.reshape(2, units, width), 1, 2),
        g_down,
    )


def solution(mesh):
    in_specs = (
        P(("dp", "tensor"), None),
        P("dp"),
        P(("dp", "tensor"), None),
        P(None, None, "tensor"),
        P("tensor", None),
        P(None, None, "tensor"),
        P("tensor", None),
        P(),
        P(),
    )
    out_specs = (
        P(("dp", "tensor"), None),
        P(("dp", "tensor"), None),
        P(),
        P(),
        P(None, None, "tensor"),
        P("tensor", None),
        P(None, None, "tensor"),
        P("tensor", None),
    )
    return jax.shard_map(
        functools.partial(per_device, (mesh.shape["dp"], mesh.shape["tensor"])),
        mesh=mesh,
        in_specs=in_specs,
        out_specs=out_specs,
        check_vma=False,
    )
```
